32 devices in a mesh: ctx: 4 (over y, x), exp: 8 (over z, core).
Axes of the slice: x: 2, y: 2, z: 4, core: 2. Of those that a mesh axis runs over, the one named last changes fastest.
Arguments:
- queries: bfloat16 [64, 2, 4096], P('exp'), may hold values from -36 to 36
- cache_keys: bfloat16 [64, 256, 256], P('exp', 'ctx'), may hold values from -6 to 6
- cache_values: bfloat16 [64, 256, 256], P('exp', 'ctx'), may hold values from -6 to 6
- new_keys: bfloat16 [64, 2, 256], P('exp'), may hold values from -6 to 6
- new_values: bfloat16 [64, 2, 256], P('exp'), may hold values from -6 to 6
- lengths: int32 [64], P('exp'), may hold values from 2 to 256, as said below
- residual: bfloat16 [64, 2, 2048], P('exp'), may hold values from -12 to 12
- out_weight: bfloat16 [4096, 2048], P('ctx'), may hold values from -0.25 to 0.25
- norm_gain: bfloat16 [2048], replicated, may hold values from 0.099609375 to 1.8984375
- expert_ids: int32 [64, 2, 8], P('exp'), may hold values from 0 to 31, all different within a row; in each aligned block of 16 rows (0 to 15, 16 to 31, ..., all dimensions but the last counted through in order) at most 4 rows name the same one
- expert_weights: float32 [64, 2, 8], P('exp'), may hold values from 0.05 to 0.5
- gate_proj: bfloat16 [8, 2048, 4096], P('exp', None, 'ctx'), may hold values from -0.125 to 0.125
- up_proj: bfloat16 [8, 2048, 4096], P('exp', None, 'ctx'), may hold values from -0.125 to 0.125
- down_proj: bfloat16 [8, 4096, 2048], P('exp', 'ctx'), may hold values from -0.1875 to 0.1875
Outputs:
- layer_output: bfloat16 [64, 2, 2048], P('exp')
The draws below stay inside these ranges and needn't reach their ends.
Inputs may be any that keep to these rules, and one draw needn't show every extreme that they name: `expert_ids`: in the 8 rows of one index of exp (both steps together) no expert is named more than 4 times; each row names 8 different experts at each step. `lengths`: some row has all 256 positions live.
All inputs are finite; a program needn't handle non-finite values.
Results may differ from the reference program's by a relative error of at most 0.0055.
Values may be sent and summed in bfloat16 or wider, within the bound.
No kernel may reach another device: no remote copies, remote signals or barrier semaphores. Data moves between devices by JAX's collectives and lax.ppermute only.
A program may use at most 64 MiB of HBM per device.

```python
import math
import jax
import jax.numpy as jnp
import numpy as np
from jax import lax

D = 2048
HEADS = 32
KV_HEADS = 2
HEAD_DIM = 128
FF = 1024
EXP_DEV = 4
TOPK = 8
STEPS = 2
ROW_DEV = 8
EXPERTS = 32
ROWS = 64
SEQ = 256
CAP = 4
N_EXP = 8


def attention_draw(key):
    key_field = jnp.clip(jax.random.normal(jax.random.fold_in(key, 101), (ROWS, SEQ, KV_HEADS * HEAD_DIM), jnp.float32), -6.0, 6.0)
    query_field = jnp.clip(jax.random.normal(jax.random.fold_in(key, 102), (ROWS, STEPS, HEADS * HEAD_DIM), jnp.float32), -6.0, 6.0)
    return (key_field, query_field)


def draw_cache_keys(key, part):
    return attention_draw(key)[0].astype(jnp.bfloat16)


def draw_queries(key, part):
    return attention_draw(key)[1].astype(jnp.bfloat16)


def draw_residual(key, part):
    base = jax.random.normal(jax.random.fold_in(key, 201), (ROWS, STEPS, D), jnp.float32)
    row_scale = jnp.exp(jax.random.uniform(jax.random.fold_in(key, 202), (ROWS, STEPS, 1), jnp.float32, jnp.log(0.3), jnp.log(3.0)))
    column_scale = jnp.exp(jax.random.uniform(jax.random.fold_in(key, 203), (1, 1, D), jnp.float32, jnp.log(0.5), jnp.log(2.0)))
    return jnp.clip(base * row_scale * column_scale, -12.0, 12.0).astype(jnp.bfloat16)


def draw_lengths(key, part):
    values = jax.random.randint(jax.random.fold_in(key, 301), (ROWS,), 2, SEQ + 1)
    longest = jax.random.randint(jax.random.fold_in(key, 302), (), 0, ROWS)
    return jnp.where(jnp.arange(ROWS) == longest, SEQ, values).astype(jnp.int32)


def steps_of(own_key, dims, pieces, smallest, top_value):
    factor_of, own = 1.0, jax.random.fold_in(own_key, 6)
    for position, shards_of in pieces:
        draws = jnp.exp(jax.random.uniform(jax.random.fold_in(own, position), (shards_of,), jnp.float32, smallest / len(pieces), top_value / len(pieces)))
        factor_of = factor_of * jnp.repeat(draws, dims[position] // shards_of).reshape([-1 if axis == position else 1 for axis in range(len(dims))])
    return factor_of


def shared_out(stream_key, own, number, rows, number_of, top, bound, lean):
    ranking = jax.random.permutation(stream_key, number_of)
    packed, common = shares(number_of, rows * top, bound, lean, True), shares(number_of, rows * top, bound, lean, False)
    places = jnp.arange(number_of)

    def named(tallies, offset_by):
        used = int((tallies > 0).sum())
        fixed = max(1, used // 4)
        moved = fixed + (places - fixed + offset_by * (used - fixed)) % max(1, number_of - fixed)
        return jnp.zeros((number_of,), jnp.int32).at[ranking[jnp.where(places < fixed, places, moved)]].set(jnp.asarray(tallies, jnp.int32))

    tallies = jnp.where(number % 4 == 0, named(packed, number // 4), named(common, number - number // 4 - 1))
    mixed = jax.random.permutation(jax.random.fold_in(own, 3), number_of)
    source_of, taker = mixed[0:number_of // 2 * 2:2], mixed[1:number_of // 2 * 2:2]
    margin = jnp.minimum(tallies[source_of] - 1, bound - tallies[taker]) // 2
    margin = jnp.where((source_of == ranking[0]) | (taker == ranking[0]) | (tallies[taker] == 0), 0, jnp.maximum(margin, 0))
    moved = jax.random.randint(jax.random.fold_in(own, 4), (number_of // 2,), 0, 1 << 20) % (margin + 1)
    tallies = tallies.at[source_of].add(-moved).at[taker].add(moved)
    members = jnp.searchsorted(jnp.cumsum(tallies), jnp.arange(rows * top), side="right").astype(jnp.int32)
    listing = members.reshape(top, rows).T
    listing = listing[jax.random.permutation(jax.random.fold_in(own, 1), rows)]
    offset_by = jax.random.randint(jax.random.fold_in(own, 2), (rows, 1), 0, top)
    return jnp.take_along_axis(listing, (jnp.arange(top)[None, :] + offset_by) % top, axis=1)


def shares(amount, total, most, skew, full):
    portions = [(1 << 20) // math.isqrt(rank ** skew) + 1 for rank in range(1, amount + 1)]
    largest = most if full else min(most, max(-(-total // amount), total * portions[0] // sum(portions)))
    least = 1 if total - largest >= amount - 1 else 0
    given, surplus = [largest] + [least] * (amount - 1), total - largest - least * (amount - 1)
    while surplus > 0:
        free = [i for i in range(1, amount) if given[i] < largest] or [i for i in range(1, amount) if given[i] < most]
        whole, budget = sum([portions[i] for i in free]), surplus
        for i in free:
            extra = min(most - given[i], max(1, budget * portions[i] // whole), surplus)
            given[i] = given[i] + extra
            surplus = surplus - extra
    return np.array(given)


def noise(key, dims, spread, limit, pieces=(), dtype=jnp.bfloat16):
    gain = steps_of(key, dims, pieces, -0.22, 0.18) if pieces else 1.0
    values = jax.random.normal(key, dims, jnp.float32) * spread * gain
    return jnp.minimum(jnp.maximum(values, -limit), limit).astype(dtype)


def setup_inputs(seed: int = 0) -> dict:
    key_of = jax.random.split(jax.random.key(seed), 15)
    queries = draw_queries(jax.random.fold_in(key_of[14], 71), 0)
    cache_keys = draw_cache_keys(jax.random.fold_in(key_of[14], 71), 0)
    cache_values = noise(key_of[2], (ROWS, SEQ, KV_HEADS * HEAD_DIM), 1.0, 6.0, ((0, 8), (1, 4)))
    new_keys = noise(key_of[3], (ROWS, STEPS, KV_HEADS * HEAD_DIM), 1.0, 6.0, ((0, 8),))
    new_values = noise(key_of[4], (ROWS, STEPS, KV_HEADS * HEAD_DIM), 1.0, 6.0, ((0, 8),))
    lengths = draw_lengths(jax.random.fold_in(key_of[14], 71), 0)
    residual = draw_residual(jax.random.fold_in(key_of[14], 71), 0)
    out_weight = noise(key_of[7], (HEADS * HEAD_DIM, D), (4 * HEAD_DIM) ** -0.5, 0.25, ((0, 4),))
    norm_gain = jnp.clip(1.0 + 0.18 * jax.random.normal(key_of[8], (D,), jnp.float32), 0.099609375, 1.8984375).astype(jnp.bfloat16)
    expert_ids_keys = jax.random.split(jax.random.fold_in(key_of[9], 1), ROWS * STEPS // (ROW_DEV * STEPS))
    expert_ids_turns = jax.random.permutation(jax.random.fold_in(key_of[9], 3), ROWS * STEPS // (ROW_DEV * STEPS))
    expert_ids = jax.vmap(lambda own, number: shared_out(jax.random.fold_in(key_of[9], 2), own, number, ROW_DEV * STEPS, EXPERTS, TOPK, CAP, 2))(expert_ids_keys, expert_ids_turns).reshape((ROWS, STEPS, TOPK))
    expert_weights = jnp.clip(jnp.exp(math.log(0.5) - 2.3025851 * jax.random.uniform(key_of[10], (ROWS, STEPS, TOPK), jnp.float32) ** steps_of(key_of[10], (ROWS, STEPS, TOPK), ((0, 8),), -0.2, 0.2)), 0.05, 0.5)
    gate_proj = noise(key_of[11], (EXPERTS // EXP_DEV, D, EXP_DEV * FF), D ** -0.5, 0.125, ((0, 8), (2, 4)))
    up_proj = noise(key_of[12], (EXPERTS // EXP_DEV, D, EXP_DEV * FF), D ** -0.5, 0.125, ((0, 8), (2, 4)))
    down_proj = noise(key_of[13], (EXPERTS // EXP_DEV, EXP_DEV * FF, D), FF ** -0.5, 0.1875, ((0, 8), (1, 4)))
    return dict(queries=queries, cache_keys=cache_keys, cache_values=cache_values, new_keys=new_keys, new_values=new_values, lengths=lengths, residual=residual, out_weight=out_weight, norm_gain=norm_gain, expert_ids=expert_ids, expert_weights=expert_weights, gate_proj=gate_proj, up_proj=up_proj, down_proj=down_proj)


NORM_EPSILON = 1e-06
MASKED_SCORE = -1e+30

def attend_row(operands):
    query_row, key_row, value_row, fresh_keys, fresh_values, length = operands
    group_size = HEADS // KV_HEADS
    score_scale = 1.0 / math.sqrt(HEAD_DIM)
    query_heads = query_row.astype(jnp.float32).reshape(STEPS, KV_HEADS, group_size, HEAD_DIM)
    all_keys = jnp.concatenate([key_row, fresh_keys], 0).astype(jnp.float32).reshape(SEQ + STEPS, KV_HEADS, HEAD_DIM)
    all_values = jnp.concatenate([value_row, fresh_values], 0).astype(jnp.float32).reshape(SEQ + STEPS, KV_HEADS, HEAD_DIM)
    scores = jnp.einsum('skgd,tkd->skgt', query_heads, all_keys, precision=lax.Precision.HIGHEST) * score_scale
    positions = jnp.arange(SEQ + STEPS).astype(jnp.int32)
    step_index = jnp.arange(STEPS).astype(jnp.int32)
    live = jnp.where(positions[None, :] < SEQ, positions[None, :] < length, positions[None, :] - SEQ <= step_index[:, None])
    live = live[:, None, None, :]
    masked_scores = jnp.where(live, scores, MASKED_SCORE)
    row_max = lax.optimization_barrier(jnp.max(masked_scores, -1, keepdims=True))
    terms = jnp.where(live, jnp.exp(masked_scores - row_max), 0.0)
    mixed = jnp.einsum('skgt,tkd->skgd', terms, all_values, precision=lax.Precision.HIGHEST)
    mixed = mixed / lax.optimization_barrier(jnp.sum(terms, -1))[..., None]
    return mixed.reshape(STEPS, HEADS * HEAD_DIM).astype(jnp.bfloat16)

def reference(queries, cache_keys, cache_values, new_keys, new_values, lengths, residual, out_weight, norm_gain, expert_ids, expert_weights, gate_proj, up_proj, down_proj):
    attended = lax.map(attend_row, (queries, cache_keys, cache_values, new_keys, new_values, lengths))
    row_total = ROWS * STEPS
    attended = attended.reshape(row_total, HEADS * HEAD_DIM)
    projected = jnp.dot(attended.astype(jnp.float32), out_weight.astype(jnp.float32), precision=lax.Precision.HIGHEST)
    state = residual.reshape(row_total, D).astype(jnp.float32) + projected
    normed = (state * lax.rsqrt(lax.optimization_barrier(jnp.mean(state * state, -1, keepdims=True)) + NORM_EPSILON) * norm_gain.astype(jnp.float32)).astype(jnp.bfloat16)
    flat_ids = expert_ids.reshape(row_total, TOPK)
    flat_weights = expert_weights.reshape(row_total, TOPK).astype(jnp.float32)
    most_rows = N_EXP * CAP
    normed_wide = normed.astype(jnp.float32)

    def one_group(mixture, tables):
        gate_table, up_table, down_table, group_index = tables
        for member in range(EXP_DEV):
            expert = group_index * EXP_DEV + member
            matches = flat_ids == expert
            combine = lax.optimization_barrier(jnp.sum(jnp.where(matches, flat_weights, 0.0), 1))
            chosen = jnp.any(matches, 1)
            order = jnp.argsort(jnp.where(chosen, 0, 1).astype(jnp.int32), stable=True)[:most_rows].astype(jnp.int32)
            picked = normed_wide[order]
            gate_cols = gate_table[:, member * FF:(member + 1) * FF].astype(jnp.float32)
            up_cols = up_table[:, member * FF:(member + 1) * FF].astype(jnp.float32)
            down_rows = down_table[member * FF:(member + 1) * FF, :].astype(jnp.float32)
            gate_terms = jnp.dot(picked, gate_cols, precision=lax.Precision.HIGHEST)
            up_terms = jnp.dot(picked, up_cols, precision=lax.Precision.HIGHEST)
            activation = (jax.nn.silu(gate_terms) * up_terms).astype(jnp.bfloat16)
            expert_out = jnp.dot(activation.astype(jnp.float32), down_rows, precision=lax.Precision.HIGHEST)
            mixture = mixture.at[order].add(combine[order][:, None] * expert_out)
        return (mixture, None)
    start_mix = jnp.zeros((row_total, D), jnp.float32)
    group_ids = jnp.arange(EXPERTS // EXP_DEV).astype(jnp.int32)
    mixture, _ = lax.scan(one_group, start_mix, (gate_proj, up_proj, down_proj, group_ids))
    return (state + mixture).astype(jnp.bfloat16).reshape(ROWS, STEPS, D)
```

```python
import functools
import math

import jax
import jax.numpy as jnp
from jax import lax
from jax.experimental import pallas as pl
from jax.experimental.pallas import tpu as pltpu
from jax.sharding import PartitionSpec as P

D = 2048
HEADS = 32
KV_HEADS = 2
HEAD_DIM = 128
EXP_DEV = 4
TOPK = 8
LANES = 128


NORM_EPSILON = 1e-06
MASKED_SCORE = -1e30


def iota(shape, dim):
    return lax.broadcasted_iota(jnp.int32, shape, dim)


def to_column(row, count):
    return jnp.transpose(jnp.broadcast_to(row, (LANES, LANES)))[:count]


def split_three(values):
    high = values.astype(jnp.bfloat16)
    rest = values - high.astype(jnp.float32)
    middle = rest.astype(jnp.bfloat16)
    low = (rest - middle.astype(jnp.float32)).astype(jnp.bfloat16)
    return high, middle, low


def attend_kernel(
    ctx_count, me_ref, len_ref, q_ref, k_ref, v_ref, nk_ref, nv_ref, *rest
):
    outs, blocks = rest[:ctx_count], rest[ctx_count]
    rows, steps, _ = q_ref.shape
    window = k_ref.shape[1]
    row_steps = rows * steps
    group = HEADS // KV_HEADS
    block_heads = HEADS // ctx_count
    high = group * row_steps
    wide = rows * window
    scale = 1.0 / math.sqrt(HEAD_DIM)
    me = me_ref[0]
    queries = jnp.concatenate([q_ref[r] for r in range(rows)], 0)
    keys = k_ref[...].reshape(wide, KV_HEADS * HEAD_DIM)
    values = v_ref[...].reshape(wide, KV_HEADS * HEAD_DIM)
    fresh_keys = jnp.concatenate([nk_ref[r] for r in range(rows)], 0)
    fresh_values = jnp.concatenate([nv_ref[r] for r in range(rows)], 0)
    column = iota((1, wide), 1)
    column_row = column // window
    position = me * window + column % window
    limit = jnp.zeros((1, wide), jnp.int32)
    for r in range(rows):
        limit = jnp.where(column_row == r, len_ref[r], limit)
    column_code = jnp.where(position < limit, column_row, -1)
    row_index = iota((high, 1), 0) % row_steps
    row_code = row_index // steps
    row_step = row_index % steps
    fresh_column = iota((1, row_steps), 1)
    fresh_row = jnp.where(me == 0, fresh_column // steps, -1)
    fresh_step = fresh_column % steps
    live = row_code == column_code
    fresh_live = (row_code == fresh_row) & (fresh_step <= row_step)
    contract_last = (((1,), (1,)), ((), ()))
    for kv in range(KV_HEADS):
        lanes = slice(kv * HEAD_DIM, (kv + 1) * HEAD_DIM)
        heads = jnp.concatenate(
            [
                queries[:, h * HEAD_DIM : (h + 1) * HEAD_DIM]
                for h in range(kv * group, (kv + 1) * group)
            ],
            0,
        )
        scores = lax.dot_general(
            heads, keys[:, lanes], contract_last, preferred_element_type=jnp.float32
        )
        fresh = lax.dot_general(
            heads, fresh_keys[:, lanes], contract_last, preferred_element_type=jnp.float32
        )
        scores = jnp.where(live, scores * scale, MASKED_SCORE)
        fresh = jnp.where(fresh_live, fresh * scale, MASKED_SCORE)
        top = jnp.maximum(
            jnp.max(scores, 1, keepdims=True), jnp.max(fresh, 1, keepdims=True)
        )
        terms = jnp.exp(scores - top)
        fresh_terms = jnp.exp(fresh - top)
        total = jnp.sum(terms, 1, keepdims=True) + jnp.sum(fresh_terms, 1, keepdims=True)
        weighted = jnp.dot(
            terms.astype(jnp.bfloat16), values[:, lanes], preferred_element_type=jnp.float32
        ) + jnp.dot(
            fresh_terms.astype(jnp.bfloat16),
            fresh_values[:, lanes],
            preferred_element_type=jnp.float32,
        )
        mean = (weighted / total).astype(jnp.bfloat16)
        level = jnp.broadcast_to(top + jnp.log(total), (high, LANES))
        span = block_heads * row_steps
        for part in range(high // LANES):
            level_row = jnp.transpose(level[part * LANES : (part + 1) * LANES])[:8]
            pieces = split_three(level_row)
            for sub in range(LANES // span):
                dest = (kv * high + part * LANES) // span + sub
                start = part * LANES + sub * span
                blocks[dest, :span, :] = mean[start : start + span]
                for i, piece in enumerate(pieces):
                    if sub > 0:
                        piece = jnp.concatenate(
                            [piece[:, sub * span :], piece[:, : sub * span]], 1
                        )
                    blocks[dest, span + 16 * i : span + 16 * (i + 1), :] = jnp.concatenate(
                        [piece, piece], 0
                    )
    for k in range(ctx_count):
        outs[k][...] = blocks[me ^ k]


def project_kernel(ctx_count, me_ref, w_ref, *rest):
    parts, own, outs, blocks = (
        rest[:ctx_count],
        rest[ctx_count],
        rest[ctx_count + 1 : 2 * ctx_count],
        rest[2 * ctx_count],
    )
    block_heads = HEADS // ctx_count
    span = parts[0].shape[0] - 48
    row_steps = span // block_heads
    width = D // ctx_count
    levels = [
        sum(
            part[span + 16 * i : span + 16 * (i + 1), :].astype(jnp.float32)[:1]
            for i in range(3)
        )
        for part in parts
    ]
    top = functools.reduce(jnp.maximum, levels)
    factors = [jnp.exp(level - top) for level in levels]
    total = functools.reduce(jnp.add, factors)
    mixed = None
    for part, factor in zip(parts, factors):
        term = part[:span, :].astype(jnp.float32) * to_column(factor / total, span)
        mixed = term if mixed is None else mixed + term
    mixed = mixed.astype(jnp.bfloat16)
    attended = jnp.concatenate(
        [mixed[h * row_steps : (h + 1) * row_steps] for h in range(block_heads)], 1
    )
    for dest in range(ctx_count):
        projected = jnp.dot(
            attended,
            w_ref[:, dest * width : (dest + 1) * width],
            preferred_element_type=jnp.float32,
        )
        for q in range(width // LANES):
            blocks[dest, q * row_steps : (q + 1) * row_steps, :] = projected[
                :, q * LANES : (q + 1) * LANES
            ]
    me = me_ref[0]
    own[...] = blocks[me]
    for k in range(1, ctx_count):
        outs[k - 1][...] = blocks[me ^ k].astype(jnp.bfloat16)


def route_kernel(
    ctx_count, exp_count, capacity, me_ref, ids_ref, weights_ref, residual_ref,
    selector_ref, high_ref, low_ref, slice_ref
):
    rows, steps, _ = residual_ref.shape
    row_steps = rows * steps
    chunks = D // ctx_count // LANES
    shard_count = ctx_count // EXP_DEV
    high, wide = chunks * row_steps, ctx_count * exp_count * chunks * capacity
    ids = jnp.concatenate([ids_ref[...]] * chunks, 0)
    weights = jnp.concatenate([weights_ref[...]] * chunks, 0)
    column = iota((1, wide), 1)
    slot = column % capacity
    chunk = column // capacity % chunks
    dest = column // (capacity * chunks)
    expert = dest % exp_count * EXP_DEV + dest // exp_count // shard_count
    matched = jnp.zeros((high, wide), jnp.float32)
    weight = jnp.zeros((high, wide), jnp.float32)
    for k in range(TOPK):
        hit = ids[:, k : k + 1] == expert
        matched = jnp.where(hit, 1.0, matched)
        weight = jnp.where(hit, weights[:, k : k + 1], weight)
    earlier_row, earlier_column = iota((high, high), 0), iota((high, high), 1)
    earlier = (earlier_column < earlier_row) & (
        earlier_column // row_steps == earlier_row // row_steps
    )
    rank = jnp.dot(
        jnp.where(earlier, 1.0, 0.0).astype(jnp.bfloat16),
        matched.astype(jnp.bfloat16),
        preferred_element_type=jnp.float32,
    )
    row_chunk = iota((high, 1), 0) // row_steps
    chosen = (
        (matched > 0.0) & (rank == slot.astype(jnp.float32)) & (row_chunk == chunk)
    )
    selector_ref[...] = jnp.where(chosen, 1.0, 0.0).astype(jnp.bfloat16)
    weight = jnp.where(chosen, weight, 0.0)
    weight_high = weight.astype(jnp.bfloat16)
    high_ref[...] = weight_high
    low_ref[...] = (weight - weight_high.astype(jnp.float32)).astype(jnp.bfloat16)
    me = me_ref[0]
    for q in range(chunks):
        start = pl.multiple_of((me * chunks + q) * LANES, LANES)
        piece = jnp.concatenate(
            [residual_ref[r, :, pl.ds(start, LANES)] for r in range(rows)], 0
        )
        slice_ref[q * row_steps : (q + 1) * row_steps, :] = piece.astype(jnp.float32)


def dispatch_kernel(ctx_count, residual_ref, selector_ref, *rest):
    parts, state_ref, out_ref = rest[:ctx_count], rest[ctx_count], rest[ctx_count + 1]
    state = residual_ref[...]
    for part in parts:
        state = state + part[...].astype(jnp.float32)
    state_ref[...] = state
    out_ref[...] = lax.dot_general(
        selector_ref[...],
        state.astype(jnp.bfloat16),
        (((0,), (0,)), ((), ())),
        preferred_element_type=jnp.float32,
    ).astype(jnp.bfloat16)


def expert_kernel(
    ctx_count, exp_count, capacity, in_ref, gain_ref, gate_ref, up_ref, down_ref, out_ref
):
    chunks = D // ctx_count // LANES
    block = exp_count * chunks * capacity
    named = exp_count * capacity
    wanted, given = iota((block, block), 0), iota((block, block), 1)
    source = (
        wanted // capacity % exp_count * (chunks * capacity)
        + wanted // named * capacity
        + wanted % capacity
    )
    order = jnp.where(source == given, 1.0, 0.0).astype(jnp.bfloat16)
    pieces = []
    for c in range(ctx_count):
        part = jnp.dot(
            order, in_ref[c * block : (c + 1) * block, :], preferred_element_type=jnp.float32
        )
        pieces += [part[q * named : (q + 1) * named] for q in range(chunks)]
    state = jnp.concatenate(pieces, 1)
    normed = (
        state
        * lax.rsqrt(jnp.mean(state * state, -1, keepdims=True) + NORM_EPSILON)
        * gain_ref[...].astype(jnp.float32)
    ).astype(jnp.bfloat16)
    gate = jnp.dot(normed, gate_ref[0], preferred_element_type=jnp.float32)
    up = jnp.dot(normed, up_ref[0], preferred_element_type=jnp.float32)
    activation = (gate / (1.0 + jnp.exp(-gate)) * up).astype(jnp.bfloat16)
    result = jnp.dot(activation, down_ref[0], preferred_element_type=jnp.float32).astype(
        jnp.bfloat16
    )
    for c in range(ctx_count):
        part = jnp.concatenate(
            [
                result[:, (c * chunks + q) * LANES : (c * chunks + q + 1) * LANES]
                for q in range(chunks)
            ],
            0,
        )
        out_ref[c * block : (c + 1) * block, :] = lax.dot_general(
            order, part, (((0,), (0,)), ((), ())), preferred_element_type=jnp.float32
        ).astype(jnp.bfloat16)


def combine_kernel(state_ref, high_ref, low_ref, in_ref, out_ref):
    returned = in_ref[...]
    mixture = jnp.dot(high_ref[...], returned, preferred_element_type=jnp.float32) + jnp.dot(
        low_ref[...], returned, preferred_element_type=jnp.float32
    )
    out_ref[...] = (state_ref[...] + mixture).astype(jnp.bfloat16)


def assemble_kernel(ctx_count, me_ref, *rest):
    parts, out_ref = rest[:ctx_count], rest[ctx_count]
    rows, steps, _ = out_ref.shape
    row_steps = rows * steps
    chunks = D // ctx_count // LANES
    me = me_ref[0]
    for k, part in enumerate(parts):
        for q in range(chunks):
            start = pl.multiple_of(((me ^ k) * chunks + q) * LANES, LANES)
            for r in range(rows):
                first = q * row_steps + r * steps
                out_ref[r, :, pl.ds(start, LANES)] = part[first : first + steps, :]


VMEM = pl.BlockSpec(memory_space=pltpu.VMEM)
SMEM = pl.BlockSpec(memory_space=pltpu.SMEM)


def call(kernel, name, in_specs, out_shapes, operands, scratch=(), vmem=None):
    return pl.pallas_call(
        kernel,
        name=name,
        in_specs=in_specs,
        out_specs=[VMEM] * len(out_shapes),
        out_shape=[jax.ShapeDtypeStruct(shape, dtype) for shape, dtype in out_shapes],
        scratch_shapes=list(scratch),
        compiler_params=pltpu.CompilerParams(vmem_limit_bytes=vmem),
    )(*operands)


def swap(blocks):
    count = lax.axis_size("ctx")
    return [
        lax.ppermute(block, "ctx", [(i, i ^ k) for i in range(count)])
        for k, block in enumerate(blocks, 1)
    ]


def per_device(
    queries,
    cache_keys,
    cache_values,
    new_keys,
    new_values,
    lengths,
    residual,
    out_weight,
    norm_gain,
    expert_ids,
    expert_weights,
    gate_proj,
    up_proj,
    down_proj,
):
    row_count, step_count, _ = queries.shape
    row_steps = row_count * step_count
    n = lax.axis_size("ctx")
    exp_count = lax.axis_size("exp")
    me = lax.axis_index("ctx").astype(jnp.int32).reshape(1)
    experts_all = exp_count * EXP_DEV
    capacity = max(2, (row_steps * TOPK + experts_all - 1) // experts_all)
    chunks = D // n // LANES
    device_rows = chunks * capacity
    all_rows = n * exp_count * device_rows
    span = HEADS // n * row_steps
    bf16, f32 = jnp.bfloat16, jnp.float32

    message = (span + 48, LANES)
    sent = call(
        functools.partial(attend_kernel, n),
        "attend",
        [SMEM, SMEM] + [VMEM] * 5,
        [(message, bf16)] * n,
        (me, lengths, queries, cache_keys, cache_values, new_keys, new_values),
        [pltpu.VMEM((n,) + message, bf16)],
    )
    got = swap(sent[1:])
    selector, weight_high, weight_low, residual_part = call(
        functools.partial(route_kernel, n, exp_count, capacity),
        "route",
        [SMEM] + [VMEM] * 3,
        [((chunks * row_steps, all_rows), bf16)] * 3 + [((chunks * row_steps, LANES), f32)],
        (
            me,
            expert_ids.reshape(row_steps, TOPK),
            expert_weights.reshape(row_steps, TOPK),
            residual,
        ),
    )
    part = (chunks * row_steps, LANES)
    sent = call(
        functools.partial(project_kernel, n),
        "project",
        [SMEM] + [VMEM] * (n + 1),
        [(part, f32)] + [(part, bf16)] * (n - 1),
        (me, out_weight, sent[0], *got),
        [pltpu.VMEM((n,) + part, f32)],
        32 * 1024 * 1024,
    )
    got = swap(sent[1:])
    state, outgoing = call(
        functools.partial(dispatch_kernel, n),
        "dispatch",
        [VMEM] * (n + 2),
        [(part, f32), ((all_rows, LANES), bf16)],
        (residual_part, selector, sent[0], *got),
    )

    def exchange(rows):
        rows = rows.reshape(n * exp_count, device_rows, LANES)
        rows = lax.all_to_all(rows, ("ctx", "exp"), split_axis=0, concat_axis=0, tiled=True)
        return rows.reshape(all_rows, LANES)

    arrived = exchange(outgoing)
    (results,) = call(
        functools.partial(expert_kernel, n, exp_count, capacity),
        "experts",
        [VMEM] * 5,
        [((all_rows, LANES), bf16)],
        (arrived, norm_gain.reshape(1, D), gate_proj, up_proj, down_proj),
        (),
        48 * 1024 * 1024,
    )
    returned = exchange(results)
    (layer_part,) = call(
        combine_kernel,
        "combine",
        [VMEM] * 4,
        [(part, bf16)],
        (state, weight_high, weight_low, returned),
    )
    got = swap([layer_part] * (n - 1))
    (layer_rows,) = call(
        functools.partial(assemble_kernel, n),
        "assemble",
        [SMEM] + [VMEM] * n,
        [((row_count, step_count, D), bf16)],
        (me, layer_part, *got),
    )
    return layer_rows


def solution(mesh):
    return jax.shard_map(
        per_device,
        mesh=mesh,
        in_specs=(
            P("exp", None, None),
            P("exp", "ctx", None),
            P("exp", "ctx", None),
            P("exp", None, None),
            P("exp", None, None),
            P("exp"),
            P("exp", None, None),
            P("ctx", None),
            P(),
            P("exp", None, None),
            P("exp", None, None),
            P("exp", None, "ctx"),
            P("exp", None, "ctx"),
            P("exp", "ctx", None),
        ),
        out_specs=P("exp", None, None),
        check_vma=False,
    )
```

```python
import functools
import math

import jax
import jax.numpy as jnp
from jax import lax
from jax.experimental import pallas as pl
from jax.experimental.pallas import tpu as pltpu
from jax.sharding import PartitionSpec as P

D = 2048
HEADS = 32
KV_HEADS = 2
HEAD_DIM = 128
EXP_DEV = 4
TOPK = 8
LANES = 128


NORM_EPSILON = 1e-06
MASKED_SCORE = -1e30


def iota(shape, dim):
    return lax.broadcasted_iota(jnp.int32, shape, dim)


def to_column(row, count):
    return jnp.transpose(jnp.broadcast_to(row, (LANES, LANES)))[:count]


def split_three(values):
    high = values.astype(jnp.bfloat16)
    rest = values - high.astype(jnp.float32)
    middle = rest.astype(jnp.bfloat16)
    low = (rest - middle.astype(jnp.float32)).astype(jnp.bfloat16)
    return high, middle, low


def attend_kernel(
    ctx_count, me_ref, len_ref, q_hbm, k_hbm, v_hbm, nk_hbm, nv_hbm, *rest
):
    outs, blocks = rest[:ctx_count], rest[ctx_count]
    q_ref, k_ref, v_ref, nk_ref, nv_ref, sems = rest[ctx_count + 1 :]
    copies = [
        pltpu.make_async_copy(source, target, sems.at[i])
        for i, (source, target) in enumerate(
            (
                (k_hbm, k_ref),
                (q_hbm, q_ref),
                (nk_hbm, nk_ref),
                (v_hbm, v_ref),
                (nv_hbm, nv_ref),
            )
        )
    ]
    for copy in copies:
        copy.start()
    rows, steps, _ = q_ref.shape
    window = k_ref.shape[1]
    row_steps = rows * steps
    group = HEADS // KV_HEADS
    block_heads = HEADS // ctx_count
    high = group * row_steps
    wide = rows * window
    scale = 1.0 / math.sqrt(HEAD_DIM)
    me = me_ref[0]
    for copy in copies:
        copy.wait()
    queries = jnp.concatenate([q_ref[r] for r in range(rows)], 0)
    keys = k_ref[...].reshape(wide, KV_HEADS * HEAD_DIM)
    values = v_ref[...].reshape(wide, KV_HEADS * HEAD_DIM)
    fresh_keys = jnp.concatenate([nk_ref[r] for r in range(rows)], 0)
    fresh_values = jnp.concatenate([nv_ref[r] for r in range(rows)], 0)
    column = iota((1, wide), 1)
    column_row = column // window
    position = me * window + column % window
    limit = jnp.zeros((1, wide), jnp.int32)
    for r in range(rows):
        limit = jnp.where(column_row == r, len_ref[r], limit)
    column_code = jnp.where(position < limit, column_row, -1)
    row_index = iota((high, 1), 0) % row_steps
    row_code = row_index // steps
    row_step = row_index % steps
    fresh_column = iota((1, row_steps), 1)
    fresh_row = jnp.where(me == 0, fresh_column // steps, -1)
    fresh_step = fresh_column % steps
    live = row_code == column_code
    fresh_live = (row_code == fresh_row) & (fresh_step <= row_step)
    contract_last = (((1,), (1,)), ((), ()))
    for kv in range(KV_HEADS):
        lanes = slice(kv * HEAD_DIM, (kv + 1) * HEAD_DIM)
        heads = jnp.concatenate(
            [
                queries[:, h * HEAD_DIM : (h + 1) * HEAD_DIM]
                for h in range(kv * group, (kv + 1) * group)
            ],
            0,
        )
        scores = lax.dot_general(
            heads, keys[:, lanes], contract_last, preferred_element_type=jnp.float32
        )
        fresh = lax.dot_general(
            heads, fresh_keys[:, lanes], contract_last, preferred_element_type=jnp.float32
        )
        scores = jnp.where(live, scores * scale, MASKED_SCORE)
        fresh = jnp.where(fresh_live, fresh * scale, MASKED_SCORE)
        top = jnp.maximum(
            jnp.max(scores, 1, keepdims=True), jnp.max(fresh, 1, keepdims=True)
        )
        terms = jnp.exp(scores - top)
        fresh_terms = jnp.exp(fresh - top)
        total = jnp.sum(terms, 1, keepdims=True) + jnp.sum(fresh_terms, 1, keepdims=True)
        weighted = jnp.dot(
            terms.astype(jnp.bfloat16), values[:, lanes], preferred_element_type=jnp.float32
        ) + jnp.dot(
            fresh_terms.astype(jnp.bfloat16),
            fresh_values[:, lanes],
            preferred_element_type=jnp.float32,
        )
        mean = (weighted / total).astype(jnp.bfloat16)
        level = jnp.broadcast_to(top + jnp.log(total), (high, LANES))
        span = block_heads * row_steps
        for part in range(high // LANES):
            level_row = jnp.transpose(level[part * LANES : (part + 1) * LANES])[:8]
            pieces = split_three(level_row)
            for sub in range(LANES // span):
                dest = (kv * high + part * LANES) // span + sub
                start = part * LANES + sub * span
                blocks[dest, :span, :] = mean[start : start + span]
                for i, piece in enumerate(pieces):
                    if sub > 0:
                        piece = jnp.concatenate(
                            [piece[:, sub * span :], piece[:, : sub * span]], 1
                        )
                    blocks[dest, span + 16 * i : span + 16 * (i + 1), :] = jnp.concatenate(
                        [piece, piece], 0
                    )
    for k in range(ctx_count):
        outs[k][...] = blocks[me ^ k]


def project_kernel(ctx_count, me_ref, w_ref, *rest):
    parts, own, outs, blocks = (
        rest[:ctx_count],
        rest[ctx_count],
        rest[ctx_count + 1 : 2 * ctx_count],
        rest[2 * ctx_count],
    )
    block_heads = HEADS // ctx_count
    span = parts[0].shape[0] - 48
    row_steps = span // block_heads
    width = D // ctx_count
    levels = [
        sum(
            part[span + 16 * i : span + 16 * (i + 1), :].astype(jnp.float32)[:1]
            for i in range(3)
        )
        for part in parts
    ]
    top = functools.reduce(jnp.maximum, levels)
    factors = [jnp.exp(level - top) for level in levels]
    total = functools.reduce(jnp.add, factors)
    mixed = None
    for part, factor in zip(parts, factors):
        term = part[:span, :].astype(jnp.float32) * to_column(factor / total, span)
        mixed = term if mixed is None else mixed + term
    mixed = mixed.astype(jnp.bfloat16)
    attended = jnp.concatenate(
        [mixed[h * row_steps : (h + 1) * row_steps] for h in range(block_heads)], 1
    )
    for dest in range(ctx_count):
        projected = jnp.dot(
            attended,
            w_ref[:, dest * width : (dest + 1) * width],
            preferred_element_type=jnp.float32,
        )
        for q in range(width // LANES):
            blocks[dest, q * row_steps : (q + 1) * row_steps, :] = projected[
                :, q * LANES : (q + 1) * LANES
            ]
    me = me_ref[0]
    own[...] = blocks[me]
    for k in range(1, ctx_count):
        outs[k - 1][...] = blocks[me ^ k].astype(jnp.bfloat16)


def route_kernel(
    ctx_count, exp_count, capacity, me_ref, ids_ref, weights_ref, residual_ref,
    selector_ref, high_ref, low_ref, slice_ref
):
    rows, steps, _ = residual_ref.shape
    row_steps = rows * steps
    chunks = D // ctx_count // LANES
    shard_count = ctx_count // EXP_DEV
    high, wide = chunks * row_steps, ctx_count * exp_count * chunks * capacity
    ids = jnp.concatenate([ids_ref[...]] * chunks, 0)
    weights = jnp.concatenate([weights_ref[...]] * chunks, 0)
    column = iota((1, wide), 1)
    slot = column % capacity
    chunk = column // capacity % chunks
    dest = column // (capacity * chunks)
    expert = dest % exp_count * EXP_DEV + dest // exp_count // shard_count
    matched = jnp.zeros((high, wide), jnp.float32)
    weight = jnp.zeros((high, wide), jnp.float32)
    for k in range(TOPK):
        hit = ids[:, k : k + 1] == expert
        matched = jnp.where(hit, 1.0, matched)
        weight = jnp.where(hit, weights[:, k : k + 1], weight)
    earlier_row, earlier_column = iota((high, high), 0), iota((high, high), 1)
    earlier = (earlier_column < earlier_row) & (
        earlier_column // row_steps == earlier_row // row_steps
    )
    rank = jnp.dot(
        jnp.where(earlier, 1.0, 0.0).astype(jnp.bfloat16),
        matched.astype(jnp.bfloat16),
        preferred_element_type=jnp.float32,
    )
    row_chunk = iota((high, 1), 0) // row_steps
    chosen = (
        (matched > 0.0) & (rank == slot.astype(jnp.float32)) & (row_chunk == chunk)
    )
    selector_ref[...] = jnp.where(chosen, 1.0, 0.0).astype(jnp.bfloat16)
    weight = jnp.where(chosen, weight, 0.0)
    weight_high = weight.astype(jnp.bfloat16)
    high_ref[...] = weight_high
    low_ref[...] = (weight - weight_high.astype(jnp.float32)).astype(jnp.bfloat16)
    me = me_ref[0]
    for q in range(chunks):
        start = pl.multiple_of((me * chunks + q) * LANES, LANES)
        piece = jnp.concatenate(
            [residual_ref[r, :, pl.ds(start, LANES)] for r in range(rows)], 0
        )
        slice_ref[q * row_steps : (q + 1) * row_steps, :] = piece.astype(jnp.float32)


def dispatch_kernel(ctx_count, residual_ref, selector_ref, *rest):
    parts, state_ref, out_ref = rest[:ctx_count], rest[ctx_count], rest[ctx_count + 1]
    state = residual_ref[...]
    for part in parts:
        state = state + part[...].astype(jnp.float32)
    state_ref[...] = state
    out_ref[...] = lax.dot_general(
        selector_ref[...],
        state.astype(jnp.bfloat16),
        (((0,), (0,)), ((), ())),
        preferred_element_type=jnp.float32,
    ).astype(jnp.bfloat16)


def expert_kernel(
    ctx_count, exp_count, capacity, in_ref, gain_ref, gate_ref, up_ref, down_ref, out_ref
):
    chunks = D // ctx_count // LANES
    block = exp_count * chunks * capacity
    named = exp_count * capacity
    wanted, given = iota((block, block), 0), iota((block, block), 1)
    source = (
        wanted // capacity % exp_count * (chunks * capacity)
        + wanted // named * capacity
        + wanted % capacity
    )
    order = jnp.where(source == given, 1.0, 0.0).astype(jnp.bfloat16)
    pieces = []
    for c in range(ctx_count):
        part = jnp.dot(
            order, in_ref[c * block : (c + 1) * block, :], preferred_element_type=jnp.float32
        )
        pieces += [part[q * named : (q + 1) * named] for q in range(chunks)]
    state = jnp.concatenate(pieces, 1)
    gains = gain_ref[...].astype(jnp.float32)
    gain = jnp.concatenate([gains[i : i + 1] for i in range(D // LANES)], 1)
    normed = (
        state
        * lax.rsqrt(jnp.mean(state * state, -1, keepdims=True) + NORM_EPSILON)
        * gain
    ).astype(jnp.bfloat16)
    gate = jnp.dot(normed, gate_ref[0], preferred_element_type=jnp.float32)
    up = jnp.dot(normed, up_ref[0], preferred_element_type=jnp.float32)
    activation = (gate / (1.0 + jnp.exp(-gate)) * up).astype(jnp.bfloat16)
    result = jnp.dot(activation, down_ref[0], preferred_element_type=jnp.float32).astype(
        jnp.bfloat16
    )
    for c in range(ctx_count):
        part = jnp.concatenate(
            [
                result[:, (c * chunks + q) * LANES : (c * chunks + q + 1) * LANES]
                for q in range(chunks)
            ],
            0,
        )
        out_ref[c * block : (c + 1) * block, :] = lax.dot_general(
            order, part, (((0,), (0,)), ((), ())), preferred_element_type=jnp.float32
        ).astype(jnp.bfloat16)


def combine_kernel(state_ref, high_ref, low_ref, in_ref, out_ref):
    returned = in_ref[...]
    mixture = jnp.dot(high_ref[...], returned, preferred_element_type=jnp.float32) + jnp.dot(
        low_ref[...], returned, preferred_element_type=jnp.float32
    )
    out_ref[...] = (state_ref[...] + mixture).astype(jnp.bfloat16)


def assemble_kernel(ctx_count, me_ref, *rest):
    parts, out_ref = rest[:ctx_count], rest[ctx_count]
    rows, steps, _ = out_ref.shape
    row_steps = rows * steps
    chunks = D // ctx_count // LANES
    me = me_ref[0]
    for k, part in enumerate(parts):
        for q in range(chunks):
            start = pl.multiple_of(((me ^ k) * chunks + q) * LANES, LANES)
            for r in range(rows):
                first = q * row_steps + r * steps
                out_ref[r, :, pl.ds(start, LANES)] = part[first : first + steps, :]


VMEM = pl.BlockSpec(memory_space=pltpu.VMEM)
HBM = pl.BlockSpec(memory_space=pltpu.HBM)
SMEM = pl.BlockSpec(memory_space=pltpu.SMEM)


def call(kernel, name, in_specs, out_shapes, operands, scratch=(), vmem=4 * 1024 * 1024, cost=None):
    return pl.pallas_call(
        kernel,
        name=name,
        in_specs=in_specs,
        out_specs=[VMEM] * len(out_shapes),
        out_shape=[jax.ShapeDtypeStruct(shape, dtype) for shape, dtype in out_shapes],
        scratch_shapes=list(scratch),
        compiler_params=pltpu.CompilerParams(vmem_limit_bytes=vmem),
        cost_estimate=cost,
    )(*operands)


def cost(micros):
    return pl.CostEstimate(flops=micros * 1_000_000_000, bytes_accessed=1 << 20, transcendentals=0)


def swap(blocks):
    count = lax.axis_size("ctx")
    return [
        lax.ppermute(block, "ctx", [(i, i ^ k) for i in range(count)])
        for k, block in enumerate(blocks, 1)
    ]


def per_device(
    queries,
    cache_keys,
    cache_values,
    new_keys,
    new_values,
    lengths,
    residual,
    out_weight,
    norm_gain,
    expert_ids,
    expert_weights,
    gate_proj,
    up_proj,
    down_proj,
):
    row_count, step_count, _ = queries.shape
    row_steps = row_count * step_count
    n = lax.axis_size("ctx")
    exp_count = lax.axis_size("exp")
    me = lax.axis_index("ctx").astype(jnp.int32).reshape(1)
    experts_all = exp_count * EXP_DEV
    capacity = max(2, (row_steps * TOPK + experts_all - 1) // experts_all)
    chunks = D // n // LANES
    device_rows = chunks * capacity
    all_rows = n * exp_count * device_rows
    span = HEADS // n * row_steps
    bf16, f32 = jnp.bfloat16, jnp.float32

    message = (span + 48, LANES)
    inputs = (queries, cache_keys, cache_values, new_keys, new_values)
    sent = call(
        functools.partial(attend_kernel, n),
        "attend",
        [SMEM, SMEM] + [HBM] * 5,
        [(message, bf16)] * n,
        (me, lengths) + tuple(pltpu.with_memory_space_constraint(x, pltpu.HBM) for x in inputs),
        [pltpu.VMEM((n,) + message, bf16)]
        + [pltpu.VMEM(x.shape, x.dtype) for x in inputs]
        + [pltpu.SemaphoreType.DMA((len(inputs),))],
        cost=cost(10),
    )
    got = swap(sent[1:])
    selector, weight_high, weight_low, residual_part = call(
        functools.partial(route_kernel, n, exp_count, capacity),
        "route",
        [SMEM] + [VMEM] * 3,
        [((chunks * row_steps, all_rows), bf16)] * 3 + [((chunks * row_steps, LANES), f32)],
        (
            me,
            expert_ids.reshape(row_steps, TOPK),
            expert_weights.reshape(row_steps, TOPK),
            residual,
        ),
    )
    part = (chunks * row_steps, LANES)
    sent = call(
        functools.partial(project_kernel, n),
        "project",
        [SMEM] + [VMEM] * (n + 1),
        [(part, f32)] + [(part, bf16)] * (n - 1),
        (me, out_weight, sent[0], *got),
        [pltpu.VMEM((n,) + part, f32)],
        8 * 1024 * 1024,
        cost(10),
    )
    got = swap(sent[1:])
    state, outgoing = call(
        functools.partial(dispatch_kernel, n),
        "dispatch",
        [VMEM] * (n + 2),
        [(part, f32), ((all_rows, LANES), bf16)],
        (residual_part, selector, sent[0], *got),
        cost=cost(10),
    )

    def exchange(rows):
        rows = rows.reshape(n * exp_count, device_rows, LANES)
        rows = lax.all_to_all(rows, ("ctx", "exp"), split_axis=0, concat_axis=0, tiled=True)
        return rows.reshape(all_rows, LANES)

    arrived = exchange(outgoing)
    (results,) = call(
        functools.partial(expert_kernel, n, exp_count, capacity),
        "experts",
        [VMEM] * 5,
        [((all_rows, LANES), bf16)],
        (arrived, norm_gain.reshape(D // LANES, LANES), gate_proj, up_proj, down_proj),
        (),
        20 * 1024 * 1024,
        cost(10),
    )
    returned = exchange(results)
    (layer_part,) = call(
        combine_kernel,
        "combine",
        [VMEM] * 4,
        [(part, bf16)],
        (state, weight_high, weight_low, returned),
    )
    got = swap([layer_part] * (n - 1))
    (layer_rows,) = call(
        functools.partial(assemble_kernel, n),
        "assemble",
        [SMEM] + [VMEM] * n,
        [((row_count, step_count, D), bf16)],
        (me, layer_part, *got),
    )
    return layer_rows


def solution(mesh):
    return jax.shard_map(
        per_device,
        mesh=mesh,
        in_specs=(
            P("exp", None, None),
            P("exp", "ctx", None),
            P("exp", "ctx", None),
            P("exp", None, None),
            P("exp", None, None),
            P("exp"),
            P("exp", None, None),
            P("ctx", None),
            P(),
            P("exp", None, None),
            P("exp", None, None),
            P("exp", None, "ctx"),
            P("exp", None, "ctx"),
            P("exp", "ctx", None),
        ),
        out_specs=P("exp", None, None),
        check_vma=False,
    )
```

```python
import functools
import math

import jax
import jax.numpy as jnp
from jax import lax
from jax.experimental import pallas as pl
from jax.experimental.pallas import tpu as pltpu
from jax.sharding import PartitionSpec as P

D = 2048
HEADS = 32
KV_HEADS = 2
HEAD_DIM = 128
EXP_DEV = 4
TOPK = 8
LANES = 128
SUBLANES = 8


NORM_EPSILON = 1e-06
MASKED_SCORE = -1e30


def iota(shape, dim):
    return lax.broadcasted_iota(jnp.int32, shape, dim)


def to_column(row, count):
    return jnp.transpose(jnp.broadcast_to(row, (LANES, LANES)))[:count]


def split_three(values):
    high = values.astype(jnp.bfloat16)
    rest = values - high.astype(jnp.float32)
    middle = rest.astype(jnp.bfloat16)
    low = (rest - middle.astype(jnp.float32)).astype(jnp.bfloat16)
    return high, middle, low


def every(values, first, step):
    count = values.shape[0] // SUBLANES
    return jnp.concatenate(
        [values[i * SUBLANES : (i + 1) * SUBLANES] for i in range(first, count, step)], 0
    )


def interleave(parts):
    count = parts[0].shape[0] // SUBLANES
    return jnp.concatenate(
        [part[i * SUBLANES : (i + 1) * SUBLANES] for i in range(count) for part in parts], 0
    )


def attend_kernel(
    ctx_count, me_ref, len_hbm, q_hbm, k_hbm, v_hbm, nk_hbm, nv_hbm, *rest
):
    outs, blocks = rest[:ctx_count], rest[ctx_count]
    len_ref, q_ref, k_ref, v_ref, nk_ref, nv_ref, sems = rest[ctx_count + 1 :]
    early, late = [
        [pltpu.make_async_copy(source, target, sems.at[i]) for i, source, target in group]
        for group in (
            (
                (0, k_hbm, k_ref),
                (1, q_hbm, q_ref),
                (2, len_hbm, len_ref),
                (3, nk_hbm, nk_ref),
            ),
            ((4, v_hbm, v_ref), (5, nv_hbm, nv_ref)),
        )
    ]
    for copy in early + late:
        copy.start()
    rows, steps, _ = q_ref.shape
    window = k_ref.shape[1]
    row_steps = rows * steps
    group = HEADS // KV_HEADS
    block_heads = HEADS // ctx_count
    high = group * row_steps
    wide = rows * window
    pieces = row_steps // SUBLANES
    piece_rows = rows // pieces
    piece_high = group * SUBLANES
    piece_wide = piece_rows * window
    scale = 1.0 / math.sqrt(HEAD_DIM)
    me = me_ref[0]
    for copy in early + late:
        copy.wait()
    values = v_ref[...].reshape(wide, KV_HEADS * HEAD_DIM)
    fresh_values = jnp.concatenate([nv_ref[r] for r in range(rows)], 0)
    queries = jnp.concatenate([q_ref[r] for r in range(rows)], 0)
    keys = k_ref[...].reshape(wide, KV_HEADS * HEAD_DIM)
    fresh_keys = jnp.concatenate([nk_ref[r] for r in range(rows)], 0)
    column = iota((1, piece_wide), 1)
    column_row = column // window
    position = me * window + column % window
    row_index = iota((piece_high, 1), 0) % SUBLANES
    fresh_column = iota((1, row_steps), 1)
    live, fresh_live = [], []
    for p in range(pieces):
        limit = jnp.zeros((1, piece_wide), jnp.int32)
        for r in range(piece_rows):
            limit = jnp.where(column_row == r, len_ref[p * piece_rows + r], limit)
        live.append(row_index // steps == jnp.where(position < limit, column_row, -1))
        fresh_row = jnp.where(me == 0, fresh_column // steps - p * piece_rows, -1)
        fresh_live.append(
            (row_index // steps == fresh_row) & (fresh_column % steps <= row_index % steps)
        )
    contract_last = (((1,), (1,)), ((), ()))
    for kv in range(KV_HEADS):
        lanes = slice(kv * HEAD_DIM, (kv + 1) * HEAD_DIM)
        heads = jnp.concatenate(
            [
                queries[:, h * HEAD_DIM : (h + 1) * HEAD_DIM]
                for h in range(kv * group, (kv + 1) * group)
            ],
            0,
        )
        scores = lax.dot_general(
            heads, keys[:, lanes], contract_last, preferred_element_type=jnp.float32
        )
        fresh = lax.dot_general(
            heads, fresh_keys[:, lanes], contract_last, preferred_element_type=jnp.float32
        )
        means, levels = [], []
        for p in range(pieces):
            span = slice(p * piece_wide, (p + 1) * piece_wide)
            part = every(scores[:, span], p, pieces)
            part = jnp.where(live[p], part * scale, MASKED_SCORE)
            last = every(fresh, p, pieces)
            last = jnp.where(fresh_live[p], last * scale, MASKED_SCORE)
            top = jnp.maximum(
                jnp.max(part, 1, keepdims=True), jnp.max(last, 1, keepdims=True)
            )
            terms = jnp.exp(part - top)
            last_terms = jnp.exp(last - top)
            total = jnp.sum(terms, 1, keepdims=True) + jnp.sum(last_terms, 1, keepdims=True)
            weighted = jnp.dot(
                terms.astype(jnp.bfloat16),
                values[span, lanes],
                preferred_element_type=jnp.float32,
            ) + jnp.dot(
                last_terms.astype(jnp.bfloat16),
                fresh_values[:, lanes],
                preferred_element_type=jnp.float32,
            )
            means.append(weighted / total)
            levels.append(jnp.broadcast_to(top + jnp.log(total), (piece_high, LANES)))
        mean = interleave(means).astype(jnp.bfloat16)
        level = interleave(levels)
        span = block_heads * row_steps
        for part in range(high // LANES):
            level_row = jnp.transpose(level[part * LANES : (part + 1) * LANES])[:SUBLANES]
            splits = split_three(level_row)
            for sub in range(LANES // span):
                dest = (kv * high + part * LANES) // span + sub
                start = part * LANES + sub * span
                blocks[dest, :span, :] = mean[start : start + span]
                for i, piece in enumerate(splits):
                    if sub > 0:
                        piece = jnp.concatenate(
                            [piece[:, sub * span :], piece[:, : sub * span]], 1
                        )
                    blocks[dest, span + 16 * i : span + 16 * (i + 1), :] = jnp.concatenate(
                        [piece, piece], 0
                    )
    for k in range(ctx_count):
        outs[k][...] = blocks[me ^ k]


def project_kernel(ctx_count, w_ref, *rest):
    parts, out_ref = rest[:ctx_count], rest[ctx_count]
    block_heads = HEADS // ctx_count
    span = parts[0].shape[0] - 48
    row_steps = span // block_heads
    levels = [
        sum(
            part[span + 16 * i : span + 16 * (i + 1), :].astype(jnp.float32)[:1]
            for i in range(3)
        )
        for part in parts
    ]
    top = functools.reduce(jnp.maximum, levels)
    factors = [jnp.exp(level - top) for level in levels]
    total = functools.reduce(jnp.add, factors)
    mixed = None
    for part, factor in zip(parts, factors):
        term = part[:span, :].astype(jnp.float32) * to_column(factor / total, span)
        mixed = term if mixed is None else mixed + term
    mixed = mixed.astype(jnp.bfloat16)
    attended = jnp.concatenate(
        [mixed[h * row_steps : (h + 1) * row_steps] for h in range(block_heads)], 1
    )
    out_ref[...] = jnp.dot(
        attended, w_ref[...], preferred_element_type=jnp.float32
    ).astype(jnp.bfloat16)


def route_kernel(
    ctx_count, exp_count, capacity, me_ref, home_ref, ids_ref, weights_ref, residual_ref,
    selector_ref, high_ref, low_ref, rows_ref
):
    rows, steps, _ = residual_ref.shape
    row_steps = rows * steps
    wide = exp_count * capacity
    me, home = me_ref[0], home_ref[0]
    column = iota((1, wide), 1)
    slot = column % capacity
    other = column // capacity % 2
    hop = column // (2 * capacity)
    crossed = jnp.where(hop == 0, 0, 1)
    device = home ^ (2 * hop) ^ crossed ^ other
    expert = device * EXP_DEV + me // (ctx_count // EXP_DEV)
    matched = jnp.zeros((row_steps, wide), jnp.float32)
    weight = jnp.zeros((row_steps, wide), jnp.float32)
    for k in range(TOPK):
        hit = ids_ref[:, k : k + 1] == expert
        matched = jnp.where(hit, 1.0, matched)
        weight = jnp.where(hit, weights_ref[:, k : k + 1], weight)
    earlier = iota((row_steps, row_steps), 1) < iota((row_steps, row_steps), 0)
    rank = jnp.dot(
        jnp.where(earlier, 1.0, 0.0).astype(jnp.bfloat16),
        matched.astype(jnp.bfloat16),
        preferred_element_type=jnp.float32,
    )
    chosen = (matched > 0.0) & (rank == slot.astype(jnp.float32))
    selector_ref[...] = jnp.where(chosen, 1.0, 0.0).astype(jnp.bfloat16)
    weight = jnp.where(chosen, weight, 0.0)
    weight_high = weight.astype(jnp.bfloat16)
    high_ref[...] = weight_high
    low_ref[...] = (weight - weight_high.astype(jnp.float32)).astype(jnp.bfloat16)
    rows_ref[...] = jnp.concatenate(
        [residual_ref[r].astype(jnp.float32) for r in range(rows)], 0
    )


def tree_sum(parts):
    values = [part[...].astype(jnp.float32) for part in parts]
    while len(values) > 1:
        values = [values[i] + values[i + 1] for i in range(0, len(values), 2)]
    return values[0]


def dispatch_kernel(ctx_count, residual_ref, selector_ref, *rest):
    parts, state_ref, outs = rest[:ctx_count], rest[ctx_count], rest[ctx_count + 1 :]
    state = residual_ref[...] + tree_sum(parts)
    state_ref[...] = state
    picked = lax.dot_general(
        selector_ref[...],
        state.astype(jnp.bfloat16),
        (((0,), (0,)), ((), ())),
        preferred_element_type=jnp.float32,
    )
    block = outs[0].shape[0]
    for j, out in enumerate(outs):
        out[...] = picked[j * block : (j + 1) * block].astype(jnp.bfloat16)


def gather_kernel(*refs):
    blocks, keep_ref, send_ref = refs[:-2], refs[-2], refs[-1]
    half = blocks[0].shape[0] // 2
    values = [block[...].astype(jnp.float32) for block in blocks]
    keep_ref[...] = jnp.concatenate([value[:half] for value in values], 0).astype(jnp.bfloat16)
    send_ref[...] = jnp.concatenate([value[half:] for value in values], 0).astype(jnp.bfloat16)


def expert_kernel(kept_ref, got_ref, gain_ref, gate_ref, up_ref, down_ref, keep_ref, send_ref):
    half = kept_ref.shape[0]
    state = jnp.concatenate(
        [kept_ref[...].astype(jnp.float32), got_ref[...].astype(jnp.float32)], 0
    )
    gains = gain_ref[...].astype(jnp.float32)
    gain = jnp.concatenate([gains[i : i + 1] for i in range(D // LANES)], 1)
    normed = (
        state
        * lax.rsqrt(jnp.mean(state * state, -1, keepdims=True) + NORM_EPSILON)
        * gain
    ).astype(jnp.bfloat16)
    spare = max(0, LANES - 2 * half)
    if spare:
        normed = jnp.concatenate([normed, jnp.zeros((spare, D), jnp.bfloat16)], 0)
    gate = jnp.dot(normed, gate_ref[0], preferred_element_type=jnp.float32)
    up = jnp.dot(normed, up_ref[0], preferred_element_type=jnp.float32)
    activation = (gate / (1.0 + jnp.exp(-gate)) * up).astype(jnp.bfloat16)
    result = jnp.dot(activation, down_ref[0], preferred_element_type=jnp.float32)
    keep_ref[...] = result[:half].astype(jnp.bfloat16)
    send_ref[...] = result[half : 2 * half].astype(jnp.bfloat16)


def scatter_kernel(kept_ref, got_ref, *outs):
    half = outs[0].shape[0] // 2
    kept, got = kept_ref[...].astype(jnp.float32), got_ref[...].astype(jnp.float32)
    for j, out in enumerate(outs):
        span = slice(j * half, (j + 1) * half)
        out[...] = jnp.concatenate([kept[span], got[span]], 0).astype(jnp.bfloat16)


def combine_kernel(high_ref, low_ref, *refs):
    blocks, out_ref = refs[:-1], refs[-1]
    returned = jnp.concatenate([block[...].astype(jnp.float32) for block in blocks], 0).astype(
        jnp.bfloat16
    )
    mixture = jnp.dot(high_ref[...], returned, preferred_element_type=jnp.float32) + jnp.dot(
        low_ref[...], returned, preferred_element_type=jnp.float32
    )
    out_ref[...] = mixture.astype(jnp.bfloat16)


def finish_kernel(state_ref, *refs):
    parts, out_ref = refs[:-1], refs[-1]
    rows, steps, _ = out_ref.shape
    layer = (state_ref[...] + tree_sum(parts)).astype(jnp.bfloat16)
    for r in range(rows):
        out_ref[r] = layer[r * steps : (r + 1) * steps]


VMEM = pl.BlockSpec(memory_space=pltpu.VMEM)
HBM = pl.BlockSpec(memory_space=pltpu.HBM)
SMEM = pl.BlockSpec(memory_space=pltpu.SMEM)


def call(kernel, name, in_specs, out_shapes, operands, scratch=(), out_spec=None, vmem=4 * 1024 * 1024, cost=None):
    return pl.pallas_call(
        kernel,
        name=name,
        in_specs=in_specs,
        out_specs=[out_spec or VMEM] * len(out_shapes),
        out_shape=[jax.ShapeDtypeStruct(shape, dtype) for shape, dtype in out_shapes],
        scratch_shapes=list(scratch),
        compiler_params=pltpu.CompilerParams(vmem_limit_bytes=vmem),
        cost_estimate=cost,
    )(*operands)


def cost(micros):
    return pl.CostEstimate(flops=micros * 1_000_000_000, bytes_accessed=1 << 20, transcendentals=0)


def move(block, ctx_hop, exp_hop):
    n, exp_count = lax.axis_size("ctx"), lax.axis_size("exp")
    pairs = [
        (c * exp_count + e, (c ^ ctx_hop) * exp_count + (e ^ exp_hop))
        for c in range(n)
        for e in range(exp_count)
    ]
    return lax.ppermute(block, ("ctx", "exp"), pairs)


def per_device(
    queries,
    cache_keys,
    cache_values,
    new_keys,
    new_values,
    lengths,
    residual,
    out_weight,
    norm_gain,
    expert_ids,
    expert_weights,
    gate_proj,
    up_proj,
    down_proj,
):
    row_count, step_count, _ = queries.shape
    row_steps = row_count * step_count
    n = lax.axis_size("ctx")
    exp_count = lax.axis_size("exp")
    me = lax.axis_index("ctx").astype(jnp.int32).reshape(1)
    home = lax.axis_index("exp").astype(jnp.int32).reshape(1)
    experts_all = exp_count * EXP_DEV
    capacity = max(2, (row_steps * TOPK + experts_all - 1) // experts_all)
    chips = exp_count // 2
    span = HEADS // n * row_steps
    bf16, f32 = jnp.bfloat16, jnp.float32
    hidden = (row_steps, D)
    block = (2 * capacity, D)
    half = (chips * capacity, D)

    message = (span + 48, LANES)
    inputs = (lengths, queries, cache_keys, cache_values, new_keys, new_values)
    sent = call(
        functools.partial(attend_kernel, n),
        "attend",
        [SMEM] + [HBM] * 6,
        [(message, bf16)] * n,
        (me,) + tuple(pltpu.with_memory_space_constraint(x, pltpu.HBM) for x in inputs),
        [pltpu.VMEM((n,) + message, bf16)]
        + [pltpu.SMEM(lengths.shape, lengths.dtype)]
        + [pltpu.VMEM(x.shape, x.dtype) for x in inputs[1:]]
        + [pltpu.SemaphoreType.DMA((len(inputs),))],
        cost=cost(10),
    )
    got = [move(x, j, 1) for j, x in enumerate(sent)]
    selector, weight_high, weight_low, residual_rows = call(
        functools.partial(route_kernel, n, exp_count, capacity),
        "route",
        [SMEM] * 2 + [VMEM] * 3,
        [((row_steps, exp_count * capacity), bf16)] * 3 + [(hidden, f32)],
        (
            me,
            home,
            expert_ids.reshape(row_steps, TOPK),
            expert_weights.reshape(row_steps, TOPK),
            residual,
        ),
    )
    (projected,) = call(
        functools.partial(project_kernel, n),
        "project",
        [VMEM] * (n + 1),
        [(hidden, bf16)],
        (out_weight, *got),
        vmem=8 * 1024 * 1024,
        cost=cost(10),
    )
    got = [move(projected, j, 1) for j in range(n)]
    state, *outgoing = call(
        functools.partial(dispatch_kernel, n),
        "dispatch",
        [VMEM] * (n + 2),
        [(hidden, f32)] + [(block, bf16)] * chips,
        (residual_rows, selector, *got),
        cost=cost(10),
    )

    def spread(blocks):
        return [blocks[0]] + [move(blocks[j], 0, 2 * j + 1) for j in range(1, chips)]

    kept, sent = call(
        gather_kernel,
        "gather",
        [VMEM] * chips,
        [(half, bf16)] * 2,
        spread(outgoing),
    )
    kept, sent = call(
        expert_kernel,
        "experts",
        [VMEM] * 6,
        [(half, bf16)] * 2,
        (
            kept,
            move(sent, 0, 1),
            norm_gain.reshape(D // LANES, LANES),
            gate_proj,
            up_proj,
            down_proj,
        ),
        vmem=20 * 1024 * 1024,
        cost=cost(10),
    )
    results = call(
        scatter_kernel,
        "scatter",
        [VMEM] * 2,
        [(block, bf16)] * chips,
        (kept, move(sent, 0, 1)),
    )
    (mixture,) = call(
        combine_kernel,
        "combine",
        [VMEM] * (chips + 2),
        [(hidden, bf16)],
        (weight_high, weight_low, *spread(results)),
    )
    got = [mixture] + [move(mixture, j, 0) for j in range(1, n)]
    (layer_rows,) = call(
        finish_kernel,
        "finish",
        [VMEM] * (n + 1),
        [((row_count, step_count, D), bf16)],
        (state, *got),
    )
    return layer_rows


def solution(mesh):
    return jax.shard_map(
        per_device,
        mesh=mesh,
        in_specs=(
            P("exp", None, None),
            P("exp", "ctx", None),
            P("exp", "ctx", None),
            P("exp", None, None),
            P("exp", None, None),
            P("exp"),
            P("exp", None, None),
            P("ctx", None),
            P(),
            P("exp", None, None),
            P("exp", None, None),
            P("exp", None, "ctx"),
            P("exp", None, "ctx"),
            P("exp", "ctx", None),
        ),
        out_specs=P("exp", None, None),
        check_vma=False,
    )
```

```python
import functools
import math

import jax
import jax.numpy as jnp
from jax import lax
from jax.experimental import pallas as pl
from jax.experimental.pallas import tpu as pltpu
from jax.sharding import PartitionSpec as P

D = 2048
HEADS = 32
KV_HEADS = 2
HEAD_DIM = 128
EXP_DEV = 4
TOPK = 8
LANES = 128
SUBLANES = 8
STAT_ROWS = 16


NORM_EPSILON = 1e-06
MASKED_SCORE = -1e30


def iota(shape, dim):
    return lax.broadcasted_iota(jnp.int32, shape, dim)


def to_column(row, count):
    return jnp.transpose(jnp.broadcast_to(row, (LANES, LANES)))[:count]


def split_three(values):
    high = values.astype(jnp.bfloat16).astype(jnp.float32)
    middle = (values - high).astype(jnp.bfloat16).astype(jnp.float32)
    return high, middle, values - high - middle


def every(values, first, step):
    count = values.shape[0] // SUBLANES
    return jnp.concatenate(
        [values[i * SUBLANES : (i + 1) * SUBLANES] for i in range(first, count, step)], 0
    )


def interleave(parts):
    count = parts[0].shape[0] // SUBLANES
    return jnp.concatenate(
        [part[i * SUBLANES : (i + 1) * SUBLANES] for i in range(count) for part in parts], 0
    )


def attend_kernel(
    ctx_count, me_ref, len_hbm, q_hbm, k_hbm, v_hbm, nk_hbm, nv_hbm, *rest
):
    outs, blocks = rest[:ctx_count], rest[ctx_count]
    len_ref, q_ref, k_ref, v_ref, nk_ref, nv_ref, sems = rest[ctx_count + 1 :]
    early, late = [
        [pltpu.make_async_copy(source, target, sems.at[i]) for i, source, target in group]
        for group in (
            (
                (0, k_hbm, k_ref),
                (1, q_hbm, q_ref),
                (2, len_hbm, len_ref),
                (3, nk_hbm, nk_ref),
            ),
            ((4, v_hbm, v_ref), (5, nv_hbm, nv_ref)),
        )
    ]
    for copy in early + late:
        copy.start()
    rows, steps, _ = q_ref.shape
    window = k_ref.shape[1]
    row_steps = rows * steps
    group = HEADS // KV_HEADS
    block_heads = HEADS // ctx_count
    high = group * row_steps
    wide = rows * window
    pieces = row_steps // SUBLANES
    piece_rows = rows // pieces
    piece_high = group * SUBLANES
    piece_wide = piece_rows * window
    scale = 1.0 / math.sqrt(HEAD_DIM)
    me = me_ref[0]
    for copy in early + late:
        copy.wait()
    values = v_ref[...].reshape(wide, KV_HEADS * HEAD_DIM)
    fresh_values = jnp.concatenate([nv_ref[r] for r in range(rows)], 0)
    queries = jnp.concatenate([q_ref[r] for r in range(rows)], 0)
    keys = k_ref[...].reshape(wide, KV_HEADS * HEAD_DIM)
    fresh_keys = jnp.concatenate([nk_ref[r] for r in range(rows)], 0)
    column = iota((1, piece_wide), 1)
    column_row = column // window
    position = me * window + column % window
    row_index = iota((piece_high, 1), 0) % SUBLANES
    fresh_column = iota((1, row_steps), 1)
    live, fresh_live = [], []
    for p in range(pieces):
        limit = jnp.zeros((1, piece_wide), jnp.int32)
        for r in range(piece_rows):
            limit = jnp.where(column_row == r, len_ref[p * piece_rows + r], limit)
        live.append(row_index // steps == jnp.where(position < limit, column_row, -1))
        fresh_row = jnp.where(me == 0, fresh_column // steps - p * piece_rows, -1)
        fresh_live.append(
            (row_index // steps == fresh_row) & (fresh_column % steps <= row_index % steps)
        )
    contract_last = (((1,), (1,)), ((), ()))
    for kv in range(KV_HEADS):
        lanes = slice(kv * HEAD_DIM, (kv + 1) * HEAD_DIM)
        heads = jnp.concatenate(
            [
                queries[:, h * HEAD_DIM : (h + 1) * HEAD_DIM]
                for h in range(kv * group, (kv + 1) * group)
            ],
            0,
        )
        scores = lax.dot_general(
            heads, keys[:, lanes], contract_last, preferred_element_type=jnp.float32
        )
        fresh = lax.dot_general(
            heads, fresh_keys[:, lanes], contract_last, preferred_element_type=jnp.float32
        )
        means, levels = [], []
        for p in range(pieces):
            span = slice(p * piece_wide, (p + 1) * piece_wide)
            part = every(scores[:, span], p, pieces)
            part = jnp.where(live[p], part * scale, MASKED_SCORE)
            last = every(fresh, p, pieces)
            last = jnp.where(fresh_live[p], last * scale, MASKED_SCORE)
            top = jnp.maximum(
                jnp.max(part, 1, keepdims=True), jnp.max(last, 1, keepdims=True)
            )
            terms = jnp.exp(part - top)
            last_terms = jnp.exp(last - top)
            total = jnp.sum(terms, 1, keepdims=True) + jnp.sum(last_terms, 1, keepdims=True)
            weighted = jnp.dot(
                terms.astype(jnp.bfloat16),
                values[span, lanes],
                preferred_element_type=jnp.float32,
            ) + jnp.dot(
                last_terms.astype(jnp.bfloat16),
                fresh_values[:, lanes],
                preferred_element_type=jnp.float32,
            )
            means.append(weighted / total)
            levels.append(jnp.broadcast_to(top + jnp.log(total), (piece_high, LANES)))
        mean = interleave(means).astype(jnp.bfloat16)
        level = interleave(levels)
        span = block_heads * row_steps
        for part in range(high // LANES):
            level_row = jnp.transpose(level[part * LANES : (part + 1) * LANES])[:SUBLANES]
            high_part, middle_part, low_part = split_three(level_row)
            row = iota((SUBLANES, LANES), 0)
            stats = jnp.where(row == 0, high_part, jnp.where(row == 1, middle_part, low_part))
            stats = jnp.concatenate([stats, stats], 0).astype(jnp.bfloat16)
            for sub in range(LANES // span):
                dest = (kv * high + part * LANES) // span + sub
                start = part * LANES + sub * span
                blocks[dest, :span, :] = mean[start : start + span]
                piece = stats
                if sub > 0:
                    piece = jnp.concatenate([stats[:, sub * span :], stats[:, : sub * span]], 1)
                blocks[dest, span:, :] = piece
    for k, out in zip(reversed(range(ctx_count)), outs):
        out[...] = blocks[me ^ k]


def project_kernel(ctx_count, w_ref, *rest):
    parts, out_ref = rest[:ctx_count], rest[ctx_count]
    block_heads = HEADS // ctx_count
    span = parts[0].shape[0] - STAT_ROWS
    row_steps = span // block_heads
    stats = [part[span:, :].astype(jnp.float32) for part in parts]
    levels = [stat[0:1] + stat[1:2] + stat[2:3] for stat in stats]
    top = functools.reduce(jnp.maximum, levels)
    factors = [jnp.exp(level - top) for level in levels]
    total = functools.reduce(jnp.add, factors)
    mixed = None
    for part, factor in zip(parts, factors):
        term = part[:span, :].astype(jnp.float32) * to_column(factor / total, span)
        mixed = term if mixed is None else mixed + term
    mixed = mixed.astype(jnp.bfloat16)
    attended = jnp.concatenate(
        [mixed[h * row_steps : (h + 1) * row_steps] for h in range(block_heads)], 1
    )
    out_ref[...] = jnp.dot(
        attended, w_ref[...], preferred_element_type=jnp.float32
    ).astype(jnp.bfloat16)


def route_kernel(
    ctx_count, exp_count, capacity, me_ref, home_ref, ids_ref, weights_ref, residual_ref,
    selector_ref, high_ref, low_ref, rows_ref
):
    rows, steps, _ = residual_ref.shape
    row_steps = rows * steps
    wide = exp_count * capacity
    me, home = me_ref[0], home_ref[0]
    column = iota((1, wide), 1)
    slot = column % capacity
    other = column // capacity % 2
    hop = column // (2 * capacity)
    crossed = jnp.where(hop == 0, 0, 1)
    device = home ^ (2 * hop) ^ crossed ^ other
    expert = device * EXP_DEV + me // (ctx_count // EXP_DEV)
    matched = jnp.zeros((row_steps, wide), jnp.float32)
    weight = jnp.zeros((row_steps, wide), jnp.float32)
    for k in range(TOPK):
        hit = ids_ref[:, k : k + 1] == expert
        matched = jnp.where(hit, 1.0, matched)
        weight = jnp.where(hit, weights_ref[:, k : k + 1], weight)
    earlier = iota((row_steps, row_steps), 1) < iota((row_steps, row_steps), 0)
    rank = jnp.dot(
        jnp.where(earlier, 1.0, 0.0).astype(jnp.bfloat16),
        matched.astype(jnp.bfloat16),
        preferred_element_type=jnp.float32,
    )
    chosen = (matched > 0.0) & (rank == slot.astype(jnp.float32))
    selector_ref[...] = jnp.where(chosen, 1.0, 0.0).astype(jnp.bfloat16)
    weight = jnp.where(chosen, weight, 0.0)
    weight_high = weight.astype(jnp.bfloat16)
    high_ref[...] = weight_high
    low_ref[...] = (weight - weight_high.astype(jnp.float32)).astype(jnp.bfloat16)
    rows_ref[...] = jnp.concatenate(
        [residual_ref[r].astype(jnp.float32) for r in range(rows)], 0
    )


def tree_sum(parts):
    values = [part[...].astype(jnp.float32) for part in parts]
    while len(values) > 1:
        values = [values[i] + values[i + 1] for i in range(0, len(values), 2)]
    return values[0]


def dispatch_kernel(ctx_count, hops, residual_ref, selector_ref, *rest):
    parts, state_ref, outs = rest[:ctx_count], rest[ctx_count], rest[ctx_count + 1 :]
    state = residual_ref[...] + tree_sum(parts)
    state_ref[...] = state
    picked = lax.dot_general(
        selector_ref[...],
        state.astype(jnp.bfloat16),
        (((0,), (0,)), ((), ())),
        preferred_element_type=jnp.float32,
    )
    block = outs[0].shape[0]
    for j, out in zip(hops, outs):
        out[...] = picked[j * block : (j + 1) * block].astype(jnp.bfloat16)


def gather_kernel(*refs):
    blocks, keep_ref, send_ref = refs[:-2], refs[-2], refs[-1]
    half = blocks[0].shape[0] // 2
    values = [block[...].astype(jnp.float32) for block in blocks]
    keep_ref[...] = jnp.concatenate([value[:half] for value in values], 0).astype(jnp.bfloat16)
    send_ref[...] = jnp.concatenate([value[half:] for value in values], 0).astype(jnp.bfloat16)


def expert_kernel(kept_ref, got_ref, gain_ref, gate_ref, up_ref, down_ref, keep_ref, send_ref):
    half = kept_ref.shape[0]
    state = jnp.concatenate(
        [kept_ref[...].astype(jnp.float32), got_ref[...].astype(jnp.float32)], 0
    )
    gains = gain_ref[...].astype(jnp.float32)
    gain = jnp.concatenate([gains[i : i + 1] for i in range(D // LANES)], 1)
    normed = (
        state
        * lax.rsqrt(jnp.mean(state * state, -1, keepdims=True) + NORM_EPSILON)
        * gain
    ).astype(jnp.bfloat16)
    spare = max(0, LANES - 2 * half)
    if spare:
        normed = jnp.concatenate([normed, jnp.zeros((spare, D), jnp.bfloat16)], 0)
    gate = jnp.dot(normed, gate_ref[0], preferred_element_type=jnp.float32)
    up = jnp.dot(normed, up_ref[0], preferred_element_type=jnp.float32)
    activation = (gate / (1.0 + jnp.exp(-gate)) * up).astype(jnp.bfloat16)
    result = jnp.dot(activation, down_ref[0], preferred_element_type=jnp.float32)
    keep_ref[...] = result[:half].astype(jnp.bfloat16)
    send_ref[...] = result[half : 2 * half].astype(jnp.bfloat16)


def scatter_kernel(kept_ref, got_ref, *outs):
    half = outs[0].shape[0] // 2
    kept, got = kept_ref[...].astype(jnp.float32), got_ref[...].astype(jnp.float32)
    for j, out in enumerate(outs):
        span = slice(j * half, (j + 1) * half)
        out[...] = jnp.concatenate([kept[span], got[span]], 0).astype(jnp.bfloat16)


def combine_kernel(hops, high_ref, low_ref, *refs):
    blocks, out_ref = [refs[hops.index(j)] for j in range(len(hops))], refs[-1]
    returned = jnp.concatenate([block[...].astype(jnp.float32) for block in blocks], 0).astype(
        jnp.bfloat16
    )
    mixture = jnp.dot(high_ref[...], returned, preferred_element_type=jnp.float32) + jnp.dot(
        low_ref[...], returned, preferred_element_type=jnp.float32
    )
    out_ref[...] = mixture.astype(jnp.bfloat16)


def finish_kernel(state_ref, *refs):
    parts, out_ref = refs[:-1], refs[-1]
    rows, steps, _ = out_ref.shape
    layer = (state_ref[...] + tree_sum(parts)).astype(jnp.bfloat16)
    for r in range(rows):
        out_ref[r] = layer[r * steps : (r + 1) * steps]


VMEM = pl.BlockSpec(memory_space=pltpu.VMEM)
HBM = pl.BlockSpec(memory_space=pltpu.HBM)
SMEM = pl.BlockSpec(memory_space=pltpu.SMEM)


def call(kernel, name, in_specs, out_shapes, operands, scratch=(), out_spec=None, vmem=4 * 1024 * 1024, cost=None):
    return pl.pallas_call(
        kernel,
        name=name,
        in_specs=in_specs,
        out_specs=[out_spec or VMEM] * len(out_shapes),
        out_shape=[jax.ShapeDtypeStruct(shape, dtype) for shape, dtype in out_shapes],
        scratch_shapes=list(scratch),
        compiler_params=pltpu.CompilerParams(vmem_limit_bytes=vmem),
        cost_estimate=cost,
    )(*operands)


def cost(micros):
    return pl.CostEstimate(flops=micros * 1_000_000_000, bytes_accessed=1 << 20, transcendentals=0)


def move(block, ctx_hop, exp_hop):
    n, exp_count = lax.axis_size("ctx"), lax.axis_size("exp")
    pairs = [
        (c * exp_count + e, (c ^ ctx_hop) * exp_count + (e ^ exp_hop))
        for c in range(n)
        for e in range(exp_count)
    ]
    return lax.ppermute(block, ("ctx", "exp"), pairs)


def per_device(
    queries,
    cache_keys,
    cache_values,
    new_keys,
    new_values,
    lengths,
    residual,
    out_weight,
    norm_gain,
    expert_ids,
    expert_weights,
    gate_proj,
    up_proj,
    down_proj,
):
    row_count, step_count, _ = queries.shape
    row_steps = row_count * step_count
    n = lax.axis_size("ctx")
    exp_count = lax.axis_size("exp")
    me = lax.axis_index("ctx").astype(jnp.int32).reshape(1)
    home = lax.axis_index("exp").astype(jnp.int32).reshape(1)
    experts_all = exp_count * EXP_DEV
    capacity = max(2, (row_steps * TOPK + experts_all - 1) // experts_all)
    chips = exp_count // 2
    hops = (chips - 1, *range(1, chips - 1), 0)
    span = HEADS // n * row_steps
    bf16, f32 = jnp.bfloat16, jnp.float32
    hidden = (row_steps, D)
    block = (2 * capacity, D)
    half = (chips * capacity, D)

    message = (span + STAT_ROWS, LANES)
    inputs = (lengths, queries, cache_keys, cache_values, new_keys, new_values)
    sent = call(
        functools.partial(attend_kernel, n),
        "attend",
        [SMEM] + [HBM] * 6,
        [(message, bf16)] * n,
        (me,) + tuple(pltpu.with_memory_space_constraint(x, pltpu.HBM) for x in inputs),
        [pltpu.VMEM((n,) + message, bf16)]
        + [pltpu.SMEM(lengths.shape, lengths.dtype)]
        + [pltpu.VMEM(x.shape, x.dtype) for x in inputs[1:]]
        + [pltpu.SemaphoreType.DMA((len(inputs),))],
        cost=cost(10),
    )
    got = [move(x, j, 1) for j, x in zip(reversed(range(n)), sent)]
    selector, weight_high, weight_low, residual_rows = call(
        functools.partial(route_kernel, n, exp_count, capacity),
        "route",
        [SMEM] * 2 + [VMEM] * 3,
        [((row_steps, exp_count * capacity), bf16)] * 3 + [(hidden, f32)],
        (
            me,
            home,
            expert_ids.reshape(row_steps, TOPK),
            expert_weights.reshape(row_steps, TOPK),
            residual,
        ),
    )
    (projected,) = call(
        functools.partial(project_kernel, n),
        "project",
        [VMEM] * (n + 1),
        [(hidden, bf16)],
        (out_weight, *got),
        vmem=8 * 1024 * 1024,
        cost=cost(10),
    )
    got = [move(projected, j, 1) for j in range(n)]
    state, *outgoing = call(
        functools.partial(dispatch_kernel, n, hops),
        "dispatch",
        [VMEM] * (n + 2),
        [(hidden, f32)] + [(block, bf16)] * chips,
        (residual_rows, selector, *got),
        cost=cost(10),
    )

    def spread(blocks):
        return [x if j == 0 else move(x, 0, 2 * j + 1) for j, x in zip(hops, blocks)]

    kept, sent = call(
        gather_kernel,
        "gather",
        [VMEM] * chips,
        [(half, bf16)] * 2,
        spread(outgoing),
    )
    kept, sent = call(
        expert_kernel,
        "experts",
        [VMEM] * 6,
        [(half, bf16)] * 2,
        (
            kept,
            move(sent, 0, 1),
            norm_gain.reshape(D // LANES, LANES),
            gate_proj,
            up_proj,
            down_proj,
        ),
        vmem=20 * 1024 * 1024,
        cost=cost(10),
    )
    results = call(
        scatter_kernel,
        "scatter",
        [VMEM] * 2,
        [(block, bf16)] * chips,
        (kept, move(sent, 0, 1)),
    )
    (mixture,) = call(
        functools.partial(combine_kernel, hops),
        "combine",
        [VMEM] * (chips + 2),
        [(hidden, bf16)],
        (weight_high, weight_low, *spread(results)),
    )
    got = [move(mixture, j, 0) if j else mixture for j in range(n)]
    (layer_rows,) = call(
        finish_kernel,
        "finish",
        [VMEM] * (n + 1),
        [((row_count, step_count, D), bf16)],
        (state, *got),
    )
    return layer_rows


def solution(mesh):
    return jax.shard_map(
        per_device,
        mesh=mesh,
        in_specs=(
            P("exp", None, None),
            P("exp", "ctx", None),
            P("exp", "ctx", None),
            P("exp", None, None),
            P("exp", None, None),
            P("exp"),
            P("exp", None, None),
            P("ctx", None),
            P(),
            P("exp", None, None),
            P("exp", None, None),
            P("exp", None, "ctx"),
            P("exp", None, "ctx"),
            P("exp", "ctx", None),
        ),
        out_specs=P("exp", None, None),
        check_vma=False,
    )
```

```python
import functools
import math

import jax
import jax.numpy as jnp
from jax import lax
from jax.experimental import pallas as pl
from jax.experimental.pallas import tpu as pltpu
from jax.sharding import PartitionSpec as P

D = 2048
HEADS = 32
KV_HEADS = 2
HEAD_DIM = 128
EXP_DEV = 4
TOPK = 8
LANES = 128
SUBLANES = 8
STAT_ROWS = 16


NORM_EPSILON = 1e-06
MASKED_SCORE = -1e30


def iota(shape, dim):
    return lax.broadcasted_iota(jnp.int32, shape, dim)


def to_column(row, count):
    return jnp.transpose(jnp.broadcast_to(row, (LANES, LANES)))[:count]


def split_three(values):
    high = values.astype(jnp.bfloat16).astype(jnp.float32)
    middle = (values - high).astype(jnp.bfloat16).astype(jnp.float32)
    return high, middle, values - high - middle


def interleave(parts):
    count = parts[0].shape[0] // SUBLANES
    return jnp.concatenate(
        [part[i * SUBLANES : (i + 1) * SUBLANES] for i in range(count) for part in parts], 0
    )


def attend_kernel(
    ctx_count, me_ref, len_hbm, q_hbm, k_hbm, v_hbm, nk_hbm, nv_hbm, *rest
):
    outs, blocks = rest[:ctx_count], rest[ctx_count]
    len_ref, q_ref, k_ref, v_ref, nk_ref, nv_ref, sems = rest[ctx_count + 1 :]
    early, late = [
        [pltpu.make_async_copy(source, target, sems.at[i]) for i, source, target in group]
        for group in (
            (
                (0, k_hbm, k_ref),
                (1, q_hbm, q_ref),
                (2, len_hbm, len_ref),
                (3, nk_hbm, nk_ref),
            ),
            ((4, v_hbm, v_ref), (5, nv_hbm, nv_ref)),
        )
    ]
    for copy in early + late:
        copy.start()
    rows, steps, _ = q_ref.shape
    window = k_ref.shape[1]
    row_steps = rows * steps
    group = HEADS // KV_HEADS
    block_heads = HEADS // ctx_count
    high = group * row_steps
    wide = rows * window
    pieces = row_steps // SUBLANES
    piece_rows = rows // pieces
    piece_high = group * SUBLANES
    piece_wide = piece_rows * window
    scale = 1.0 / math.sqrt(HEAD_DIM)
    me = me_ref[0]
    for copy in early + late:
        copy.wait()
    values = v_ref[...].reshape(wide, KV_HEADS * HEAD_DIM)
    fresh_values = jnp.concatenate([nv_ref[r] for r in range(rows)], 0)
    queries = [
        jnp.concatenate([q_ref[p * piece_rows + r] for r in range(piece_rows)], 0)
        for p in range(pieces)
    ]
    keys = k_ref[...].reshape(wide, KV_HEADS * HEAD_DIM)
    fresh_keys = jnp.concatenate([nk_ref[r] for r in range(rows)], 0)
    column = iota((1, piece_wide), 1)
    column_row = column // window
    position = me * window + column % window
    row_index = iota((piece_high, 1), 0) % SUBLANES
    fresh_column = iota((1, row_steps), 1)
    live, fresh_live = [], []
    for p in range(pieces):
        limit = jnp.zeros((1, piece_wide), jnp.int32)
        for r in range(piece_rows):
            limit = jnp.where(column_row == r, len_ref[p * piece_rows + r], limit)
        live.append(row_index // steps == jnp.where(position < limit, column_row, -1))
        fresh_row = jnp.where(me == 0, fresh_column // steps - p * piece_rows, -1)
        fresh_live.append(
            (row_index // steps == fresh_row) & (fresh_column % steps <= row_index % steps)
        )
    contract_last = (((1,), (1,)), ((), ()))
    kv_lanes = [slice(kv * HEAD_DIM, (kv + 1) * HEAD_DIM) for kv in range(KV_HEADS)]
    spans = [slice(p * piece_wide, (p + 1) * piece_wide) for p in range(pieces)]
    scores, fresh = {}, {}
    for kv, lanes in enumerate(kv_lanes):
        for p, span in enumerate(spans):
            heads = jnp.concatenate(
                [
                    queries[p][:, h * HEAD_DIM : (h + 1) * HEAD_DIM]
                    for h in range(kv * group, (kv + 1) * group)
                ],
                0,
            )
            scores[kv, p] = lax.dot_general(
                heads, keys[span, lanes], contract_last, preferred_element_type=jnp.float32
            )
            fresh[kv, p] = lax.dot_general(
                heads, fresh_keys[:, lanes], contract_last, preferred_element_type=jnp.float32
            )
    terms, last_terms, tops, totals = {}, {}, {}, {}
    for kv in range(KV_HEADS):
        for p in range(pieces):
            part = jnp.where(live[p], scores[kv, p] * scale, MASKED_SCORE)
            last = jnp.where(fresh_live[p], fresh[kv, p] * scale, MASKED_SCORE)
            top = jnp.maximum(
                jnp.max(part, 1, keepdims=True), jnp.max(last, 1, keepdims=True)
            )
            part, last = jnp.exp(part - top), jnp.exp(last - top)
            terms[kv, p], last_terms[kv, p] = part.astype(jnp.bfloat16), last.astype(jnp.bfloat16)
            tops[kv, p] = top
            totals[kv, p] = jnp.sum(part, 1, keepdims=True) + jnp.sum(last, 1, keepdims=True)
    weighted = {}
    for kv, lanes in enumerate(kv_lanes):
        for p, span in enumerate(spans):
            weighted[kv, p] = jnp.dot(
                terms[kv, p], values[span, lanes], preferred_element_type=jnp.float32
            ) + jnp.dot(
                last_terms[kv, p], fresh_values[:, lanes], preferred_element_type=jnp.float32
            )
    span = block_heads * row_steps
    row = iota((SUBLANES, LANES), 0)
    for kv in range(KV_HEADS):
        level = interleave(
            [
                jnp.broadcast_to(tops[kv, p] + jnp.log(totals[kv, p]), (piece_high, LANES))
                for p in range(pieces)
            ]
        )
        mean = interleave([weighted[kv, p] / totals[kv, p] for p in range(pieces)])
        mean = mean.astype(jnp.bfloat16)
        for part in range(high // LANES):
            level_row = jnp.transpose(level[part * LANES : (part + 1) * LANES])[:SUBLANES]
            high_part, middle_part, low_part = split_three(level_row)
            stats = jnp.where(row == 0, high_part, jnp.where(row == 1, middle_part, low_part))
            stats = jnp.concatenate([stats, stats], 0).astype(jnp.bfloat16)
            for sub in range(LANES // span):
                dest = (kv * high + part * LANES) // span + sub
                start = part * LANES + sub * span
                blocks[dest, :span, :] = mean[start : start + span]
                piece = stats
                if sub > 0:
                    piece = jnp.concatenate([stats[:, sub * span :], stats[:, : sub * span]], 1)
                blocks[dest, span:, :] = piece
    for k, out in zip(reversed(range(ctx_count)), outs):
        out[...] = blocks[me ^ k]


def project_kernel(ctx_count, w_ref, *rest):
    parts, out_ref = rest[:ctx_count], rest[ctx_count]
    block_heads = HEADS // ctx_count
    span = parts[0].shape[0] - STAT_ROWS
    row_steps = span // block_heads
    stats = [part[span:, :].astype(jnp.float32) for part in parts]
    levels = [stat[0:1] + stat[1:2] + stat[2:3] for stat in stats]
    top = functools.reduce(jnp.maximum, levels)
    factors = [jnp.exp(level - top) for level in levels]
    total = functools.reduce(jnp.add, factors)
    mixed = None
    for part, factor in zip(parts, factors):
        term = part[:span, :].astype(jnp.float32) * to_column(factor / total, span)
        mixed = term if mixed is None else mixed + term
    mixed = mixed.astype(jnp.bfloat16)
    attended = jnp.concatenate(
        [mixed[h * row_steps : (h + 1) * row_steps] for h in range(block_heads)], 1
    )
    out_ref[...] = jnp.dot(
        attended, w_ref[...], preferred_element_type=jnp.float32
    ).astype(jnp.bfloat16)


def route_kernel(
    ctx_count, exp_count, capacity, me_ref, home_ref, ids_ref, weights_ref, residual_ref,
    selector_ref, high_ref, low_ref, rows_ref
):
    rows, steps, _ = residual_ref.shape
    row_steps = rows * steps
    wide = exp_count * capacity
    me, home = me_ref[0], home_ref[0]
    column = iota((1, wide), 1)
    slot = column % capacity
    other = column // capacity % 2
    hop = column // (2 * capacity)
    crossed = jnp.where(hop == 0, 0, 1)
    device = home ^ (2 * hop) ^ crossed ^ other
    expert = device * EXP_DEV + me // (ctx_count // EXP_DEV)
    matched = jnp.zeros((row_steps, wide), jnp.float32)
    weight = jnp.zeros((row_steps, wide), jnp.float32)
    for k in range(TOPK):
        hit = ids_ref[:, k : k + 1] == expert
        matched = jnp.where(hit, 1.0, matched)
        weight = jnp.where(hit, weights_ref[:, k : k + 1], weight)
    earlier = iota((row_steps, row_steps), 1) < iota((row_steps, row_steps), 0)
    rank = jnp.dot(
        jnp.where(earlier, 1.0, 0.0).astype(jnp.bfloat16),
        matched.astype(jnp.bfloat16),
        preferred_element_type=jnp.float32,
    )
    chosen = (matched > 0.0) & (rank == slot.astype(jnp.float32))
    selector_ref[...] = jnp.where(chosen, 1.0, 0.0).astype(jnp.bfloat16)
    weight = jnp.where(chosen, weight, 0.0)
    weight_high = weight.astype(jnp.bfloat16)
    high_ref[...] = weight_high
    low_ref[...] = (weight - weight_high.astype(jnp.float32)).astype(jnp.bfloat16)
    rows_ref[...] = jnp.concatenate(
        [residual_ref[r].astype(jnp.float32) for r in range(rows)], 0
    )


def tree_sum(parts):
    values = [part[...].astype(jnp.float32) for part in parts]
    while len(values) > 1:
        values = [values[i] + values[i + 1] for i in range(0, len(values), 2)]
    return values[0]


def dispatch_kernel(ctx_count, hops, residual_ref, selector_ref, *rest):
    parts, state_ref, outs = rest[:ctx_count], rest[ctx_count], rest[ctx_count + 1 :]
    state = residual_ref[...] + tree_sum(parts)
    state_ref[...] = state
    picked = lax.dot_general(
        selector_ref[...],
        state.astype(jnp.bfloat16),
        (((0,), (0,)), ((), ())),
        preferred_element_type=jnp.float32,
    )
    block = outs[0].shape[0]
    for j, out in zip(hops, outs):
        out[...] = picked[j * block : (j + 1) * block].astype(jnp.bfloat16)


def gather_kernel(*refs):
    blocks, keep_ref, send_ref = refs[:-2], refs[-2], refs[-1]
    half = blocks[0].shape[0] // 2
    values = [block[...].astype(jnp.float32) for block in blocks]
    keep_ref[...] = jnp.concatenate([value[:half] for value in values], 0).astype(jnp.bfloat16)
    send_ref[...] = jnp.concatenate([value[half:] for value in values], 0).astype(jnp.bfloat16)


def expert_kernel(kept_ref, got_ref, gain_ref, gate_ref, up_ref, down_ref, keep_ref, send_ref):
    half = kept_ref.shape[0]
    state = jnp.concatenate(
        [kept_ref[...].astype(jnp.float32), got_ref[...].astype(jnp.float32)], 0
    )
    gains = gain_ref[...].astype(jnp.float32)
    gain = jnp.concatenate([gains[i : i + 1] for i in range(D // LANES)], 1)
    normed = (
        state
        * lax.rsqrt(jnp.mean(state * state, -1, keepdims=True) + NORM_EPSILON)
        * gain
    ).astype(jnp.bfloat16)
    spare = max(0, LANES - 2 * half)
    if spare:
        normed = jnp.concatenate([normed, jnp.zeros((spare, D), jnp.bfloat16)], 0)
    gate = jnp.dot(normed, gate_ref[0], preferred_element_type=jnp.float32)
    up = jnp.dot(normed, up_ref[0], preferred_element_type=jnp.float32)
    activation = (gate / (1.0 + jnp.exp(-gate)) * up).astype(jnp.bfloat16)
    result = jnp.dot(activation, down_ref[0], preferred_element_type=jnp.float32)
    keep_ref[...] = result[:half].astype(jnp.bfloat16)
    send_ref[...] = result[half : 2 * half].astype(jnp.bfloat16)


def scatter_kernel(kept_ref, got_ref, *outs):
    half = outs[0].shape[0] // 2
    kept, got = kept_ref[...].astype(jnp.float32), got_ref[...].astype(jnp.float32)
    for j, out in enumerate(outs):
        span = slice(j * half, (j + 1) * half)
        out[...] = jnp.concatenate([kept[span], got[span]], 0).astype(jnp.bfloat16)


def combine_kernel(hops, high_ref, low_ref, *refs):
    blocks, out_ref = [refs[hops.index(j)] for j in range(len(hops))], refs[-1]
    returned = jnp.concatenate([block[...].astype(jnp.float32) for block in blocks], 0).astype(
        jnp.bfloat16
    )
    mixture = jnp.dot(high_ref[...], returned, preferred_element_type=jnp.float32) + jnp.dot(
        low_ref[...], returned, preferred_element_type=jnp.float32
    )
    out_ref[...] = mixture.astype(jnp.bfloat16)


def finish_kernel(state_ref, *refs):
    parts, out_ref = refs[:-1], refs[-1]
    rows, steps, _ = out_ref.shape
    layer = (state_ref[...] + tree_sum(parts)).astype(jnp.bfloat16)
    for r in range(rows):
        out_ref[r] = layer[r * steps : (r + 1) * steps]


VMEM = pl.BlockSpec(memory_space=pltpu.VMEM)
HBM = pl.BlockSpec(memory_space=pltpu.HBM)
SMEM = pl.BlockSpec(memory_space=pltpu.SMEM)


def call(kernel, name, in_specs, out_shapes, operands, scratch=(), out_spec=None, vmem=4 * 1024 * 1024, cost=None):
    return pl.pallas_call(
        kernel,
        name=name,
        in_specs=in_specs,
        out_specs=[out_spec or VMEM] * len(out_shapes),
        out_shape=[jax.ShapeDtypeStruct(shape, dtype) for shape, dtype in out_shapes],
        scratch_shapes=list(scratch),
        compiler_params=pltpu.CompilerParams(vmem_limit_bytes=vmem),
        cost_estimate=cost,
    )(*operands)


def cost(micros):
    return pl.CostEstimate(flops=micros * 1_000_000_000, bytes_accessed=1 << 20, transcendentals=0)


def move(block, ctx_hop, exp_hop):
    n, exp_count = lax.axis_size("ctx"), lax.axis_size("exp")
    pairs = [
        (c * exp_count + e, (c ^ ctx_hop) * exp_count + (e ^ exp_hop))
        for c in range(n)
        for e in range(exp_count)
    ]
    return lax.ppermute(block, ("ctx", "exp"), pairs)


def per_device(
    queries,
    cache_keys,
    cache_values,
    new_keys,
    new_values,
    lengths,
    residual,
    out_weight,
    norm_gain,
    expert_ids,
    expert_weights,
    gate_proj,
    up_proj,
    down_proj,
):
    row_count, step_count, _ = queries.shape
    row_steps = row_count * step_count
    n = lax.axis_size("ctx")
    exp_count = lax.axis_size("exp")
    me = lax.axis_index("ctx").astype(jnp.int32).reshape(1)
    home = lax.axis_index("exp").astype(jnp.int32).reshape(1)
    experts_all = exp_count * EXP_DEV
    capacity = max(2, (row_steps * TOPK + experts_all - 1) // experts_all)
    chips = exp_count // 2
    hops = (chips - 1, *range(1, chips - 1), 0)
    span = HEADS // n * row_steps
    bf16, f32 = jnp.bfloat16, jnp.float32
    hidden = (row_steps, D)
    block = (2 * capacity, D)
    half = (chips * capacity, D)

    message = (span + STAT_ROWS, LANES)
    inputs = (lengths, queries, cache_keys, cache_values, new_keys, new_values)
    sent = call(
        functools.partial(attend_kernel, n),
        "attend",
        [SMEM] + [HBM] * 6,
        [(message, bf16)] * n,
        (me,) + tuple(pltpu.with_memory_space_constraint(x, pltpu.HBM) for x in inputs),
        [pltpu.VMEM((n,) + message, bf16)]
        + [pltpu.SMEM(lengths.shape, lengths.dtype)]
        + [pltpu.VMEM(x.shape, x.dtype) for x in inputs[1:]]
        + [pltpu.SemaphoreType.DMA((len(inputs),))],
        cost=cost(10),
    )
    got = [move(x, j, 1) for j, x in zip(reversed(range(n)), sent)]
    selector, weight_high, weight_low, residual_rows = call(
        functools.partial(route_kernel, n, exp_count, capacity),
        "route",
        [SMEM] * 2 + [VMEM] * 3,
        [((row_steps, exp_count * capacity), bf16)] * 3 + [(hidden, f32)],
        (
            me,
            home,
            expert_ids.reshape(row_steps, TOPK),
            expert_weights.reshape(row_steps, TOPK),
            residual,
        ),
    )
    (projected,) = call(
        functools.partial(project_kernel, n),
        "project",
        [VMEM] * (n + 1),
        [(hidden, bf16)],
        (out_weight, *got),
        vmem=8 * 1024 * 1024,
        cost=cost(10),
    )
    got = [move(projected, j, 1) for j in range(n)]
    state, *outgoing = call(
        functools.partial(dispatch_kernel, n, hops),
        "dispatch",
        [VMEM] * (n + 2),
        [(hidden, f32)] + [(block, bf16)] * chips,
        (residual_rows, selector, *got),
        cost=cost(10),
    )

    def spread(blocks):
        return [x if j == 0 else move(x, 0, 2 * j + 1) for j, x in zip(hops, blocks)]

    kept, sent = call(
        gather_kernel,
        "gather",
        [VMEM] * chips,
        [(half, bf16)] * 2,
        spread(outgoing),
    )
    kept, sent = call(
        expert_kernel,
        "experts",
        [VMEM] * 6,
        [(half, bf16)] * 2,
        (
            kept,
            move(sent, 0, 1),
            norm_gain.reshape(D // LANES, LANES),
            gate_proj,
            up_proj,
            down_proj,
        ),
        vmem=20 * 1024 * 1024,
        cost=cost(10),
    )
    results = call(
        scatter_kernel,
        "scatter",
        [VMEM] * 2,
        [(block, bf16)] * chips,
        (kept, move(sent, 0, 1)),
    )
    (mixture,) = call(
        functools.partial(combine_kernel, hops),
        "combine",
        [VMEM] * (chips + 2),
        [(hidden, bf16)],
        (weight_high, weight_low, *spread(results)),
    )
    got = [move(mixture, j, 0) if j else mixture for j in range(n)]
    (layer_rows,) = call(
        finish_kernel,
        "finish",
        [VMEM] * (n + 1),
        [((row_count, step_count, D), bf16)],
        (state, *got),
    )
    return layer_rows


def solution(mesh):
    return jax.shard_map(
        per_device,
        mesh=mesh,
        in_specs=(
            P("exp", None, None),
            P("exp", "ctx", None),
            P("exp", "ctx", None),
            P("exp", None, None),
            P("exp", None, None),
            P("exp"),
            P("exp", None, None),
            P("ctx", None),
            P(),
            P("exp", None, None),
            P("exp", None, None),
            P("exp", None, "ctx"),
            P("exp", None, "ctx"),
            P("exp", "ctx", None),
        ),
        out_specs=P("exp", None, None),
        check_vma=False,
    )
```

```python
import functools
import math

import jax
import jax.numpy as jnp
from jax import lax
from jax.experimental import pallas as pl
from jax.experimental.pallas import tpu as pltpu
from jax.sharding import PartitionSpec as P

D = 2048
HEADS = 32
KV_HEADS = 2
HEAD_DIM = 128
EXP_DEV = 4
TOPK = 8
LANES = 128
SUBLANES = 8
STAT_ROWS = 16
MEAN_SCALE = 2.0**26


NORM_EPSILON = 1e-06
MASKED_SCORE = -1e30


def iota(shape, dim):
    return lax.broadcasted_iota(jnp.int32, shape, dim)


def to_column(row, count):
    return jnp.transpose(jnp.broadcast_to(row, (LANES, LANES)))[:count]


def encode(values):
    square = values * values
    return jnp.where(values < 0.0, -square * square, square * square).astype(jnp.bfloat16)


def decode(codes):
    codes = codes.astype(jnp.float32)
    root = lax.rsqrt(lax.rsqrt(jnp.abs(codes)))
    return jnp.where(codes < 0.0, -root, root)


def encode_mean(values):
    return encode(values * jnp.abs(values) * MEAN_SCALE)


def decode_mean(codes):
    root = decode(codes)
    size = jnp.abs(root)
    return jnp.where(size > 0.0, root * lax.rsqrt(size) * MEAN_SCALE**-0.5, 0.0)


def split_two(values):
    high = values.astype(jnp.bfloat16)
    return high, (values - high.astype(jnp.float32)).astype(jnp.bfloat16)


def split_three(values):
    high = values.astype(jnp.bfloat16).astype(jnp.float32)
    middle = (values - high).astype(jnp.bfloat16).astype(jnp.float32)
    return high, middle, values - high - middle


def interleave(parts):
    count = parts[0].shape[0] // SUBLANES
    return jnp.concatenate(
        [part[i * SUBLANES : (i + 1) * SUBLANES] for i in range(count) for part in parts], 0
    )


def attend_kernel(
    ctx_count, me_ref, len_hbm, q_hbm, k_hbm, v_hbm, nk_hbm, nv_hbm, *rest
):
    outs, blocks = rest[:ctx_count], rest[ctx_count]
    len_ref, q_ref, k_ref, v_ref, nk_ref, nv_ref, sems = rest[ctx_count + 1 :]
    early, late = [
        [pltpu.make_async_copy(source, target, sems.at[i]) for i, source, target in group]
        for group in (
            (
                (0, k_hbm, k_ref),
                (1, q_hbm, q_ref),
                (2, len_hbm, len_ref),
                (3, nk_hbm, nk_ref),
            ),
            ((4, v_hbm, v_ref), (5, nv_hbm, nv_ref)),
        )
    ]
    for copy in early + late:
        copy.start()
    rows, steps, _ = q_ref.shape
    window = k_ref.shape[1]
    row_steps = rows * steps
    group = HEADS // KV_HEADS
    block_heads = HEADS // ctx_count
    high = group * row_steps
    wide = rows * window
    pieces = row_steps // SUBLANES
    piece_rows = rows // pieces
    piece_high = group * SUBLANES
    piece_wide = piece_rows * window
    scale = 1.0 / math.sqrt(HEAD_DIM)
    me = me_ref[0]
    for copy in early + late:
        copy.wait()
    values = v_ref[...].reshape(wide, KV_HEADS * HEAD_DIM)
    fresh_values = jnp.concatenate([nv_ref[r] for r in range(rows)], 0)
    queries = [
        jnp.concatenate([q_ref[p * piece_rows + r] for r in range(piece_rows)], 0)
        for p in range(pieces)
    ]
    keys = k_ref[...].reshape(wide, KV_HEADS * HEAD_DIM)
    fresh_keys = jnp.concatenate([nk_ref[r] for r in range(rows)], 0)
    column = iota((1, piece_wide), 1)
    column_row = column // window
    position = me * window + column % window
    row_index = iota((piece_high, 1), 0) % SUBLANES
    fresh_column = iota((1, row_steps), 1)
    live, fresh_live = [], []
    for p in range(pieces):
        limit = jnp.zeros((1, piece_wide), jnp.int32)
        for r in range(piece_rows):
            limit = jnp.where(column_row == r, len_ref[p * piece_rows + r], limit)
        live.append(row_index // steps == jnp.where(position < limit, column_row, -1))
        fresh_row = jnp.where(me == 0, fresh_column // steps - p * piece_rows, -1)
        fresh_live.append(
            (row_index // steps == fresh_row) & (fresh_column % steps <= row_index % steps)
        )
    contract_last = (((1,), (1,)), ((), ()))
    kv_lanes = [slice(kv * HEAD_DIM, (kv + 1) * HEAD_DIM) for kv in range(KV_HEADS)]
    spans = [slice(p * piece_wide, (p + 1) * piece_wide) for p in range(pieces)]
    scores, fresh = {}, {}
    for kv, lanes in enumerate(kv_lanes):
        for p, span in enumerate(spans):
            heads = jnp.concatenate(
                [
                    queries[p][:, h * HEAD_DIM : (h + 1) * HEAD_DIM]
                    for h in range(kv * group, (kv + 1) * group)
                ],
                0,
            )
            scores[kv, p] = lax.dot_general(
                heads, keys[span, lanes], contract_last, preferred_element_type=jnp.float32
            )
            fresh[kv, p] = lax.dot_general(
                heads, fresh_keys[:, lanes], contract_last, preferred_element_type=jnp.float32
            )
    terms, last_terms, tops, totals = {}, {}, {}, {}
    for kv in range(KV_HEADS):
        for p in range(pieces):
            part = jnp.where(live[p], scores[kv, p] * scale, MASKED_SCORE)
            last = jnp.where(fresh_live[p], fresh[kv, p] * scale, MASKED_SCORE)
            top = jnp.maximum(
                jnp.max(part, 1, keepdims=True), jnp.max(last, 1, keepdims=True)
            )
            part, last = jnp.exp(part - top), jnp.exp(last - top)
            terms[kv, p], last_terms[kv, p] = split_two(part), split_two(last)
            tops[kv, p] = top
            totals[kv, p] = jnp.sum(part, 1, keepdims=True) + jnp.sum(last, 1, keepdims=True)
    weighted = {}
    for kv, lanes in enumerate(kv_lanes):
        for p, span in enumerate(spans):
            weighted[kv, p] = sum(
                jnp.dot(term, values[span, lanes], preferred_element_type=jnp.float32)
                + jnp.dot(last, fresh_values[:, lanes], preferred_element_type=jnp.float32)
                for term, last in zip(terms[kv, p], last_terms[kv, p])
            )
    span = block_heads * row_steps
    row = iota((SUBLANES, LANES), 0)
    for kv in range(KV_HEADS):
        level = interleave(
            [
                jnp.broadcast_to(tops[kv, p] + jnp.log(totals[kv, p]), (piece_high, LANES))
                for p in range(pieces)
            ]
        )
        mean = interleave([weighted[kv, p] / totals[kv, p] for p in range(pieces)])
        mean = encode_mean(mean)
        for part in range(high // LANES):
            level_row = jnp.transpose(level[part * LANES : (part + 1) * LANES])[:SUBLANES]
            high_part, middle_part, low_part = split_three(level_row)
            stats = jnp.where(row == 0, high_part, jnp.where(row == 1, middle_part, low_part))
            stats = jnp.concatenate([stats, stats], 0).astype(jnp.bfloat16)
            for sub in range(LANES // span):
                dest = (kv * high + part * LANES) // span + sub
                start = part * LANES + sub * span
                blocks[dest, :span, :] = mean[start : start + span]
                piece = stats
                if sub > 0:
                    piece = jnp.concatenate([stats[:, sub * span :], stats[:, : sub * span]], 1)
                blocks[dest, span:, :] = piece
    for k, out in zip(reversed(range(ctx_count)), outs):
        out[...] = blocks[me ^ k]


def project_kernel(ctx_count, w_ref, *rest):
    parts, out_ref = rest[:ctx_count], rest[ctx_count]
    block_heads = HEADS // ctx_count
    span = parts[0].shape[0] - STAT_ROWS
    row_steps = span // block_heads
    stats = [part[span:, :].astype(jnp.float32) for part in parts]
    levels = [stat[0:1] + stat[1:2] + stat[2:3] for stat in stats]
    top = functools.reduce(jnp.maximum, levels)
    factors = [jnp.exp(level - top) for level in levels]
    total = functools.reduce(jnp.add, factors)
    mixed = None
    for part, factor in zip(parts, factors):
        term = decode_mean(part[:span, :]) * to_column(factor / total, span)
        mixed = term if mixed is None else mixed + term
    mixed = mixed.astype(jnp.bfloat16)
    attended = jnp.concatenate(
        [mixed[h * row_steps : (h + 1) * row_steps] for h in range(block_heads)], 1
    )
    out_ref[...] = encode(
        jnp.dot(attended, w_ref[...], preferred_element_type=jnp.float32)
    )


def route_kernel(
    ctx_count, exp_count, capacity, me_ref, home_ref, ids_ref, weights_ref, residual_ref,
    selector_ref, high_ref, low_ref, rows_ref
):
    rows, steps, _ = residual_ref.shape
    row_steps = rows * steps
    wide = exp_count * capacity
    me, home = me_ref[0], home_ref[0]
    column = iota((1, wide), 1)
    slot = column % capacity
    other = column // capacity % 2
    hop = column // (2 * capacity)
    crossed = jnp.where(hop == 0, 0, 1)
    device = home ^ (2 * hop) ^ crossed ^ other
    expert = device * EXP_DEV + me // (ctx_count // EXP_DEV)
    matched = jnp.zeros((row_steps, wide), jnp.float32)
    weight = jnp.zeros((row_steps, wide), jnp.float32)
    for k in range(TOPK):
        hit = ids_ref[:, k : k + 1] == expert
        matched = jnp.where(hit, 1.0, matched)
        weight = jnp.where(hit, weights_ref[:, k : k + 1], weight)
    earlier = iota((row_steps, row_steps), 1) < iota((row_steps, row_steps), 0)
    rank = jnp.dot(
        jnp.where(earlier, 1.0, 0.0).astype(jnp.bfloat16),
        matched.astype(jnp.bfloat16),
        preferred_element_type=jnp.float32,
    )
    chosen = (matched > 0.0) & (rank == slot.astype(jnp.float32))
    selector_ref[...] = jnp.where(chosen, 1.0, 0.0).astype(jnp.bfloat16)
    weight = jnp.where(chosen, weight, 0.0)
    weight_high = weight.astype(jnp.bfloat16)
    high_ref[...] = weight_high
    low_ref[...] = (weight - weight_high.astype(jnp.float32)).astype(jnp.bfloat16)
    rows_ref[...] = jnp.concatenate(
        [residual_ref[r].astype(jnp.float32) for r in range(rows)], 0
    )


def tree_sum(parts):
    values = list(parts)
    while len(values) > 1:
        values = [values[i] + values[i + 1] for i in range(0, len(values), 2)]
    return values[0]


def dispatch_kernel(ctx_count, hops, residual_ref, gain_ref, selector_ref, *rest):
    parts, state_ref, outs = rest[:ctx_count], rest[ctx_count], rest[ctx_count + 1 :]
    state = residual_ref[...] + tree_sum([decode(part[...]) for part in parts])
    state_ref[...] = state
    gains = gain_ref[...].astype(jnp.float32)
    gain = jnp.concatenate([gains[i : i + 1] for i in range(D // LANES)], 1)
    normed = (
        state
        * lax.rsqrt(jnp.mean(state * state, -1, keepdims=True) + NORM_EPSILON)
        * gain
    ).astype(jnp.bfloat16)
    picked = lax.dot_general(
        selector_ref[...],
        normed,
        (((0,), (0,)), ((), ())),
        preferred_element_type=jnp.float32,
    )
    block = outs[0].shape[0]
    for j, out in zip(hops, outs):
        out[...] = picked[j * block : (j + 1) * block].astype(jnp.bfloat16)


def gather_kernel(*refs):
    blocks, keep_ref, send_ref = refs[:-2], refs[-2], refs[-1]
    half = blocks[0].shape[0] // 2
    values = [block[...].astype(jnp.float32) for block in blocks]
    keep_ref[...] = jnp.concatenate([value[:half] for value in values], 0).astype(jnp.bfloat16)
    send_ref[...] = jnp.concatenate([value[half:] for value in values], 0).astype(jnp.bfloat16)


def expert_kernel(kept_ref, got_ref, gate_ref, up_ref, down_ref, keep_ref, send_ref):
    half = kept_ref.shape[0]
    normed = jnp.concatenate(
        [kept_ref[...].astype(jnp.float32), got_ref[...].astype(jnp.float32)], 0
    ).astype(jnp.bfloat16)
    spare = max(0, LANES - 2 * half)
    if spare:
        normed = jnp.concatenate([normed, jnp.zeros((spare, D), jnp.bfloat16)], 0)
    gate = jnp.dot(normed, gate_ref[0], preferred_element_type=jnp.float32)
    up = jnp.dot(normed, up_ref[0], preferred_element_type=jnp.float32)
    activation = (gate / (1.0 + jnp.exp(-gate)) * up).astype(jnp.bfloat16)
    result = jnp.dot(activation, down_ref[0], preferred_element_type=jnp.float32)
    keep_ref[...] = encode(result[:half])
    send_ref[...] = encode(result[half : 2 * half])


def scatter_kernel(kept_ref, got_ref, *outs):
    half = outs[0].shape[0] // 2
    kept, got = kept_ref[...].astype(jnp.float32), got_ref[...].astype(jnp.float32)
    for j, out in enumerate(outs):
        span = slice(j * half, (j + 1) * half)
        out[...] = jnp.concatenate([kept[span], got[span]], 0).astype(jnp.bfloat16)


def combine_kernel(hops, high_ref, low_ref, *refs):
    blocks, out_ref = [refs[hops.index(j)] for j in range(len(hops))], refs[-1]
    returned = decode(
        jnp.concatenate([block[...].astype(jnp.float32) for block in blocks], 0)
    )
    returned_high, returned_low = split_two(returned)
    weight_high, weight_low = high_ref[...], low_ref[...]
    mixture = (
        jnp.dot(weight_high, returned_high, preferred_element_type=jnp.float32)
        + jnp.dot(weight_high, returned_low, preferred_element_type=jnp.float32)
        + jnp.dot(weight_low, returned_high, preferred_element_type=jnp.float32)
    )
    out_ref[...] = encode(mixture)


def finish_kernel(state_ref, *refs):
    parts, out_ref = refs[:-1], refs[-1]
    rows, steps, _ = out_ref.shape
    layer = (
        state_ref[...] + tree_sum([decode(part[...]) for part in parts])
    ).astype(jnp.bfloat16)
    for r in range(rows):
        out_ref[r] = layer[r * steps : (r + 1) * steps]


VMEM = pl.BlockSpec(memory_space=pltpu.VMEM)
HBM = pl.BlockSpec(memory_space=pltpu.HBM)
SMEM = pl.BlockSpec(memory_space=pltpu.SMEM)


def call(kernel, name, in_specs, out_shapes, operands, scratch=(), out_spec=None, vmem=4 * 1024 * 1024, cost=None):
    return pl.pallas_call(
        kernel,
        name=name,
        in_specs=in_specs,
        out_specs=[out_spec or VMEM] * len(out_shapes),
        out_shape=[jax.ShapeDtypeStruct(shape, dtype) for shape, dtype in out_shapes],
        scratch_shapes=list(scratch),
        compiler_params=pltpu.CompilerParams(vmem_limit_bytes=vmem),
        cost_estimate=cost,
    )(*operands)


def cost(micros):
    return pl.CostEstimate(flops=micros * 1_000_000_000, bytes_accessed=1 << 20, transcendentals=0)


def move(block, ctx_hop, exp_hop):
    n, exp_count = lax.axis_size("ctx"), lax.axis_size("exp")
    pairs = [
        (c * exp_count + e, (c ^ ctx_hop) * exp_count + (e ^ exp_hop))
        for c in range(n)
        for e in range(exp_count)
    ]
    return lax.ppermute(block, ("ctx", "exp"), pairs)


def per_device(
    queries,
    cache_keys,
    cache_values,
    new_keys,
    new_values,
    lengths,
    residual,
    out_weight,
    norm_gain,
    expert_ids,
    expert_weights,
    gate_proj,
    up_proj,
    down_proj,
):
    row_count, step_count, _ = queries.shape
    row_steps = row_count * step_count
    n = lax.axis_size("ctx")
    exp_count = lax.axis_size("exp")
    me = lax.axis_index("ctx").astype(jnp.int32).reshape(1)
    home = lax.axis_index("exp").astype(jnp.int32).reshape(1)
    experts_all = exp_count * EXP_DEV
    capacity = max(2, (row_steps * TOPK + experts_all - 1) // experts_all)
    chips = exp_count // 2
    hops = (chips - 1, *range(1, chips - 1), 0)
    span = HEADS // n * row_steps
    bf16, f32 = jnp.bfloat16, jnp.float32
    hidden = (row_steps, D)
    block = (2 * capacity, D)
    half = (chips * capacity, D)

    message = (span + STAT_ROWS, LANES)
    inputs = (lengths, queries, cache_keys, cache_values, new_keys, new_values)
    sent = call(
        functools.partial(attend_kernel, n),
        "attend",
        [SMEM] + [HBM] * 6,
        [(message, bf16)] * n,
        (me,) + tuple(pltpu.with_memory_space_constraint(x, pltpu.HBM) for x in inputs),
        [pltpu.VMEM((n,) + message, bf16)]
        + [pltpu.SMEM(lengths.shape, lengths.dtype)]
        + [pltpu.VMEM(x.shape, x.dtype) for x in inputs[1:]]
        + [pltpu.SemaphoreType.DMA((len(inputs),))],
        cost=cost(10),
    )
    got = [move(x, j, 1) for j, x in zip(reversed(range(n)), sent)]
    selector, weight_high, weight_low, residual_rows = call(
        functools.partial(route_kernel, n, exp_count, capacity),
        "route",
        [SMEM] * 2 + [VMEM] * 3,
        [((row_steps, exp_count * capacity), bf16)] * 3 + [(hidden, f32)],
        (
            me,
            home,
            expert_ids.reshape(row_steps, TOPK),
            expert_weights.reshape(row_steps, TOPK),
            residual,
        ),
    )
    (projected,) = call(
        functools.partial(project_kernel, n),
        "project",
        [VMEM] * (n + 1),
        [(hidden, bf16)],
        (out_weight, *got),
        vmem=8 * 1024 * 1024,
        cost=cost(10),
    )
    got = [move(projected, j, 1) for j in range(n)]
    state, *outgoing = call(
        functools.partial(dispatch_kernel, n, hops),
        "dispatch",
        [VMEM] * (n + 3),
        [(hidden, f32)] + [(block, bf16)] * chips,
        (residual_rows, norm_gain.reshape(D // LANES, LANES), selector, *got),
        cost=cost(10),
    )

    def spread(blocks):
        return [x if j == 0 else move(x, 0, 2 * j + 1) for j, x in zip(hops, blocks)]

    kept, sent = call(
        gather_kernel,
        "gather",
        [VMEM] * chips,
        [(half, bf16)] * 2,
        spread(outgoing),
    )
    kept, sent = call(
        expert_kernel,
        "experts",
        [VMEM] * 5,
        [(half, bf16)] * 2,
        (
            kept,
            move(sent, 0, 1),
            gate_proj,
            up_proj,
            down_proj,
        ),
        vmem=20 * 1024 * 1024,
        cost=cost(10),
    )
    results = call(
        scatter_kernel,
        "scatter",
        [VMEM] * 2,
        [(block, bf16)] * chips,
        (kept, move(sent, 0, 1)),
    )
    (mixture,) = call(
        functools.partial(combine_kernel, hops),
        "combine",
        [VMEM] * (chips + 2),
        [(hidden, bf16)],
        (weight_high, weight_low, *spread(results)),
    )
    got = [move(mixture, j, 0) if j else mixture for j in range(n)]
    (layer_rows,) = call(
        finish_kernel,
        "finish",
        [VMEM] * (n + 1),
        [((row_count, step_count, D), bf16)],
        (state, *got),
    )
    return layer_rows


def solution(mesh):
    return jax.shard_map(
        per_device,
        mesh=mesh,
        in_specs=(
            P("exp", None, None),
            P("exp", "ctx", None),
            P("exp", "ctx", None),
            P("exp", None, None),
            P("exp", None, None),
            P("exp"),
            P("exp", None, None),
            P("ctx", None),
            P(),
            P("exp", None, None),
            P("exp", None, None),
            P("exp", None, "ctx"),
            P("exp", None, "ctx"),
            P("exp", "ctx", None),
        ),
        out_specs=P("exp", None, None),
        check_vma=False,
    )
```

```python
import functools
import math

import jax
import jax.numpy as jnp
from jax import lax
from jax.experimental import pallas as pl
from jax.experimental.pallas import tpu as pltpu
from jax.sharding import PartitionSpec as P

D = 2048
HEADS = 32
KV_HEADS = 2
HEAD_DIM = 128
EXP_DEV = 4
TOPK = 8
LANES = 128
SUBLANES = 8
STAT_ROWS = 16
MEAN_SCALE = 2.0**26
TERM_SCALE = 2.0**20


NORM_EPSILON = 1e-06
MASKED_SCORE = -1e30


def iota(shape, dim):
    return lax.broadcasted_iota(jnp.int32, shape, dim)


def to_column(row, count):
    return jnp.transpose(jnp.broadcast_to(row, (LANES, LANES)))[:count]


def encode(values):
    square = values * values
    return jnp.where(values < 0.0, -square * square, square * square).astype(jnp.bfloat16)


def decode(codes):
    codes = codes.astype(jnp.float32)
    root = lax.rsqrt(lax.rsqrt(jnp.abs(codes)))
    return jnp.where(codes < 0.0, -root, root)


def encode_mean(values):
    return encode(values * jnp.abs(values) * MEAN_SCALE)


def decode_mean(codes):
    root = decode(codes)
    size = jnp.abs(root)
    return jnp.where(size > 0.0, root * lax.rsqrt(size) * MEAN_SCALE**-0.5, 0.0)


def split_two(values):
    high = values.astype(jnp.bfloat16)
    return high, (values - high.astype(jnp.float32)).astype(jnp.bfloat16)


def split_three(values):
    high = values.astype(jnp.bfloat16).astype(jnp.float32)
    middle = (values - high).astype(jnp.bfloat16).astype(jnp.float32)
    return high, middle, values - high - middle


def interleave(parts):
    count = parts[0].shape[0] // SUBLANES
    return jnp.concatenate(
        [part[i * SUBLANES : (i + 1) * SUBLANES] for i in range(count) for part in parts], 0
    )


def attend_kernel(
    ctx_count, me_ref, len_hbm, q_hbm, k_hbm, v_hbm, nk_hbm, nv_hbm, *rest
):
    outs, blocks = rest[:ctx_count], rest[ctx_count]
    len_ref, q_ref, k_ref, v_ref, nk_ref, nv_ref, sems = rest[ctx_count + 1 :]
    early, late = [
        [pltpu.make_async_copy(source, target, sems.at[i]) for i, source, target in group]
        for group in (
            (
                (0, k_hbm, k_ref),
                (1, q_hbm, q_ref),
                (2, len_hbm, len_ref),
                (3, nk_hbm, nk_ref),
            ),
            ((4, v_hbm, v_ref), (5, nv_hbm, nv_ref)),
        )
    ]
    for copy in early + late:
        copy.start()
    rows, steps, _ = q_ref.shape
    window = k_ref.shape[1]
    row_steps = rows * steps
    group = HEADS // KV_HEADS
    block_heads = HEADS // ctx_count
    high = group * row_steps
    wide = rows * window
    pieces = row_steps // SUBLANES
    piece_rows = rows // pieces
    piece_high = group * SUBLANES
    piece_wide = piece_rows * window
    scale = 1.0 / math.sqrt(HEAD_DIM)
    me = me_ref[0]
    for copy in early + late:
        copy.wait()
    values = v_ref[...].reshape(wide, KV_HEADS * HEAD_DIM)
    fresh_values = jnp.concatenate([nv_ref[r] for r in range(rows)], 0)
    queries = [
        jnp.concatenate([q_ref[p * piece_rows + r] for r in range(piece_rows)], 0)
        for p in range(pieces)
    ]
    keys = k_ref[...].reshape(wide, KV_HEADS * HEAD_DIM)
    fresh_keys = jnp.concatenate([nk_ref[r] for r in range(rows)], 0)
    column = iota((1, piece_wide), 1)
    column_row = column // window
    position = me * window + column % window
    row_index = iota((piece_high, 1), 0) % SUBLANES
    fresh_column = iota((1, row_steps), 1)
    live, fresh_live = [], []
    for p in range(pieces):
        limit = jnp.zeros((1, piece_wide), jnp.int32)
        for r in range(piece_rows):
            limit = jnp.where(column_row == r, len_ref[p * piece_rows + r], limit)
        live.append(row_index // steps == jnp.where(position < limit, column_row, -1))
        fresh_row = jnp.where(me == 0, fresh_column // steps - p * piece_rows, -1)
        fresh_live.append(
            (row_index // steps == fresh_row) & (fresh_column % steps <= row_index % steps)
        )
    contract_last = (((1,), (1,)), ((), ()))
    kv_lanes = [slice(kv * HEAD_DIM, (kv + 1) * HEAD_DIM) for kv in range(KV_HEADS)]
    spans = [slice(p * piece_wide, (p + 1) * piece_wide) for p in range(pieces)]
    scores, fresh = {}, {}
    for kv, lanes in enumerate(kv_lanes):
        for p, span in enumerate(spans):
            heads = jnp.concatenate(
                [
                    queries[p][:, h * HEAD_DIM : (h + 1) * HEAD_DIM]
                    for h in range(kv * group, (kv + 1) * group)
                ],
                0,
            )
            scores[kv, p] = lax.dot_general(
                heads, keys[span, lanes], contract_last, preferred_element_type=jnp.float32
            )
            fresh[kv, p] = lax.dot_general(
                heads, fresh_keys[:, lanes], contract_last, preferred_element_type=jnp.float32
            )
    terms, last_terms, tops, totals = {}, {}, {}, {}
    for kv in range(KV_HEADS):
        for p in range(pieces):
            part = jnp.where(live[p], scores[kv, p] * scale, MASKED_SCORE)
            last = jnp.where(fresh_live[p], fresh[kv, p] * scale, MASKED_SCORE)
            top = jnp.maximum(
                jnp.max(part, 1, keepdims=True), jnp.max(last, 1, keepdims=True)
            )
            part, last = jnp.exp(part - top), jnp.exp(last - top)
            terms[kv, p], last_terms[kv, p] = split_two(part), split_two(last)
            tops[kv, p] = top
            totals[kv, p] = jnp.sum(part, 1, keepdims=True) + jnp.sum(last, 1, keepdims=True)
    weighted = {}
    for kv, lanes in enumerate(kv_lanes):
        for p, span in enumerate(spans):
            weighted[kv, p] = sum(
                jnp.dot(term, values[span, lanes], preferred_element_type=jnp.float32)
                + jnp.dot(last, fresh_values[:, lanes], preferred_element_type=jnp.float32)
                for term, last in zip(terms[kv, p], last_terms[kv, p])
            )
    span = block_heads * row_steps
    row = iota((SUBLANES, LANES), 0)
    for kv in range(KV_HEADS):
        level = interleave(
            [
                jnp.broadcast_to(tops[kv, p] + jnp.log(totals[kv, p]), (piece_high, LANES))
                for p in range(pieces)
            ]
        )
        mean = interleave([weighted[kv, p] / totals[kv, p] for p in range(pieces)])
        mean = encode_mean(mean)
        for part in range(high // LANES):
            level_row = jnp.transpose(level[part * LANES : (part + 1) * LANES])[:SUBLANES]
            high_part, middle_part, low_part = split_three(level_row)
            stats = jnp.where(row == 0, high_part, jnp.where(row == 1, middle_part, low_part))
            stats = jnp.concatenate([stats, stats], 0).astype(jnp.bfloat16)
            for sub in range(LANES // span):
                dest = (kv * high + part * LANES) // span + sub
                start = part * LANES + sub * span
                blocks[dest, :span, :] = mean[start : start + span]
                piece = stats
                if sub > 0:
                    piece = jnp.concatenate([stats[:, sub * span :], stats[:, : sub * span]], 1)
                blocks[dest, span:, :] = piece
    for k, out in zip(reversed(range(ctx_count)), outs):
        out[...] = blocks[me ^ k]


def project_kernel(ctx_count, w_ref, *rest):
    parts, out_ref = rest[:ctx_count], rest[ctx_count]
    block_heads = HEADS // ctx_count
    span = parts[0].shape[0] - STAT_ROWS
    row_steps = span // block_heads
    stats = [part[span:, :].astype(jnp.float32) for part in parts]
    levels = [stat[0:1] + stat[1:2] + stat[2:3] for stat in stats]
    top = functools.reduce(jnp.maximum, levels)
    factors = [jnp.exp(level - top) for level in levels]
    total = functools.reduce(jnp.add, factors)
    mixed = None
    for part, factor in zip(parts, factors):
        term = decode_mean(part[:span, :]) * to_column(factor / total, span)
        mixed = term if mixed is None else mixed + term
    mixed = (mixed * TERM_SCALE).astype(jnp.bfloat16)
    attended = jnp.concatenate(
        [mixed[h * row_steps : (h + 1) * row_steps] for h in range(block_heads)], 1
    )
    out_ref[...] = encode(
        jnp.dot(attended, w_ref[...], preferred_element_type=jnp.float32)
    )


def route_kernel(
    ctx_count, exp_count, capacity, me_ref, home_ref, ids_ref, weights_ref, residual_ref,
    selector_ref, high_ref, low_ref, rows_ref
):
    rows, steps, _ = residual_ref.shape
    row_steps = rows * steps
    wide = exp_count * capacity
    me, home = me_ref[0], home_ref[0]
    column = iota((1, wide), 1)
    slot = column % capacity
    other = column // capacity % 2
    hop = column // (2 * capacity)
    crossed = jnp.where(hop == 0, 0, 1)
    device = home ^ (2 * hop) ^ crossed ^ other
    expert = device * EXP_DEV + me // (ctx_count // EXP_DEV)
    matched = jnp.zeros((row_steps, wide), jnp.float32)
    weight = jnp.zeros((row_steps, wide), jnp.float32)
    for k in range(TOPK):
        hit = ids_ref[:, k : k + 1] == expert
        matched = jnp.where(hit, 1.0, matched)
        weight = jnp.where(hit, weights_ref[:, k : k + 1], weight)
    earlier = iota((row_steps, row_steps), 1) < iota((row_steps, row_steps), 0)
    rank = jnp.dot(
        jnp.where(earlier, 1.0, 0.0).astype(jnp.bfloat16),
        matched.astype(jnp.bfloat16),
        preferred_element_type=jnp.float32,
    )
    chosen = (matched > 0.0) & (rank == slot.astype(jnp.float32))
    selector_ref[...] = jnp.where(chosen, 1.0, 0.0).astype(jnp.bfloat16)
    weight = jnp.where(chosen, weight, 0.0)
    weight_high = weight.astype(jnp.bfloat16)
    high_ref[...] = weight_high
    low_ref[...] = (weight - weight_high.astype(jnp.float32)).astype(jnp.bfloat16)
    rows_ref[...] = jnp.concatenate(
        [residual_ref[r].astype(jnp.float32) for r in range(rows)], 0
    )


def tree_sum(parts):
    values = list(parts)
    while len(values) > 1:
        values = [values[i] + values[i + 1] for i in range(0, len(values), 2)]
    return values[0]


def dispatch_kernel(ctx_count, hops, residual_ref, gain_ref, selector_ref, *rest):
    parts, state_ref, outs = rest[:ctx_count], rest[ctx_count], rest[ctx_count + 1 :]
    terms = tree_sum([decode(part[...]) for part in parts])
    state = residual_ref[...] + terms * (1.0 / TERM_SCALE)
    state_ref[...] = state
    gains = gain_ref[...].astype(jnp.float32)
    gain = jnp.concatenate([gains[i : i + 1] for i in range(D // LANES)], 1)
    normed = (
        state
        * lax.rsqrt(jnp.mean(state * state, -1, keepdims=True) + NORM_EPSILON)
        * gain
    ).astype(jnp.bfloat16)
    picked = lax.dot_general(
        selector_ref[...],
        normed,
        (((0,), (0,)), ((), ())),
        preferred_element_type=jnp.float32,
    )
    block = outs[0].shape[0]
    for j, out in zip(hops, outs):
        out[...] = picked[j * block : (j + 1) * block].astype(jnp.bfloat16)


def gather_kernel(*refs):
    blocks, keep_ref, send_ref = refs[:-2], refs[-2], refs[-1]
    half = blocks[0].shape[0] // 2
    values = [block[...].astype(jnp.float32) for block in blocks]
    keep_ref[...] = jnp.concatenate([value[:half] for value in values], 0).astype(jnp.bfloat16)
    send_ref[...] = jnp.concatenate([value[half:] for value in values], 0).astype(jnp.bfloat16)


def expert_kernel(kept_ref, got_ref, gate_ref, up_ref, down_ref, keep_ref, send_ref):
    half = kept_ref.shape[0]
    normed = jnp.concatenate(
        [kept_ref[...].astype(jnp.float32), got_ref[...].astype(jnp.float32)], 0
    ).astype(jnp.bfloat16)
    spare = max(0, LANES - 2 * half)
    if spare:
        normed = jnp.concatenate([normed, jnp.zeros((spare, D), jnp.bfloat16)], 0)
    gate = jnp.dot(normed, gate_ref[0], preferred_element_type=jnp.float32)
    up = jnp.dot(normed, up_ref[0], preferred_element_type=jnp.float32)
    activation = (gate / (1.0 + jnp.exp(-gate)) * up).astype(jnp.bfloat16)
    result = jnp.dot(activation, down_ref[0], preferred_element_type=jnp.float32)
    keep_ref[...] = encode(result[:half])
    send_ref[...] = encode(result[half : 2 * half])


def scatter_kernel(kept_ref, got_ref, *outs):
    half = outs[0].shape[0] // 2
    kept, got = kept_ref[...].astype(jnp.float32), got_ref[...].astype(jnp.float32)
    for j, out in enumerate(outs):
        span = slice(j * half, (j + 1) * half)
        out[...] = jnp.concatenate([kept[span], got[span]], 0).astype(jnp.bfloat16)


def combine_kernel(hops, high_ref, low_ref, *refs):
    blocks, out_ref = [refs[hops.index(j)] for j in range(len(hops))], refs[-1]
    returned = decode(
        jnp.concatenate([block[...].astype(jnp.float32) for block in blocks], 0)
    )
    returned_high, returned_low = split_two(returned)
    weight_high, weight_low = high_ref[...], low_ref[...]
    mixture = (
        jnp.dot(weight_high, returned_high, preferred_element_type=jnp.float32)
        + jnp.dot(weight_high, returned_low, preferred_element_type=jnp.float32)
        + jnp.dot(weight_low, returned_high, preferred_element_type=jnp.float32)
    )
    out_ref[...] = encode(mixture)


def finish_kernel(state_ref, *refs):
    parts, out_ref = refs[:-1], refs[-1]
    rows, steps, _ = out_ref.shape
    layer = (
        state_ref[...] + tree_sum([decode(part[...]) for part in parts])
    ).astype(jnp.bfloat16)
    for r in range(rows):
        out_ref[r] = layer[r * steps : (r + 1) * steps]


VMEM = pl.BlockSpec(memory_space=pltpu.VMEM)
HBM = pl.BlockSpec(memory_space=pltpu.HBM)
SMEM = pl.BlockSpec(memory_space=pltpu.SMEM)


def call(kernel, name, in_specs, out_shapes, operands, scratch=(), out_spec=None, vmem=4 * 1024 * 1024, cost=None):
    return pl.pallas_call(
        kernel,
        name=name,
        in_specs=in_specs,
        out_specs=[out_spec or VMEM] * len(out_shapes),
        out_shape=[jax.ShapeDtypeStruct(shape, dtype) for shape, dtype in out_shapes],
        scratch_shapes=list(scratch),
        compiler_params=pltpu.CompilerParams(vmem_limit_bytes=vmem),
        cost_estimate=cost,
    )(*operands)


def cost(micros):
    return pl.CostEstimate(flops=micros * 1_000_000_000, bytes_accessed=1 << 20, transcendentals=0)


def move(block, ctx_hop, exp_hop):
    n, exp_count = lax.axis_size("ctx"), lax.axis_size("exp")
    pairs = [
        (c * exp_count + e, (c ^ ctx_hop) * exp_count + (e ^ exp_hop))
        for c in range(n)
        for e in range(exp_count)
    ]
    return lax.ppermute(block, ("ctx", "exp"), pairs)


def per_device(
    queries,
    cache_keys,
    cache_values,
    new_keys,
    new_values,
    lengths,
    residual,
    out_weight,
    norm_gain,
    expert_ids,
    expert_weights,
    gate_proj,
    up_proj,
    down_proj,
):
    row_count, step_count, _ = queries.shape
    row_steps = row_count * step_count
    n = lax.axis_size("ctx")
    exp_count = lax.axis_size("exp")
    me = lax.axis_index("ctx").astype(jnp.int32).reshape(1)
    home = lax.axis_index("exp").astype(jnp.int32).reshape(1)
    experts_all = exp_count * EXP_DEV
    capacity = max(2, (row_steps * TOPK + experts_all - 1) // experts_all)
    chips = exp_count // 2
    hops = (chips - 1, *range(1, chips - 1), 0)
    span = HEADS // n * row_steps
    bf16, f32 = jnp.bfloat16, jnp.float32
    hidden = (row_steps, D)
    block = (2 * capacity, D)
    half = (chips * capacity, D)

    message = (span + STAT_ROWS, LANES)
    inputs = (lengths, queries, cache_keys, cache_values, new_keys, new_values)
    sent = call(
        functools.partial(attend_kernel, n),
        "attend",
        [SMEM] + [HBM] * 6,
        [(message, bf16)] * n,
        (me,) + tuple(pltpu.with_memory_space_constraint(x, pltpu.HBM) for x in inputs),
        [pltpu.VMEM((n,) + message, bf16)]
        + [pltpu.SMEM(lengths.shape, lengths.dtype)]
        + [pltpu.VMEM(x.shape, x.dtype) for x in inputs[1:]]
        + [pltpu.SemaphoreType.DMA((len(inputs),))],
        cost=cost(10),
    )
    got = [move(x, j, 1) for j, x in zip(reversed(range(n)), sent)]
    selector, weight_high, weight_low, residual_rows = call(
        functools.partial(route_kernel, n, exp_count, capacity),
        "route",
        [SMEM] * 2 + [VMEM] * 3,
        [((row_steps, exp_count * capacity), bf16)] * 3 + [(hidden, f32)],
        (
            me,
            home,
            expert_ids.reshape(row_steps, TOPK),
            expert_weights.reshape(row_steps, TOPK),
            residual,
        ),
    )
    (projected,) = call(
        functools.partial(project_kernel, n),
        "project",
        [VMEM] * (n + 1),
        [(hidden, bf16)],
        (out_weight, *got),
        vmem=8 * 1024 * 1024,
        cost=cost(10),
    )
    got = [move(projected, j, 1) for j in range(n)]
    state, *outgoing = call(
        functools.partial(dispatch_kernel, n, hops),
        "dispatch",
        [VMEM] * (n + 3),
        [(hidden, f32)] + [(block, bf16)] * chips,
        (residual_rows, norm_gain.reshape(D // LANES, LANES), selector, *got),
        cost=cost(10),
    )

    def spread(blocks):
        return [x if j == 0 else move(x, 0, 2 * j + 1) for j, x in zip(hops, blocks)]

    kept, sent = call(
        gather_kernel,
        "gather",
        [VMEM] * chips,
        [(half, bf16)] * 2,
        spread(outgoing),
    )
    kept, sent = call(
        expert_kernel,
        "experts",
        [VMEM] * 5,
        [(half, bf16)] * 2,
        (
            kept,
            move(sent, 0, 1),
            gate_proj,
            up_proj,
            down_proj,
        ),
        vmem=20 * 1024 * 1024,
        cost=cost(10),
    )
    results = call(
        scatter_kernel,
        "scatter",
        [VMEM] * 2,
        [(block, bf16)] * chips,
        (kept, move(sent, 0, 1)),
    )
    (mixture,) = call(
        functools.partial(combine_kernel, hops),
        "combine",
        [VMEM] * (chips + 2),
        [(hidden, bf16)],
        (weight_high, weight_low, *spread(results)),
    )
    got = [move(mixture, j, 0) if j else mixture for j in range(n)]
    (layer_rows,) = call(
        finish_kernel,
        "finish",
        [VMEM] * (n + 1),
        [((row_count, step_count, D), bf16)],
        (state, *got),
    )
    return layer_rows


def solution(mesh):
    return jax.shard_map(
        per_device,
        mesh=mesh,
        in_specs=(
            P("exp", None, None),
            P("exp", "ctx", None),
            P("exp", "ctx", None),
            P("exp", None, None),
            P("exp", None, None),
            P("exp"),
            P("exp", None, None),
            P("ctx", None),
            P(),
            P("exp", None, None),
            P("exp", None, None),
            P("exp", None, "ctx"),
            P("exp", None, "ctx"),
            P("exp", "ctx", None),
        ),
        out_specs=P("exp", None, None),
        check_vma=False,
    )
```

```python
import functools
import math

import jax
import jax.numpy as jnp
from jax import lax
from jax.experimental import pallas as pl
from jax.experimental.pallas import tpu as pltpu
from jax.sharding import PartitionSpec as P

D = 2048
HEADS = 32
KV_HEADS = 2
HEAD_DIM = 128
EXP_DEV = 4
TOPK = 8
LANES = 128
SUBLANES = 8
STAT_ROWS = 16
MEAN_SCALE = 2.0**26
TERM_SCALE = 2.0**20


NORM_EPSILON = 1e-06
MASKED_SCORE = -1e30


def iota(shape, dim):
    return lax.broadcasted_iota(jnp.int32, shape, dim)


def to_column(row, count):
    return jnp.transpose(jnp.broadcast_to(row, (LANES, LANES)))[:count]


def encode(values):
    square = values * values
    return jnp.where(values < 0.0, -square * square, square * square).astype(jnp.bfloat16)


def decode(codes):
    codes = codes.astype(jnp.float32)
    root = lax.rsqrt(lax.rsqrt(jnp.abs(codes)))
    return jnp.where(codes < 0.0, -root, root)


def encode_square(values):
    return (values * jnp.abs(values)).astype(jnp.bfloat16)


def decode_square(codes):
    codes = codes.astype(jnp.float32)
    return codes * lax.rsqrt(jnp.maximum(jnp.abs(codes), 1e-37))


def encode_mean(values):
    return encode(values * jnp.abs(values) * MEAN_SCALE)


def decode_mean(codes):
    root = decode(codes)
    size = jnp.abs(root)
    return jnp.where(size > 0.0, root * lax.rsqrt(size) * MEAN_SCALE**-0.5, 0.0)


def split_two(values):
    high = values.astype(jnp.bfloat16)
    return high, (values - high.astype(jnp.float32)).astype(jnp.bfloat16)


def split_three(values):
    high = values.astype(jnp.bfloat16).astype(jnp.float32)
    middle = (values - high).astype(jnp.bfloat16).astype(jnp.float32)
    return high, middle, values - high - middle


def interleave(parts):
    count = parts[0].shape[0] // SUBLANES
    return jnp.concatenate(
        [part[i * SUBLANES : (i + 1) * SUBLANES] for i in range(count) for part in parts], 0
    )


def attend_kernel(
    ctx_count, me_ref, len_hbm, q_hbm, k_hbm, v_hbm, nk_hbm, nv_hbm, *rest
):
    outs, blocks = rest[:ctx_count], rest[ctx_count]
    len_ref, q_ref, k_ref, v_ref, nk_ref, nv_ref, sems = rest[ctx_count + 1 :]
    early, late = [
        [pltpu.make_async_copy(source, target, sems.at[i]) for i, source, target in group]
        for group in (
            (
                (0, k_hbm, k_ref),
                (1, q_hbm, q_ref),
                (2, len_hbm, len_ref),
                (3, nk_hbm, nk_ref),
            ),
            ((4, v_hbm, v_ref), (5, nv_hbm, nv_ref)),
        )
    ]
    for copy in early + late:
        copy.start()
    rows, steps, _ = q_ref.shape
    window = k_ref.shape[1]
    row_steps = rows * steps
    group = HEADS // KV_HEADS
    block_heads = HEADS // ctx_count
    high = group * row_steps
    wide = rows * window
    pieces = row_steps // SUBLANES
    piece_rows = rows // pieces
    piece_high = group * SUBLANES
    piece_wide = piece_rows * window
    scale = 1.0 / math.sqrt(HEAD_DIM)
    me = me_ref[0]
    for copy in early + late:
        copy.wait()
    values = v_ref[...].reshape(wide, KV_HEADS * HEAD_DIM)
    fresh_values = jnp.concatenate([nv_ref[r] for r in range(rows)], 0)
    queries = [
        jnp.concatenate([q_ref[p * piece_rows + r] for r in range(piece_rows)], 0)
        for p in range(pieces)
    ]
    keys = k_ref[...].reshape(wide, KV_HEADS * HEAD_DIM)
    fresh_keys = jnp.concatenate([nk_ref[r] for r in range(rows)], 0)
    column = iota((1, piece_wide), 1)
    column_row = column // window
    position = me * window + column % window
    row_index = iota((piece_high, 1), 0) % SUBLANES
    fresh_column = iota((1, row_steps), 1)
    live, fresh_live = [], []
    for p in range(pieces):
        limit = jnp.zeros((1, piece_wide), jnp.int32)
        for r in range(piece_rows):
            limit = jnp.where(column_row == r, len_ref[p * piece_rows + r], limit)
        live.append(row_index // steps == jnp.where(position < limit, column_row, -1))
        fresh_row = jnp.where(me == 0, fresh_column // steps - p * piece_rows, -1)
        fresh_live.append(
            (row_index // steps == fresh_row) & (fresh_column % steps <= row_index % steps)
        )
    contract_last = (((1,), (1,)), ((), ()))
    kv_lanes = [slice(kv * HEAD_DIM, (kv + 1) * HEAD_DIM) for kv in range(KV_HEADS)]
    spans = [slice(p * piece_wide, (p + 1) * piece_wide) for p in range(pieces)]
    scores, fresh = {}, {}
    for kv, lanes in enumerate(kv_lanes):
        for p, span in enumerate(spans):
            heads = jnp.concatenate(
                [
                    queries[p][:, h * HEAD_DIM : (h + 1) * HEAD_DIM]
                    for h in range(kv * group, (kv + 1) * group)
                ],
                0,
            )
            scores[kv, p] = lax.dot_general(
                heads, keys[span, lanes], contract_last, preferred_element_type=jnp.float32
            )
            fresh[kv, p] = lax.dot_general(
                heads, fresh_keys[:, lanes], contract_last, preferred_element_type=jnp.float32
            )
    terms, last_terms, tops, totals = {}, {}, {}, {}
    for kv in range(KV_HEADS):
        for p in range(pieces):
            part = jnp.where(live[p], scores[kv, p] * scale, MASKED_SCORE)
            last = jnp.where(fresh_live[p], fresh[kv, p] * scale, MASKED_SCORE)
            top = jnp.maximum(
                jnp.max(part, 1, keepdims=True), jnp.max(last, 1, keepdims=True)
            )
            part, last = jnp.exp(part - top), jnp.exp(last - top)
            terms[kv, p], last_terms[kv, p] = split_two(part), split_two(last)
            tops[kv, p] = top
            totals[kv, p] = jnp.sum(part, 1, keepdims=True) + jnp.sum(last, 1, keepdims=True)
    weighted = {}
    for kv, lanes in enumerate(kv_lanes):
        for p, span in enumerate(spans):
            weighted[kv, p] = sum(
                jnp.dot(term, values[span, lanes], preferred_element_type=jnp.float32)
                + jnp.dot(last, fresh_values[:, lanes], preferred_element_type=jnp.float32)
                for term, last in zip(terms[kv, p], last_terms[kv, p])
            )
    span = block_heads * row_steps
    row = iota((SUBLANES, LANES), 0)
    for kv in range(KV_HEADS):
        level = interleave(
            [
                jnp.broadcast_to(tops[kv, p] + jnp.log(totals[kv, p]), (piece_high, LANES))
                for p in range(pieces)
            ]
        )
        mean = interleave([weighted[kv, p] / totals[kv, p] for p in range(pieces)])
        mean = encode_mean(mean)
        for part in range(high // LANES):
            level_row = jnp.transpose(level[part * LANES : (part + 1) * LANES])[:SUBLANES]
            high_part, middle_part, low_part = split_three(level_row)
            stats = jnp.where(row == 0, high_part, jnp.where(row == 1, middle_part, low_part))
            stats = jnp.concatenate([stats, stats], 0).astype(jnp.bfloat16)
            for sub in range(LANES // span):
                dest = (kv * high + part * LANES) // span + sub
                start = part * LANES + sub * span
                blocks[dest, :span, :] = mean[start : start + span]
                piece = stats
                if sub > 0:
                    piece = jnp.concatenate([stats[:, sub * span :], stats[:, : sub * span]], 1)
                blocks[dest, span:, :] = piece
    for k, out in zip(reversed(range(ctx_count)), outs):
        out[...] = blocks[me ^ k]


def project_kernel(ctx_count, w_ref, *rest):
    parts, out_ref = rest[:ctx_count], rest[ctx_count]
    block_heads = HEADS // ctx_count
    span = parts[0].shape[0] - STAT_ROWS
    row_steps = span // block_heads
    stats = [part[span:, :].astype(jnp.float32) for part in parts]
    levels = [stat[0:1] + stat[1:2] + stat[2:3] for stat in stats]
    top = functools.reduce(jnp.maximum, levels)
    factors = [jnp.exp(level - top) for level in levels]
    total = functools.reduce(jnp.add, factors)
    mixed = None
    for part, factor in zip(parts, factors):
        term = decode_mean(part[:span, :]) * to_column(factor / total, span)
        mixed = term if mixed is None else mixed + term
    mixed = (mixed * TERM_SCALE).astype(jnp.bfloat16)
    attended = jnp.concatenate(
        [mixed[h * row_steps : (h + 1) * row_steps] for h in range(block_heads)], 1
    )
    out_ref[...] = encode(
        jnp.dot(attended, w_ref[...], preferred_element_type=jnp.float32)
    )


def route_kernel(
    ctx_count, exp_count, capacity, me_ref, home_ref, ids_ref, weights_ref, residual_ref,
    selector_ref, high_ref, low_ref, rows_ref
):
    rows, steps, _ = residual_ref.shape
    row_steps = rows * steps
    wide = exp_count * capacity
    me, home = me_ref[0], home_ref[0]
    column = iota((1, wide), 1)
    slot = column % capacity
    other = column // capacity % 2
    hop = column // (2 * capacity)
    crossed = jnp.where(hop == 0, 0, 1)
    device = home ^ (2 * hop) ^ crossed ^ other
    expert = device * EXP_DEV + me // (ctx_count // EXP_DEV)
    matched = jnp.zeros((row_steps, wide), jnp.float32)
    weight = jnp.zeros((row_steps, wide), jnp.float32)
    for k in range(TOPK):
        hit = ids_ref[:, k : k + 1] == expert
        matched = jnp.where(hit, 1.0, matched)
        weight = jnp.where(hit, weights_ref[:, k : k + 1], weight)
    earlier = iota((row_steps, row_steps), 1) < iota((row_steps, row_steps), 0)
    rank = jnp.dot(
        jnp.where(earlier, 1.0, 0.0).astype(jnp.bfloat16),
        matched.astype(jnp.bfloat16),
        preferred_element_type=jnp.float32,
    )
    chosen = (matched > 0.0) & (rank == slot.astype(jnp.float32))
    selector_ref[...] = jnp.where(chosen, 1.0, 0.0).astype(jnp.bfloat16)
    weight = jnp.where(chosen, weight, 0.0)
    weight_high = weight.astype(jnp.bfloat16)
    high_ref[...] = weight_high
    low_ref[...] = (weight - weight_high.astype(jnp.float32)).astype(jnp.bfloat16)
    rows_ref[...] = jnp.concatenate(
        [residual_ref[r].astype(jnp.float32) for r in range(rows)], 0
    )


def tree_sum(parts):
    values = list(parts)
    while len(values) > 1:
        values = [values[i] + values[i + 1] for i in range(0, len(values), 2)]
    return values[0]


def dispatch_kernel(ctx_count, hops, residual_ref, gain_ref, selector_ref, *rest):
    parts, state_ref, outs = rest[:ctx_count], rest[ctx_count], rest[ctx_count + 1 :]
    terms = tree_sum([decode(part[...]) for part in parts])
    state = residual_ref[...] + terms * (1.0 / TERM_SCALE)
    state_ref[...] = state
    gains = gain_ref[...].astype(jnp.float32)
    gain = jnp.concatenate([gains[i : i + 1] for i in range(D // LANES)], 1)
    normed = (
        state
        * lax.rsqrt(jnp.mean(state * state, -1, keepdims=True) + NORM_EPSILON)
        * gain
    ).astype(jnp.bfloat16)
    picked = lax.dot_general(
        selector_ref[...],
        normed,
        (((0,), (0,)), ((), ())),
        preferred_element_type=jnp.float32,
    )
    block = outs[0].shape[0]
    for j, out in zip(hops, outs):
        out[...] = picked[j * block : (j + 1) * block].astype(jnp.bfloat16)


def gather_kernel(*refs):
    blocks, keep_ref, send_ref = refs[:-2], refs[-2], refs[-1]
    half = blocks[0].shape[0] // 2
    values = [block[...].astype(jnp.float32) for block in blocks]
    keep_ref[...] = jnp.concatenate([value[:half] for value in values], 0).astype(jnp.bfloat16)
    send_ref[...] = jnp.concatenate([value[half:] for value in values], 0).astype(jnp.bfloat16)


def expert_kernel(kept_ref, got_ref, gate_ref, up_ref, down_ref, keep_ref, send_ref):
    half = kept_ref.shape[0]
    normed = jnp.concatenate(
        [kept_ref[...].astype(jnp.float32), got_ref[...].astype(jnp.float32)], 0
    ).astype(jnp.bfloat16)
    spare = max(0, LANES - 2 * half)
    if spare:
        normed = jnp.concatenate([normed, jnp.zeros((spare, D), jnp.bfloat16)], 0)
    gate = jnp.dot(normed, gate_ref[0], preferred_element_type=jnp.float32)
    up = jnp.dot(normed, up_ref[0], preferred_element_type=jnp.float32)
    activation = (gate / (1.0 + jnp.exp(-gate)) * up).astype(jnp.bfloat16)
    result = jnp.dot(activation, down_ref[0], preferred_element_type=jnp.float32)
    keep_ref[...] = encode_square(result[:half])
    send_ref[...] = encode_square(result[half : 2 * half])


def scatter_kernel(kept_ref, got_ref, *outs):
    half = outs[0].shape[0] // 2
    kept, got = kept_ref[...].astype(jnp.float32), got_ref[...].astype(jnp.float32)
    for j, out in enumerate(outs):
        span = slice(j * half, (j + 1) * half)
        out[...] = jnp.concatenate([kept[span], got[span]], 0).astype(jnp.bfloat16)


def combine_kernel(hops, high_ref, low_ref, *refs):
    blocks, out_ref = [refs[hops.index(j)] for j in range(len(hops))], refs[-1]
    returned = decode_square(
        jnp.concatenate([block[...].astype(jnp.float32) for block in blocks], 0)
    )
    returned_high, returned_low = split_two(returned)
    weight_high, weight_low = high_ref[...], low_ref[...]
    mixture = (
        jnp.dot(weight_high, returned_high, preferred_element_type=jnp.float32)
        + jnp.dot(weight_high, returned_low, preferred_element_type=jnp.float32)
        + jnp.dot(weight_low, returned_high, preferred_element_type=jnp.float32)
    )
    out_ref[...] = encode_square(mixture)


def finish_kernel(state_ref, *refs):
    parts, out_ref = refs[:-1], refs[-1]
    rows, steps, _ = out_ref.shape
    layer = (
        state_ref[...] + tree_sum([decode_square(part[...]) for part in parts])
    ).astype(jnp.bfloat16)
    for r in range(rows):
        out_ref[r] = layer[r * steps : (r + 1) * steps]


VMEM = pl.BlockSpec(memory_space=pltpu.VMEM)
HBM = pl.BlockSpec(memory_space=pltpu.HBM)
SMEM = pl.BlockSpec(memory_space=pltpu.SMEM)


def call(kernel, name, in_specs, out_shapes, operands, scratch=(), out_spec=None, vmem=4 * 1024 * 1024, cost=None):
    return pl.pallas_call(
        kernel,
        name=name,
        in_specs=in_specs,
        out_specs=[out_spec or VMEM] * len(out_shapes),
        out_shape=[jax.ShapeDtypeStruct(shape, dtype) for shape, dtype in out_shapes],
        scratch_shapes=list(scratch),
        compiler_params=pltpu.CompilerParams(vmem_limit_bytes=vmem),
        cost_estimate=cost,
    )(*operands)


def cost(micros):
    return pl.CostEstimate(flops=micros * 1_000_000_000, bytes_accessed=1 << 20, transcendentals=0)


def move(block, ctx_hop, exp_hop):
    n, exp_count = lax.axis_size("ctx"), lax.axis_size("exp")
    pairs = [
        (c * exp_count + e, (c ^ ctx_hop) * exp_count + (e ^ exp_hop))
        for c in range(n)
        for e in range(exp_count)
    ]
    return lax.ppermute(block, ("ctx", "exp"), pairs)


def per_device(
    queries,
    cache_keys,
    cache_values,
    new_keys,
    new_values,
    lengths,
    residual,
    out_weight,
    norm_gain,
    expert_ids,
    expert_weights,
    gate_proj,
    up_proj,
    down_proj,
):
    row_count, step_count, _ = queries.shape
    row_steps = row_count * step_count
    n = lax.axis_size("ctx")
    exp_count = lax.axis_size("exp")
    me = lax.axis_index("ctx").astype(jnp.int32).reshape(1)
    home = lax.axis_index("exp").astype(jnp.int32).reshape(1)
    experts_all = exp_count * EXP_DEV
    capacity = max(2, (row_steps * TOPK + experts_all - 1) // experts_all)
    chips = exp_count // 2
    hops = (chips - 1, *range(1, chips - 1), 0)
    span = HEADS // n * row_steps
    bf16, f32 = jnp.bfloat16, jnp.float32
    hidden = (row_steps, D)
    block = (2 * capacity, D)
    half = (chips * capacity, D)

    message = (span + STAT_ROWS, LANES)
    inputs = (lengths, queries, cache_keys, cache_values, new_keys, new_values)
    sent = call(
        functools.partial(attend_kernel, n),
        "attend",
        [SMEM] + [HBM] * 6,
        [(message, bf16)] * n,
        (me,) + tuple(pltpu.with_memory_space_constraint(x, pltpu.HBM) for x in inputs),
        [pltpu.VMEM((n,) + message, bf16)]
        + [pltpu.SMEM(lengths.shape, lengths.dtype)]
        + [pltpu.VMEM(x.shape, x.dtype) for x in inputs[1:]]
        + [pltpu.SemaphoreType.DMA((len(inputs),))],
        cost=cost(10),
    )
    got = [move(x, j, 1) for j, x in zip(reversed(range(n)), sent)]
    selector, weight_high, weight_low, residual_rows = call(
        functools.partial(route_kernel, n, exp_count, capacity),
        "route",
        [SMEM] * 2 + [VMEM] * 3,
        [((row_steps, exp_count * capacity), bf16)] * 3 + [(hidden, f32)],
        (
            me,
            home,
            expert_ids.reshape(row_steps, TOPK),
            expert_weights.reshape(row_steps, TOPK),
            residual,
        ),
    )
    (projected,) = call(
        functools.partial(project_kernel, n),
        "project",
        [VMEM] * (n + 1),
        [(hidden, bf16)],
        (out_weight, *got),
        vmem=8 * 1024 * 1024,
        cost=cost(10),
    )
    got = [move(projected, j, 1) for j in range(n)]
    state, *outgoing = call(
        functools.partial(dispatch_kernel, n, hops),
        "dispatch",
        [VMEM] * (n + 3),
        [(hidden, f32)] + [(block, bf16)] * chips,
        (residual_rows, norm_gain.reshape(D // LANES, LANES), selector, *got),
        cost=cost(10),
    )

    def spread(blocks):
        return [x if j == 0 else move(x, 0, 2 * j + 1) for j, x in zip(hops, blocks)]

    kept, sent = call(
        gather_kernel,
        "gather",
        [VMEM] * chips,
        [(half, bf16)] * 2,
        spread(outgoing),
    )
    kept, sent = call(
        expert_kernel,
        "experts",
        [VMEM] * 5,
        [(half, bf16)] * 2,
        (
            kept,
            move(sent, 0, 1),
            gate_proj,
            up_proj,
            down_proj,
        ),
        vmem=20 * 1024 * 1024,
        cost=cost(10),
    )
    results = call(
        scatter_kernel,
        "scatter",
        [VMEM] * 2,
        [(block, bf16)] * chips,
        (kept, move(sent, 0, 1)),
    )
    (mixture,) = call(
        functools.partial(combine_kernel, hops),
        "combine",
        [VMEM] * (chips + 2),
        [(hidden, bf16)],
        (weight_high, weight_low, *spread(results)),
    )
    got = [move(mixture, j, 0) if j else mixture for j in range(n)]
    (layer_rows,) = call(
        finish_kernel,
        "finish",
        [VMEM] * (n + 1),
        [((row_count, step_count, D), bf16)],
        (state, *got),
    )
    return layer_rows


def solution(mesh):
    return jax.shard_map(
        per_device,
        mesh=mesh,
        in_specs=(
            P("exp", None, None),
            P("exp", "ctx", None),
            P("exp", "ctx", None),
            P("exp", None, None),
            P("exp", None, None),
            P("exp"),
            P("exp", None, None),
            P("ctx", None),
            P(),
            P("exp", None, None),
            P("exp", None, None),
            P("exp", None, "ctx"),
            P("exp", None, "ctx"),
            P("exp", "ctx", None),
        ),
        out_specs=P("exp", None, None),
        check_vma=False,
    )
```

```python
import functools
import math

import jax
import jax.numpy as jnp
from jax import lax
from jax.experimental import pallas as pl
from jax.experimental.pallas import tpu as pltpu
from jax.sharding import PartitionSpec as P

D = 2048
HEADS = 32
KV_HEADS = 2
HEAD_DIM = 128
EXP_DEV = 4
TOPK = 8
LANES = 128
SUBLANES = 8
STAT_ROWS = 16
MEAN_SCALE = 2.0**26
TERM_SCALE = 2.0**20


NORM_EPSILON = 1e-06
MASKED_SCORE = -1e30


def iota(shape, dim):
    return lax.broadcasted_iota(jnp.int32, shape, dim)


def to_column(row, count):
    return jnp.transpose(jnp.broadcast_to(row, (LANES, LANES)))[:count]


def encode(values):
    square = values * values
    return jnp.where(values < 0.0, -square * square, square * square).astype(jnp.bfloat16)


def decode(codes):
    codes = codes.astype(jnp.float32)
    root = lax.rsqrt(lax.rsqrt(jnp.abs(codes)))
    return jnp.where(codes < 0.0, -root, root)


def encode_square(values):
    return (values * jnp.abs(values)).astype(jnp.bfloat16)


def decode_square(codes):
    codes = codes.astype(jnp.float32)
    return codes * lax.rsqrt(jnp.maximum(jnp.abs(codes), 1e-37))


def encode_mean(values):
    return encode(values * jnp.abs(values) * MEAN_SCALE)


def decode_mean(codes):
    root = decode(codes)
    size = jnp.abs(root)
    return jnp.where(size > 0.0, root * lax.rsqrt(size) * MEAN_SCALE**-0.5, 0.0)


def split_two(values):
    high = values.astype(jnp.bfloat16)
    return high, (values - high.astype(jnp.float32)).astype(jnp.bfloat16)


def split_three(values):
    high = values.astype(jnp.bfloat16).astype(jnp.float32)
    middle = (values - high).astype(jnp.bfloat16).astype(jnp.float32)
    return high, middle, values - high - middle


def interleave(parts):
    count = parts[0].shape[0] // SUBLANES
    return jnp.concatenate(
        [part[i * SUBLANES : (i + 1) * SUBLANES] for i in range(count) for part in parts], 0
    )


def attend_kernel(
    ctx_count, me_ref, len_hbm, q_hbm, k_hbm, v_hbm, nk_hbm, nv_hbm, *rest
):
    outs, blocks = rest[:ctx_count], rest[ctx_count]
    len_ref, q_ref, k_ref, v_ref, nk_ref, nv_ref, sems = rest[ctx_count + 1 :]
    early, late = [
        [pltpu.make_async_copy(source, target, sems.at[i]) for i, source, target in group]
        for group in (
            (
                (0, k_hbm, k_ref),
                (1, q_hbm, q_ref),
                (2, len_hbm, len_ref),
                (3, nk_hbm, nk_ref),
            ),
            ((4, v_hbm, v_ref), (5, nv_hbm, nv_ref)),
        )
    ]
    for copy in early + late:
        copy.start()
    rows, steps, _ = q_ref.shape
    window = k_ref.shape[1]
    row_steps = rows * steps
    group = HEADS // KV_HEADS
    block_heads = HEADS // ctx_count
    high = group * row_steps
    wide = rows * window
    pieces = row_steps // SUBLANES
    piece_rows = rows // pieces
    piece_high = group * SUBLANES
    piece_wide = piece_rows * window
    scale = 1.0 / math.sqrt(HEAD_DIM)
    me = me_ref[0]
    for copy in early + late:
        copy.wait()
    values = v_ref[...].reshape(wide, KV_HEADS * HEAD_DIM)
    fresh_values = jnp.concatenate([nv_ref[r] for r in range(rows)], 0)
    queries = [
        jnp.concatenate([q_ref[p * piece_rows + r] for r in range(piece_rows)], 0)
        for p in range(pieces)
    ]
    keys = k_ref[...].reshape(wide, KV_HEADS * HEAD_DIM)
    fresh_keys = jnp.concatenate([nk_ref[r] for r in range(rows)], 0)
    column = iota((1, piece_wide), 1)
    column_row = column // window
    position = me * window + column % window
    row_index = iota((piece_high, 1), 0) % SUBLANES
    fresh_column = iota((1, row_steps), 1)
    live, fresh_live = [], []
    for p in range(pieces):
        limit = jnp.zeros((1, piece_wide), jnp.int32)
        for r in range(piece_rows):
            limit = jnp.where(column_row == r, len_ref[p * piece_rows + r], limit)
        live.append(row_index // steps == jnp.where(position < limit, column_row, -1))
        fresh_row = jnp.where(me == 0, fresh_column // steps - p * piece_rows, -1)
        fresh_live.append(
            (row_index // steps == fresh_row) & (fresh_column % steps <= row_index % steps)
        )
    contract_last = (((1,), (1,)), ((), ()))
    kv_lanes = [slice(kv * HEAD_DIM, (kv + 1) * HEAD_DIM) for kv in range(KV_HEADS)]
    spans = [slice(p * piece_wide, (p + 1) * piece_wide) for p in range(pieces)]
    scores, fresh = {}, {}
    for kv, lanes in enumerate(kv_lanes):
        for p, span in enumerate(spans):
            heads = jnp.concatenate(
                [
                    queries[p][:, h * HEAD_DIM : (h + 1) * HEAD_DIM]
                    for h in range(kv * group, (kv + 1) * group)
                ],
                0,
            )
            scores[kv, p] = lax.dot_general(
                heads, keys[span, lanes], contract_last, preferred_element_type=jnp.float32
            )
            fresh[kv, p] = lax.dot_general(
                heads, fresh_keys[:, lanes], contract_last, preferred_element_type=jnp.float32
            )
    terms, last_terms, tops, totals = {}, {}, {}, {}
    for kv in range(KV_HEADS):
        for p in range(pieces):
            part = jnp.where(live[p], scores[kv, p] * scale, MASKED_SCORE)
            last = jnp.where(fresh_live[p], fresh[kv, p] * scale, MASKED_SCORE)
            top = jnp.maximum(
                jnp.max(part, 1, keepdims=True), jnp.max(last, 1, keepdims=True)
            )
            part, last = jnp.exp(part - top), jnp.exp(last - top)
            terms[kv, p], last_terms[kv, p] = split_two(part), split_two(last)
            tops[kv, p] = top
            totals[kv, p] = jnp.sum(part, 1, keepdims=True) + jnp.sum(last, 1, keepdims=True)
    weighted = {}
    for kv, lanes in enumerate(kv_lanes):
        for p, span in enumerate(spans):
            weighted[kv, p] = sum(
                jnp.dot(term, values[span, lanes], preferred_element_type=jnp.float32)
                + jnp.dot(last, fresh_values[:, lanes], preferred_element_type=jnp.float32)
                for term, last in zip(terms[kv, p], last_terms[kv, p])
            )
    span = block_heads * row_steps
    row = iota((SUBLANES, LANES), 0)
    for kv in range(KV_HEADS):
        level = interleave(
            [
                jnp.broadcast_to(tops[kv, p] + jnp.log(totals[kv, p]), (piece_high, LANES))
                for p in range(pieces)
            ]
        )
        mean = interleave([weighted[kv, p] / totals[kv, p] for p in range(pieces)])
        mean = encode_mean(mean)
        for part in range(high // LANES):
            level_row = jnp.transpose(level[part * LANES : (part + 1) * LANES])[:SUBLANES]
            high_part, middle_part, low_part = split_three(level_row)
            stats = jnp.where(row == 0, high_part, jnp.where(row == 1, middle_part, low_part))
            stats = jnp.concatenate([stats, stats], 0).astype(jnp.bfloat16)
            for sub in range(LANES // span):
                dest = (kv * high + part * LANES) // span + sub
                start = part * LANES + sub * span
                blocks[dest, :span, :] = mean[start : start + span]
                piece = stats
                if sub > 0:
                    piece = jnp.concatenate([stats[:, sub * span :], stats[:, : sub * span]], 1)
                blocks[dest, span:, :] = piece
    for k, out in zip(reversed(range(ctx_count)), outs):
        out[...] = blocks[me ^ k]


def project_kernel(ctx_count, w_ref, *rest):
    parts, out_ref = rest[:ctx_count], rest[ctx_count]
    block_heads = HEADS // ctx_count
    span = parts[0].shape[0] - STAT_ROWS
    row_steps = span // block_heads
    stats = [part[span:, :].astype(jnp.float32) for part in parts]
    levels = [stat[0:1] + stat[1:2] + stat[2:3] for stat in stats]
    top = functools.reduce(jnp.maximum, levels)
    factors = [jnp.exp(level - top) for level in levels]
    total = functools.reduce(jnp.add, factors)
    mixed = None
    for part, factor in zip(parts, factors):
        term = decode_mean(part[:span, :]) * to_column(factor / total, span)
        mixed = term if mixed is None else mixed + term
    mixed = (mixed * TERM_SCALE).astype(jnp.bfloat16)
    attended = jnp.concatenate(
        [mixed[h * row_steps : (h + 1) * row_steps] for h in range(block_heads)], 1
    )
    out_ref[...] = encode(
        jnp.dot(attended, w_ref[...], preferred_element_type=jnp.float32)
    )


def route_kernel(
    ctx_count, exp_count, capacity, me_ref, home_ref, ids_ref, weights_ref, gain_ref, residual_ref,
    selector_ref, high_ref, low_ref, rows_ref, gains_ref
):
    rows, steps, _ = residual_ref.shape
    row_steps = rows * steps
    wide = exp_count * capacity
    me, home = me_ref[0], home_ref[0]
    column = iota((1, wide), 1)
    slot = column % capacity
    other = column // capacity % 2
    hop = column // (2 * capacity)
    crossed = jnp.where(hop == 0, 0, 1)
    device = home ^ (2 * hop) ^ crossed ^ other
    expert = device * EXP_DEV + me // (ctx_count // EXP_DEV)
    matched = jnp.zeros((row_steps, wide), jnp.float32)
    weight = jnp.zeros((row_steps, wide), jnp.float32)
    for k in range(TOPK):
        hit = ids_ref[:, k : k + 1] == expert
        matched = jnp.where(hit, 1.0, matched)
        weight = jnp.where(hit, weights_ref[:, k : k + 1], weight)
    earlier = iota((row_steps, row_steps), 1) < iota((row_steps, row_steps), 0)
    rank = jnp.dot(
        jnp.where(earlier, 1.0, 0.0).astype(jnp.bfloat16),
        matched.astype(jnp.bfloat16),
        preferred_element_type=jnp.float32,
    )
    chosen = (matched > 0.0) & (rank == slot.astype(jnp.float32))
    selector_ref[...] = jnp.where(chosen, 1.0, 0.0).astype(jnp.bfloat16)
    weight = jnp.where(chosen, weight, 0.0)
    weight_high = weight.astype(jnp.bfloat16)
    high_ref[...] = weight_high
    low_ref[...] = (weight - weight_high.astype(jnp.float32)).astype(jnp.bfloat16)
    gain = gain_ref[...].astype(jnp.float32)
    for i in range(D // LANES):
        gains_ref[:, i * LANES : (i + 1) * LANES] = jnp.broadcast_to(
            gain[i : i + 1], (row_steps, LANES)
        )
    rows_ref[...] = jnp.concatenate(
        [residual_ref[r].astype(jnp.float32) for r in range(rows)], 0
    )


def tree_sum(parts):
    values = list(parts)
    while len(values) > 1:
        values = [values[i] + values[i + 1] for i in range(0, len(values), 2)]
    return values[0]


def dispatch_kernel(ctx_count, hops, residual_ref, gain_ref, selector_ref, *rest):
    parts, state_ref, outs = rest[:ctx_count], rest[ctx_count], rest[ctx_count + 1 :]
    terms = tree_sum([decode(part[...]) for part in parts])
    state = residual_ref[...] + terms * (1.0 / TERM_SCALE)
    state_ref[...] = state
    normed = (
        state
        * lax.rsqrt(jnp.mean(state * state, -1, keepdims=True) + NORM_EPSILON)
        * gain_ref[...]
    ).astype(jnp.bfloat16)
    picked = lax.dot_general(
        selector_ref[...],
        normed,
        (((0,), (0,)), ((), ())),
        preferred_element_type=jnp.float32,
    )
    block = outs[0].shape[0]
    for j, out in zip(hops, outs):
        out[...] = picked[j * block : (j + 1) * block].astype(jnp.bfloat16)


def gather_kernel(*refs):
    blocks, keep_ref, send_ref = refs[:-2], refs[-2], refs[-1]
    half = blocks[0].shape[0] // 2
    values = [block[...].astype(jnp.float32) for block in blocks]
    keep_ref[...] = jnp.concatenate([value[:half] for value in values], 0).astype(jnp.bfloat16)
    send_ref[...] = jnp.concatenate([value[half:] for value in values], 0).astype(jnp.bfloat16)


def expert_kernel(kept_ref, got_ref, gate_ref, up_ref, down_ref, keep_ref, send_ref):
    half = kept_ref.shape[0]
    normed = jnp.concatenate(
        [kept_ref[...].astype(jnp.float32), got_ref[...].astype(jnp.float32)], 0
    ).astype(jnp.bfloat16)
    spare = max(0, LANES - 2 * half)
    if spare:
        normed = jnp.concatenate([normed, jnp.zeros((spare, D), jnp.bfloat16)], 0)
    gate = jnp.dot(normed, gate_ref[0], preferred_element_type=jnp.float32)
    up = jnp.dot(normed, up_ref[0], preferred_element_type=jnp.float32)
    activation = (gate / (1.0 + jnp.exp(-gate)) * up).astype(jnp.bfloat16)
    result = jnp.dot(activation, down_ref[0], preferred_element_type=jnp.float32)
    keep_ref[...] = encode_square(result[:half])
    send_ref[...] = encode_square(result[half : 2 * half])


def scatter_kernel(hops, back, kept_ref, got_ref, *outs):
    half = outs[0].shape[0] // 2
    kept, got = kept_ref[...].astype(jnp.float32), got_ref[...].astype(jnp.float32)
    for j, out in zip(back, outs):
        first = hops.index(j) * half
        span = slice(first, first + half)
        out[...] = jnp.concatenate([kept[span], got[span]], 0).astype(jnp.bfloat16)


def combine_kernel(hops, high_ref, low_ref, *refs):
    blocks, out_ref = [refs[hops.index(j)] for j in range(len(hops))], refs[-1]
    returned = decode_square(
        jnp.concatenate([block[...].astype(jnp.float32) for block in blocks], 0)
    )
    returned_high, returned_low = split_two(returned)
    weight_high, weight_low = high_ref[...], low_ref[...]
    mixture = (
        jnp.dot(weight_high, returned_high, preferred_element_type=jnp.float32)
        + jnp.dot(weight_high, returned_low, preferred_element_type=jnp.float32)
        + jnp.dot(weight_low, returned_high, preferred_element_type=jnp.float32)
    )
    out_ref[...] = encode_square(mixture)


def finish_kernel(state_ref, *refs):
    parts, out_ref = refs[:-1], refs[-1]
    rows, steps, _ = out_ref.shape
    layer = (
        state_ref[...] + tree_sum([decode_square(part[...]) for part in parts])
    ).astype(jnp.bfloat16)
    for r in range(rows):
        out_ref[r] = layer[r * steps : (r + 1) * steps]


VMEM = pl.BlockSpec(memory_space=pltpu.VMEM)
HBM = pl.BlockSpec(memory_space=pltpu.HBM)
SMEM = pl.BlockSpec(memory_space=pltpu.SMEM)


def call(kernel, name, in_specs, out_shapes, operands, scratch=(), out_spec=None, vmem=4 * 1024 * 1024, cost=None):
    return pl.pallas_call(
        kernel,
        name=name,
        in_specs=in_specs,
        out_specs=[out_spec or VMEM] * len(out_shapes),
        out_shape=[jax.ShapeDtypeStruct(shape, dtype) for shape, dtype in out_shapes],
        scratch_shapes=list(scratch),
        compiler_params=pltpu.CompilerParams(vmem_limit_bytes=vmem),
        cost_estimate=cost,
    )(*operands)


def cost(micros):
    return pl.CostEstimate(flops=micros * 1_000_000_000, bytes_accessed=1 << 20, transcendentals=0)


def move(block, ctx_hop, exp_hop):
    n, exp_count = lax.axis_size("ctx"), lax.axis_size("exp")
    pairs = [
        (c * exp_count + e, (c ^ ctx_hop) * exp_count + (e ^ exp_hop))
        for c in range(n)
        for e in range(exp_count)
    ]
    return lax.ppermute(block, ("ctx", "exp"), pairs)


def per_device(
    queries,
    cache_keys,
    cache_values,
    new_keys,
    new_values,
    lengths,
    residual,
    out_weight,
    norm_gain,
    expert_ids,
    expert_weights,
    gate_proj,
    up_proj,
    down_proj,
):
    row_count, step_count, _ = queries.shape
    row_steps = row_count * step_count
    n = lax.axis_size("ctx")
    exp_count = lax.axis_size("exp")
    me = lax.axis_index("ctx").astype(jnp.int32).reshape(1)
    home = lax.axis_index("exp").astype(jnp.int32).reshape(1)
    experts_all = exp_count * EXP_DEV
    capacity = max(2, (row_steps * TOPK + experts_all - 1) // experts_all)
    chips = exp_count // 2
    hops = tuple(reversed(range(chips)))
    back = (chips - 1, *range(1, chips - 1), 0)
    span = HEADS // n * row_steps
    bf16, f32 = jnp.bfloat16, jnp.float32
    hidden = (row_steps, D)
    block = (2 * capacity, D)
    half = (chips * capacity, D)

    message = (span + STAT_ROWS, LANES)
    inputs = (lengths, queries, cache_keys, cache_values, new_keys, new_values)
    sent = call(
        functools.partial(attend_kernel, n),
        "attend",
        [SMEM] + [HBM] * 6,
        [(message, bf16)] * n,
        (me,) + tuple(pltpu.with_memory_space_constraint(x, pltpu.HBM) for x in inputs),
        [pltpu.VMEM((n,) + message, bf16)]
        + [pltpu.SMEM(lengths.shape, lengths.dtype)]
        + [pltpu.VMEM(x.shape, x.dtype) for x in inputs[1:]]
        + [pltpu.SemaphoreType.DMA((len(inputs),))],
        cost=cost(10),
    )
    got = [move(x, j, 1) for j, x in zip(reversed(range(n)), sent)]
    selector, weight_high, weight_low, residual_rows, gain_rows = call(
        functools.partial(route_kernel, n, exp_count, capacity),
        "route",
        [SMEM] * 2 + [VMEM] * 4,
        [((row_steps, exp_count * capacity), bf16)] * 3 + [(hidden, f32)] * 2,
        (
            me,
            home,
            expert_ids.reshape(row_steps, TOPK),
            expert_weights.reshape(row_steps, TOPK),
            norm_gain.reshape(D // LANES, LANES),
            residual,
        ),
    )
    (projected,) = call(
        functools.partial(project_kernel, n),
        "project",
        [VMEM] * (n + 1),
        [(hidden, bf16)],
        (out_weight, *got),
        vmem=8 * 1024 * 1024,
        cost=cost(10),
    )
    got = [move(projected, j, 1) for j in range(n)]
    state, *outgoing = call(
        functools.partial(dispatch_kernel, n, hops),
        "dispatch",
        [VMEM] * (n + 3),
        [(hidden, f32)] + [(block, bf16)] * chips,
        (residual_rows, gain_rows, selector, *got),
        cost=cost(10),
    )

    def spread(hops, blocks):
        return [x if j == 0 else move(x, 0, 2 * j + 1) for j, x in zip(hops, blocks)]

    kept, sent = call(
        gather_kernel,
        "gather",
        [VMEM] * chips,
        [(half, bf16)] * 2,
        spread(hops, outgoing),
    )
    kept, sent = call(
        expert_kernel,
        "experts",
        [VMEM] * 5,
        [(half, bf16)] * 2,
        (
            kept,
            move(sent, 0, 1),
            gate_proj,
            up_proj,
            down_proj,
        ),
        vmem=20 * 1024 * 1024,
        cost=cost(10),
    )
    results = call(
        functools.partial(scatter_kernel, hops, back),
        "scatter",
        [VMEM] * 2,
        [(block, bf16)] * chips,
        (kept, move(sent, 0, 1)),
    )
    (mixture,) = call(
        functools.partial(combine_kernel, back),
        "combine",
        [VMEM] * (chips + 2),
        [(hidden, bf16)],
        (weight_high, weight_low, *spread(back, results)),
    )
    got = [move(mixture, j, 0) if j else mixture for j in range(n)]
    (layer_rows,) = call(
        finish_kernel,
        "finish",
        [VMEM] * (n + 1),
        [((row_count, step_count, D), bf16)],
        (state, *got),
    )
    return layer_rows


def solution(mesh):
    return jax.shard_map(
        per_device,
        mesh=mesh,
        in_specs=(
            P("exp", None, None),
            P("exp", "ctx", None),
            P("exp", "ctx", None),
            P("exp", None, None),
            P("exp", None, None),
            P("exp"),
            P("exp", None, None),
            P("ctx", None),
            P(),
            P("exp", None, None),
            P("exp", None, None),
            P("exp", None, "ctx"),
            P("exp", None, "ctx"),
            P("exp", "ctx", None),
        ),
        out_specs=P("exp", None, None),
        check_vma=False,
    )
```

```python
import functools
import math

import jax
import jax.numpy as jnp
from jax import lax
from jax.experimental import pallas as pl
from jax.experimental.pallas import tpu as pltpu
from jax.sharding import PartitionSpec as P

D = 2048
HEADS = 32
KV_HEADS = 2
HEAD_DIM = 128
EXP_DEV = 4
TOPK = 8
LANES = 128
SUBLANES = 8
STAT_ROWS = 16
MEAN_SCALE = 2.0**26
TERM_SCALE = 2.0**20


NORM_EPSILON = 1e-06
MASKED_SCORE = -1e30


def iota(shape, dim):
    return lax.broadcasted_iota(jnp.int32, shape, dim)


def to_column(row, count):
    return jnp.transpose(jnp.broadcast_to(row, (LANES, LANES)))[:count]


def encode(values):
    square = values * values
    return jnp.where(values < 0.0, -square * square, square * square).astype(jnp.bfloat16)


def decode(codes):
    codes = codes.astype(jnp.float32)
    root = lax.rsqrt(lax.rsqrt(jnp.abs(codes)))
    return jnp.where(codes < 0.0, -root, root)


def encode_square(values):
    return (values * jnp.abs(values)).astype(jnp.bfloat16)


def decode_square(codes):
    codes = codes.astype(jnp.float32)
    return codes * lax.rsqrt(jnp.maximum(jnp.abs(codes), 1e-37))


def encode_mean(values):
    return encode(values * jnp.abs(values) * MEAN_SCALE)


def decode_mean(codes):
    root = decode(codes)
    size = jnp.abs(root)
    return jnp.where(size > 0.0, root * lax.rsqrt(size) * MEAN_SCALE**-0.5, 0.0)


def split_two(values):
    high = values.astype(jnp.bfloat16)
    return high, (values - high.astype(jnp.float32)).astype(jnp.bfloat16)


def split_three(values):
    high = values.astype(jnp.bfloat16).astype(jnp.float32)
    middle = (values - high).astype(jnp.bfloat16).astype(jnp.float32)
    return high, middle, values - high - middle


def interleave(parts):
    count = parts[0].shape[0] // SUBLANES
    return jnp.concatenate(
        [part[i * SUBLANES : (i + 1) * SUBLANES] for i in range(count) for part in parts], 0
    )


def attend_kernel(
    ctx_count, me_ref, len_hbm, q_hbm, k_hbm, v_hbm, nk_hbm, nv_hbm, *rest
):
    outs, blocks = rest[:ctx_count], rest[ctx_count]
    len_ref, q_ref, k_ref, v_ref, nk_ref, nv_ref, sems = rest[ctx_count + 1 :]
    early, late = [
        [pltpu.make_async_copy(source, target, sems.at[i]) for i, source, target in group]
        for group in (
            (
                (0, k_hbm, k_ref),
                (1, q_hbm, q_ref),
                (2, len_hbm, len_ref),
                (3, nk_hbm, nk_ref),
            ),
            ((4, v_hbm, v_ref), (5, nv_hbm, nv_ref)),
        )
    ]
    for copy in early + late:
        copy.start()
    rows, steps, _ = q_ref.shape
    window = k_ref.shape[1]
    row_steps = rows * steps
    group = HEADS // KV_HEADS
    block_heads = HEADS // ctx_count
    high = group * row_steps
    wide = rows * window
    pieces = row_steps // SUBLANES
    piece_rows = rows // pieces
    piece_high = group * SUBLANES
    piece_wide = piece_rows * window
    scale = 1.0 / math.sqrt(HEAD_DIM)
    me = me_ref[0]
    for copy in early + late:
        copy.wait()
    values = v_ref[...].reshape(wide, KV_HEADS * HEAD_DIM)
    fresh_values = jnp.concatenate([nv_ref[r] for r in range(rows)], 0)
    queries = [
        jnp.concatenate([q_ref[p * piece_rows + r] for r in range(piece_rows)], 0)
        for p in range(pieces)
    ]
    keys = k_ref[...].reshape(wide, KV_HEADS * HEAD_DIM)
    fresh_keys = jnp.concatenate([nk_ref[r] for r in range(rows)], 0)
    column = iota((1, piece_wide), 1)
    column_row = column // window
    position = me * window + column % window
    row_index = iota((piece_high, 1), 0) % SUBLANES
    fresh_column = iota((1, row_steps), 1)
    live, fresh_live = [], []
    for p in range(pieces):
        limit = jnp.zeros((1, piece_wide), jnp.int32)
        for r in range(piece_rows):
            limit = jnp.where(column_row == r, len_ref[p * piece_rows + r], limit)
        live.append(row_index // steps == jnp.where(position < limit, column_row, -1))
        fresh_row = jnp.where(me == 0, fresh_column // steps - p * piece_rows, -1)
        fresh_live.append(
            (row_index // steps == fresh_row) & (fresh_column % steps <= row_index % steps)
        )
    contract_last = (((1,), (1,)), ((), ()))
    kv_lanes = [slice(kv * HEAD_DIM, (kv + 1) * HEAD_DIM) for kv in range(KV_HEADS)]
    spans = [slice(p * piece_wide, (p + 1) * piece_wide) for p in range(pieces)]
    scores, fresh = {}, {}
    for kv, lanes in enumerate(kv_lanes):
        for p, span in enumerate(spans):
            heads = jnp.concatenate(
                [
                    queries[p][:, h * HEAD_DIM : (h + 1) * HEAD_DIM]
                    for h in range(kv * group, (kv + 1) * group)
                ],
                0,
            )
            scores[kv, p] = lax.dot_general(
                heads, keys[span, lanes], contract_last, preferred_element_type=jnp.float32
            )
            fresh[kv, p] = lax.dot_general(
                heads, fresh_keys[:, lanes], contract_last, preferred_element_type=jnp.float32
            )
    terms, last_terms, tops, totals = {}, {}, {}, {}
    for kv in range(KV_HEADS):
        for p in range(pieces):
            part = jnp.where(live[p], scores[kv, p] * scale, MASKED_SCORE)
            last = jnp.where(fresh_live[p], fresh[kv, p] * scale, MASKED_SCORE)
            top = jnp.maximum(
                jnp.max(part, 1, keepdims=True), jnp.max(last, 1, keepdims=True)
            )
            part, last = jnp.exp(part - top), jnp.exp(last - top)
            terms[kv, p], last_terms[kv, p] = split_two(part), split_two(last)
            tops[kv, p] = top
            totals[kv, p] = jnp.sum(part, 1, keepdims=True) + jnp.sum(last, 1, keepdims=True)
    weighted = {}
    for kv, lanes in enumerate(kv_lanes):
        for p, span in enumerate(spans):
            weighted[kv, p] = sum(
                jnp.dot(term, values[span, lanes], preferred_element_type=jnp.float32)
                + jnp.dot(last, fresh_values[:, lanes], preferred_element_type=jnp.float32)
                for term, last in zip(terms[kv, p], last_terms[kv, p])
            )
    span = block_heads * row_steps
    row = iota((SUBLANES, LANES), 0)
    for kv in range(KV_HEADS):
        level = interleave(
            [
                jnp.broadcast_to(tops[kv, p] + jnp.log(totals[kv, p]), (piece_high, LANES))
                for p in range(pieces)
            ]
        )
        mean = interleave([weighted[kv, p] / totals[kv, p] for p in range(pieces)])
        mean = encode_mean(mean)
        for part in range(high // LANES):
            level_row = jnp.transpose(level[part * LANES : (part + 1) * LANES])[:SUBLANES]
            high_part, middle_part, low_part = split_three(level_row)
            stats = jnp.where(row == 0, high_part, jnp.where(row == 1, middle_part, low_part))
            stats = jnp.concatenate([stats, stats], 0).astype(jnp.bfloat16)
            for sub in range(LANES // span):
                dest = (kv * high + part * LANES) // span + sub
                start = part * LANES + sub * span
                blocks[dest, :span, :] = mean[start : start + span]
                piece = stats
                if sub > 0:
                    piece = jnp.concatenate([stats[:, sub * span :], stats[:, : sub * span]], 1)
                blocks[dest, span:, :] = piece
    for k, out in zip((*reversed(range(2, ctx_count)), 0, 1), outs):
        out[...] = blocks[me ^ k]


def project_kernel(ctx_count, w_ref, *rest):
    parts, out_ref = rest[:ctx_count], rest[ctx_count]
    block_heads = HEADS // ctx_count
    span = parts[0].shape[0] - STAT_ROWS
    row_steps = span // block_heads
    stats = [part[span:, :].astype(jnp.float32) for part in parts]
    levels = [stat[0:1] + stat[1:2] + stat[2:3] for stat in stats]
    top = functools.reduce(jnp.maximum, levels)
    factors = [jnp.exp(level - top) for level in levels]
    total = functools.reduce(jnp.add, factors)
    mixed = None
    for part, factor in zip(parts, factors):
        term = decode_mean(part[:span, :]) * to_column(factor / total, span)
        mixed = term if mixed is None else mixed + term
    mixed = (mixed * TERM_SCALE).astype(jnp.bfloat16)
    attended = jnp.concatenate(
        [mixed[h * row_steps : (h + 1) * row_steps] for h in range(block_heads)], 1
    )
    out_ref[...] = encode(
        jnp.dot(attended, w_ref[...], preferred_element_type=jnp.float32)
    )


def route_kernel(
    ctx_count, exp_count, capacity, me_ref, home_ref, ids_ref, weights_ref, gain_ref, residual_ref,
    selector_ref, high_ref, low_ref, rows_ref, gains_ref
):
    rows, steps, _ = residual_ref.shape
    row_steps = rows * steps
    wide = exp_count * capacity
    me, home = me_ref[0], home_ref[0]
    column = iota((1, wide), 1)
    slot = column % capacity
    other = column // capacity % 2
    hop = column // (2 * capacity)
    crossed = jnp.where(hop == 0, 0, 1)
    device = home ^ (2 * hop) ^ crossed ^ other
    expert = device * EXP_DEV + me // (ctx_count // EXP_DEV)
    matched = jnp.zeros((row_steps, wide), jnp.float32)
    weight = jnp.zeros((row_steps, wide), jnp.float32)
    for k in range(TOPK):
        hit = ids_ref[:, k : k + 1] == expert
        matched = jnp.where(hit, 1.0, matched)
        weight = jnp.where(hit, weights_ref[:, k : k + 1], weight)
    earlier = iota((row_steps, row_steps), 1) < iota((row_steps, row_steps), 0)
    rank = jnp.dot(
        jnp.where(earlier, 1.0, 0.0).astype(jnp.bfloat16),
        matched.astype(jnp.bfloat16),
        preferred_element_type=jnp.float32,
    )
    chosen = (matched > 0.0) & (rank == slot.astype(jnp.float32))
    selector_ref[...] = jnp.where(chosen, 1.0, 0.0).astype(jnp.bfloat16)
    weight = jnp.where(chosen, weight, 0.0)
    weight_high = weight.astype(jnp.bfloat16)
    high_ref[...] = weight_high
    low_ref[...] = (weight - weight_high.astype(jnp.float32)).astype(jnp.bfloat16)
    gain = gain_ref[...].astype(jnp.float32)
    for i in range(D // LANES):
        gains_ref[:, i * LANES : (i + 1) * LANES] = jnp.broadcast_to(
            gain[i : i + 1], (row_steps, LANES)
        )
    rows_ref[...] = jnp.concatenate(
        [residual_ref[r].astype(jnp.float32) for r in range(rows)], 0
    )


def tree_sum(parts):
    values = list(parts)
    while len(values) > 1:
        values = [values[i] + values[i + 1] for i in range(0, len(values), 2)]
    return values[0]


def dispatch_kernel(ctx_count, hops, residual_ref, gain_ref, selector_ref, *rest):
    parts, state_ref, outs = rest[:ctx_count], rest[ctx_count], rest[ctx_count + 1 :]
    terms = tree_sum([decode(part[...]) for part in parts])
    state = residual_ref[...] + terms * (1.0 / TERM_SCALE)
    state_ref[...] = state
    normed = (
        state
        * lax.rsqrt(jnp.mean(state * state, -1, keepdims=True) + NORM_EPSILON)
        * gain_ref[...]
    ).astype(jnp.bfloat16)
    picked = lax.dot_general(
        selector_ref[...],
        normed,
        (((0,), (0,)), ((), ())),
        preferred_element_type=jnp.float32,
    )
    block = outs[0].shape[0]
    for j, out in zip(hops, outs):
        out[...] = picked[j * block : (j + 1) * block].astype(jnp.bfloat16)


def gather_kernel(*refs):
    blocks, keep_ref, send_ref = refs[:-2], refs[-2], refs[-1]
    half = blocks[0].shape[0] // 2
    values = [block[...].astype(jnp.float32) for block in blocks]
    keep_ref[...] = jnp.concatenate([value[:half] for value in values], 0).astype(jnp.bfloat16)
    send_ref[...] = jnp.concatenate([value[half:] for value in values], 0).astype(jnp.bfloat16)


def expert_kernel(kept_ref, got_ref, gate_ref, up_ref, down_ref, keep_ref, send_ref):
    half = kept_ref.shape[0]
    normed = jnp.concatenate(
        [kept_ref[...].astype(jnp.float32), got_ref[...].astype(jnp.float32)], 0
    ).astype(jnp.bfloat16)
    spare = max(0, LANES - 2 * half)
    if spare:
        normed = jnp.concatenate([normed, jnp.zeros((spare, D), jnp.bfloat16)], 0)
    gate = jnp.dot(normed, gate_ref[0], preferred_element_type=jnp.float32)
    up = jnp.dot(normed, up_ref[0], preferred_element_type=jnp.float32)
    activation = (gate / (1.0 + jnp.exp(-gate)) * up).astype(jnp.bfloat16)
    result = jnp.dot(activation, down_ref[0], preferred_element_type=jnp.float32)
    keep_ref[...] = encode_square(result[:half])
    send_ref[...] = encode_square(result[half : 2 * half])


def scatter_kernel(hops, back, kept_ref, got_ref, *outs):
    half = outs[0].shape[0] // 2
    kept, got = kept_ref[...].astype(jnp.float32), got_ref[...].astype(jnp.float32)
    for j, out in zip(back, outs):
        first = hops.index(j) * half
        span = slice(first, first + half)
        out[...] = jnp.concatenate([kept[span], got[span]], 0).astype(jnp.bfloat16)


def combine_kernel(hops, high_ref, low_ref, *refs):
    blocks, out_ref = [refs[hops.index(j)] for j in range(len(hops))], refs[-1]
    returned = decode_square(
        jnp.concatenate([block[...].astype(jnp.float32) for block in blocks], 0)
    )
    returned_high, returned_low = split_two(returned)
    weight_high, weight_low = high_ref[...], low_ref[...]
    mixture = (
        jnp.dot(weight_high, returned_high, preferred_element_type=jnp.float32)
        + jnp.dot(weight_high, returned_low, preferred_element_type=jnp.float32)
        + jnp.dot(weight_low, returned_high, preferred_element_type=jnp.float32)
    )
    out_ref[...] = encode_square(mixture)


def finish_kernel(state_ref, *refs):
    parts, out_ref = refs[:-1], refs[-1]
    rows, steps, _ = out_ref.shape
    layer = (
        state_ref[...] + tree_sum([decode_square(part[...]) for part in parts])
    ).astype(jnp.bfloat16)
    for r in range(rows):
        out_ref[r] = layer[r * steps : (r + 1) * steps]


VMEM = pl.BlockSpec(memory_space=pltpu.VMEM)
HBM = pl.BlockSpec(memory_space=pltpu.HBM)
SMEM = pl.BlockSpec(memory_space=pltpu.SMEM)


def call(kernel, name, in_specs, out_shapes, operands, scratch=(), out_spec=None, vmem=4 * 1024 * 1024, cost=None):
    return pl.pallas_call(
        kernel,
        name=name,
        in_specs=in_specs,
        out_specs=[out_spec or VMEM] * len(out_shapes),
        out_shape=[jax.ShapeDtypeStruct(shape, dtype) for shape, dtype in out_shapes],
        scratch_shapes=list(scratch),
        compiler_params=pltpu.CompilerParams(vmem_limit_bytes=vmem),
        cost_estimate=cost,
    )(*operands)


def cost(micros):
    return pl.CostEstimate(flops=micros * 1_000_000_000, bytes_accessed=1 << 20, transcendentals=0)


def move(block, ctx_hop, exp_hop):
    n, exp_count = lax.axis_size("ctx"), lax.axis_size("exp")
    pairs = [
        (c * exp_count + e, (c ^ ctx_hop) * exp_count + (e ^ exp_hop))
        for c in range(n)
        for e in range(exp_count)
    ]
    return lax.ppermute(block, ("ctx", "exp"), pairs)


def per_device(
    queries,
    cache_keys,
    cache_values,
    new_keys,
    new_values,
    lengths,
    residual,
    out_weight,
    norm_gain,
    expert_ids,
    expert_weights,
    gate_proj,
    up_proj,
    down_proj,
):
    row_count, step_count, _ = queries.shape
    row_steps = row_count * step_count
    n = lax.axis_size("ctx")
    exp_count = lax.axis_size("exp")
    me = lax.axis_index("ctx").astype(jnp.int32).reshape(1)
    home = lax.axis_index("exp").astype(jnp.int32).reshape(1)
    experts_all = exp_count * EXP_DEV
    capacity = max(2, (row_steps * TOPK + experts_all - 1) // experts_all)
    chips = exp_count // 2
    hops = tuple(reversed(range(chips)))
    back = (chips - 1, *range(1, chips - 1), 0)
    span = HEADS // n * row_steps
    bf16, f32 = jnp.bfloat16, jnp.float32
    hidden = (row_steps, D)
    block = (2 * capacity, D)
    half = (chips * capacity, D)

    message = (span + STAT_ROWS, LANES)
    inputs = (lengths, queries, cache_keys, cache_values, new_keys, new_values)
    sent = call(
        functools.partial(attend_kernel, n),
        "attend",
        [SMEM] + [HBM] * 6,
        [(message, bf16)] * n,
        (me,) + tuple(pltpu.with_memory_space_constraint(x, pltpu.HBM) for x in inputs),
        [pltpu.VMEM((n,) + message, bf16)]
        + [pltpu.SMEM(lengths.shape, lengths.dtype)]
        + [pltpu.VMEM(x.shape, x.dtype) for x in inputs[1:]]
        + [pltpu.SemaphoreType.DMA((len(inputs),))],
        cost=cost(10),
    )
    got = [move(x, j, 1) for j, x in zip((*reversed(range(2, n)), 0, 1), sent)]
    selector, weight_high, weight_low, residual_rows, gain_rows = call(
        functools.partial(route_kernel, n, exp_count, capacity),
        "route",
        [SMEM] * 2 + [VMEM] * 4,
        [((row_steps, exp_count * capacity), bf16)] * 3 + [(hidden, f32)] * 2,
        (
            me,
            home,
            expert_ids.reshape(row_steps, TOPK),
            expert_weights.reshape(row_steps, TOPK),
            norm_gain.reshape(D // LANES, LANES),
            residual,
        ),
    )
    (projected,) = call(
        functools.partial(project_kernel, n),
        "project",
        [VMEM] * (n + 1),
        [(hidden, bf16)],
        (out_weight, *got),
        vmem=8 * 1024 * 1024,
        cost=cost(10),
    )
    got = [move(projected, j, 1) for j in range(n)]
    state, *outgoing = call(
        functools.partial(dispatch_kernel, n, hops),
        "dispatch",
        [VMEM] * (n + 3),
        [(hidden, f32)] + [(block, bf16)] * chips,
        (residual_rows, gain_rows, selector, *got),
        cost=cost(10),
    )

    def spread(hops, blocks):
        return [x if j == 0 else move(x, 0, 2 * j + 1) for j, x in zip(hops, blocks)]

    kept, sent = call(
        gather_kernel,
        "gather",
        [VMEM] * chips,
        [(half, bf16)] * 2,
        spread(hops, outgoing),
    )
    kept, sent = call(
        expert_kernel,
        "experts",
        [VMEM] * 5,
        [(half, bf16)] * 2,
        (
            kept,
            move(sent, 0, 1),
            gate_proj,
            up_proj,
            down_proj,
        ),
        vmem=20 * 1024 * 1024,
        cost=cost(10),
    )
    results = call(
        functools.partial(scatter_kernel, hops, back),
        "scatter",
        [VMEM] * 2,
        [(block, bf16)] * chips,
        (kept, move(sent, 0, 1)),
    )
    (mixture,) = call(
        functools.partial(combine_kernel, back),
        "combine",
        [VMEM] * (chips + 2),
        [(hidden, bf16)],
        (weight_high, weight_low, *spread(back, results)),
    )
    got = [move(mixture, j, 0) if j else mixture for j in range(n)]
    (layer_rows,) = call(
        finish_kernel,
        "finish",
        [VMEM] * (n + 1),
        [((row_count, step_count, D), bf16)],
        (state, *got),
    )
    return layer_rows


def solution(mesh):
    return jax.shard_map(
        per_device,
        mesh=mesh,
        in_specs=(
            P("exp", None, None),
            P("exp", "ctx", None),
            P("exp", "ctx", None),
            P("exp", None, None),
            P("exp", None, None),
            P("exp"),
            P("exp", None, None),
            P("ctx", None),
            P(),
            P("exp", None, None),
            P("exp", None, None),
            P("exp", None, "ctx"),
            P("exp", None, "ctx"),
            P("exp", "ctx", None),
        ),
        out_specs=P("exp", None, None),
        check_vma=False,
    )
```
